32 devices in a mesh: dp: 8 (over y, x, core), seq: 4 (over z).
Axes of the slice: x: 2, y: 2, z: 4, core: 2. Of those that a mesh axis runs over, the one named last changes fastest.
Arguments:
- tokens: bfloat16 [8, 1024, 2048], P('dp', 'seq'), may hold values from -6 to 6
- lengths: int32 [8], P('dp'), may hold values from 128 to 1024, as said below
- repos: int32 [8], P('dp'), may hold values from 0 to 3
- ln1_gain: bfloat16 [2048], P(('dp', 'seq')), may hold values from 0.25 to 1.75
- ln1_bias: bfloat16 [2048], P(('dp', 'seq')), may hold values from -2 to 2
- w_query: bfloat16 [2048, 2048], P(('dp', 'seq')), may hold values from -0.125 to 0.125
- b_query: bfloat16 [2048], P(('dp', 'seq')), may hold values from -3 to 3
- w_key: bfloat16 [2048, 128], P(('dp', 'seq')), may hold values from -0.125 to 0.125
- w_value: bfloat16 [2048, 128], P(('dp', 'seq')), may hold values from -0.125 to 0.125
- b_value: bfloat16 [128], P(('dp', 'seq')), may hold values from -0.29882812 to 0.29882812
- w_out: bfloat16 [2048, 2048], P(('dp', 'seq')), may hold values from -1.5 to 1.5
- b_out: bfloat16 [2048], P(('dp', 'seq')), may hold values from -3 to 3
- ln2_gain: bfloat16 [2048], P(('dp', 'seq')), may hold values from 0.25 to 1.75
- ln2_bias: bfloat16 [2048], P(('dp', 'seq')), may hold values from -2 to 2
- w_fc: bfloat16 [2048, 8192], P(('dp', 'seq')), may hold values from -0.125 to 0.125
- b_fc: bfloat16 [8192], P(('dp', 'seq')), may hold values from -3 to 3
- w_proj: bfloat16 [8192, 2048], P(('dp', 'seq')), may hold values from -0.0625 to 0.0625
- b_proj: bfloat16 [2048], P(('dp', 'seq')), may hold values from -3 to 3
- grad_out: bfloat16 [8, 1024, 2048], P('dp', 'seq'), may hold values from -6 to 6
Outputs:
- output: bfloat16 [8, 1024, 2048], P('dp', 'seq')
- grad_tokens: bfloat16 [8, 1024, 2048], P('dp', 'seq')
- d_ln1_gain: float32 [2048], P(('dp', 'seq'))
- d_ln1_bias: float32 [2048], P(('dp', 'seq'))
- d_w_query: float32 [2048, 2048], P(('dp', 'seq'))
- d_b_query: float32 [2048], P(('dp', 'seq'))
- d_w_key: float32 [2048, 128], P(('dp', 'seq'))
- d_w_value: float32 [2048, 128], P(('dp', 'seq'))
- d_b_value: float32 [128], P(('dp', 'seq'))
- d_w_out: float32 [2048, 2048], P(('dp', 'seq'))
- d_b_out: float32 [2048], P(('dp', 'seq'))
- d_ln2_gain: float32 [2048], P(('dp', 'seq'))
- d_ln2_bias: float32 [2048], P(('dp', 'seq'))
- d_w_fc: float32 [2048, 8192], P(('dp', 'seq'))
- d_b_fc: float32 [8192], P(('dp', 'seq'))
- d_w_proj: float32 [8192, 2048], P(('dp', 'seq'))
- d_b_proj: float32 [2048], P(('dp', 'seq'))
The draws below stay inside these ranges and needn't reach their ends.
Inputs may be any that keep to these rules, and one draw needn't show every extreme that they name: `lengths`: tokens at positions at or beyond a window's length are padding.
All inputs are finite; a program needn't handle non-finite values.
Results may differ from the reference program's by a relative error of at most 0.014.
Values may be sent and summed in bfloat16 or wider, within the bound.
No kernel may reach another device: no remote copies, remote signals or barrier semaphores. Data moves between devices by JAX's collectives and lax.ppermute only.
A program may use at most 384 MiB of HBM per device.

```python
import math
import jax
import jax.numpy as jnp
from jax import lax

D = 2048
HEADS = 16
HEAD = 128
FF = 8192
REPOS = 4
LENGTH = 1024
WINDOWS = 8


def draw_lengths(key, part):
    key_base, key_long, key_short = jax.random.split(key, 3)
    drawn = jax.random.randint(key_base, (WINDOWS,), LENGTH // 8, LENGTH + 1, dtype=jnp.int32)
    longest = jax.random.randint(key_long, (), 0, WINDOWS, dtype=jnp.int32)
    offset = jax.random.randint(key_short, (), 1, WINDOWS, dtype=jnp.int32)
    shortest = (longest + offset) % WINDOWS
    slots = jnp.arange(WINDOWS, dtype=jnp.int32)
    drawn = jnp.where(slots == longest, LENGTH, drawn)
    drawn = jnp.where(slots == shortest, LENGTH // 8, drawn)
    return drawn


def plant(entries, key, smallest, high):
    extent = entries.shape
    place = [jax.random.randint(jax.random.fold_in(key, axis), (), 0, extent[axis]) for axis in range(len(extent))]
    entries = entries.at[tuple(place)].set(smallest)
    longest = extent.index(max(extent))
    place[longest] = (place[longest] + 1) % extent[longest]
    return entries.at[tuple(place)].set(high)


def steps_of(rng, dims, pieces, low, largest):
    loudness, own = 1.0, jax.random.fold_in(rng, 6)
    for axis_at, blocks in pieces:
        draws = jnp.exp(jax.random.uniform(jax.random.fold_in(own, axis_at), (blocks,), jnp.float32, low / len(pieces), largest / len(pieces)))
        loudness = loudness * jnp.repeat(draws, dims[axis_at] // blocks).reshape([-1 if axis == axis_at else 1 for axis in range(len(dims))])
    return loudness


def bell_draw(stream_key, extent, deviation, most, cuts=(), held_as=jnp.bfloat16):
    values = jax.random.normal(stream_key, extent, jnp.float32) * deviation
    if len(cuts) > 0:
        values = steps_of(stream_key, extent, cuts, -0.22, 0.18) * values
    return jnp.clip(values, min=-most, max=most).astype(held_as)


def setup_inputs(seed: int = 0) -> dict:
    keys = jax.random.split(jax.random.key(seed), 20)
    return {
        "tokens": bell_draw(keys[0], (WINDOWS, LENGTH, D), 1.0, 6.0, ((0, 8), (1, 4))),
        "lengths": draw_lengths(jax.random.fold_in(keys[19], 71), 0),
        "repos": plant(jax.random.randint(keys[2], (WINDOWS,), 0, REPOS), jax.random.fold_in(keys[2], 1), 0, REPOS - 1).astype(jnp.int32),
        "ln1_gain": jnp.clip(1.0 + 0.15 * jax.random.normal(keys[3], (D,), jnp.float32), 0.25, 1.75).astype(jnp.bfloat16),
        "ln1_bias": bell_draw(keys[4], (D,), 0.3, 2.0, ((0, 32),)),
        "w_query": bell_draw(keys[5], (D, D), D ** -0.5, 0.125, ((0, 32),)),
        "b_query": bell_draw(keys[6], (D,), 0.5, 3.0, ((0, 32),)),
        "w_key": bell_draw(keys[7], (D, HEAD), D ** -0.5, 0.125, ((0, 32),)),
        "w_value": bell_draw(keys[8], (D, HEAD), D ** -0.5, 0.125, ((0, 32),)),
        "b_value": bell_draw(keys[9], (HEAD,), 0.05, 0.29882812, ((0, 32),)),
        "w_out": bell_draw(keys[10], (D, D), (D // 128) ** -0.5, 1.5, ((0, 32),)),
        "b_out": bell_draw(keys[11], (D,), 0.5, 3.0, ((0, 32),)),
        "ln2_gain": jnp.clip(1.0 + 0.15 * jax.random.normal(keys[12], (D,), jnp.float32), 0.25, 1.75).astype(jnp.bfloat16),
        "ln2_bias": bell_draw(keys[13], (D,), 0.3, 2.0, ((0, 32),)),
        "w_fc": bell_draw(keys[14], (D, FF), D ** -0.5, 0.125, ((0, 32),)),
        "b_fc": bell_draw(keys[15], (FF,), 0.5, 3.0, ((0, 32),)),
        "w_proj": bell_draw(keys[16], (FF, D), FF ** -0.5, 0.0625, ((0, 32),)),
        "b_proj": bell_draw(keys[17], (D,), 0.5, 3.0, ((0, 32),)),
        "grad_out": bell_draw(keys[18], (WINDOWS, LENGTH, D), 1.0, 6.0, ((0, 8), (1, 4))),
    }


@jax.custom_vjp
def low(v):
    return lax.optimization_barrier(v.astype(jnp.bfloat16)).astype(jnp.float32)

@jax.custom_vjp
def low_back(v):
    return v

def low_keep(v):
    return (low(v), None)

def low_pass(kept, grad):
    return (grad,)

def back_keep(v):
    return (v, None)

def back_low(kept, grad):
    return (low(grad),)
low.defvjp(low_keep, low_pass)
low_back.defvjp(back_keep, back_low)

def matmul(left, right):
    return jnp.dot(left, right, precision=lax.Precision.HIGHEST)

def normalize(values, gain, offset):
    centre = lax.optimization_barrier(jnp.mean(values, axis=-1, keepdims=True))
    shifted = values - centre
    spread = lax.optimization_barrier(jnp.mean(shifted * shifted, axis=-1, keepdims=True))
    return shifted * lax.rsqrt(spread + 1e-05) * gain + offset

def layer(params, inputs, valid):
    ln1_gain, ln1_bias, w_query, b_query, w_key, w_value, b_value, w_out, b_out, ln2_gain, ln2_bias, w_fc, b_fc, w_proj, b_proj = params
    length = inputs.shape[0]
    attn_in = low(normalize(inputs, ln1_gain, ln1_bias))
    queries = low_back(low(matmul(attn_in, w_query) + b_query))
    key_rows = low_back(low(matmul(attn_in, w_key)))
    value_rows = low_back(low(matmul(attn_in, w_value) + b_value))
    block_len = math.gcd(length, 256)
    blocks = length // block_len
    query_blocks = queries.reshape(blocks, block_len, HEADS, HEAD)
    starts = jnp.arange(blocks, dtype=jnp.int32) * block_len
    scale = 1.0 / math.sqrt(HEAD)

    def attend(block_args):
        query_block, block_start = block_args
        scores = low_back(scale * jnp.einsum('thd,jd->thj', query_block, key_rows, precision=lax.Precision.HIGHEST))
        places = block_start + jnp.arange(block_len, dtype=jnp.int32)
        allowed = jnp.arange(length, dtype=jnp.int32)[None, None, :] <= places[:, None, None]
        scores = jnp.where(allowed, scores, -1e+30)
        probs = jax.nn.softmax(scores, axis=-1)
        return low_back(jnp.einsum('thj,jd->thd', low(probs), value_rows, precision=lax.Precision.HIGHEST))
    attended = lax.map(jax.checkpoint(attend), (query_blocks, starts))
    attn_low = low(attended.reshape(length, HEADS * HEAD) * valid[:, None])
    hidden_one = inputs + low_back(matmul(attn_low, w_out) + b_out)
    mlp_in = low(normalize(hidden_one, ln2_gain, ln2_bias))
    pre_act = low_back(matmul(mlp_in, w_fc) + b_fc)
    act_low = low(jax.nn.gelu(pre_act, approximate=True))
    return hidden_one + low_back(matmul(act_low, w_proj) + b_proj)

def reference(tokens, lengths, repos, ln1_gain, ln1_bias, w_query, b_query, w_key, w_value, b_value, w_out, b_out, ln2_gain, ln2_bias, w_fc, b_fc, w_proj, b_proj, grad_out):
    params = tuple((item.astype(jnp.float32) for item in (ln1_gain, ln1_bias, w_query, b_query, w_key, w_value, b_value, w_out, b_out, ln2_gain, ln2_bias, w_fc, b_fc, w_proj, b_proj)))
    repo_ids = jnp.arange(REPOS, dtype=jnp.int32)
    member = (repos[:, None] == repo_ids[None, :]).astype(jnp.float32)
    counts = lax.optimization_barrier(jnp.sum(member * lengths.astype(jnp.float32)[:, None], axis=0))
    overall = jnp.sum(counts)
    own_count = lax.optimization_barrier(jnp.sum(member * counts[None, :], axis=1))
    window_weight = overall / (REPOS * own_count)
    places = jnp.arange(LENGTH, dtype=jnp.int32)
    valid = (places[None, :] < lengths[:, None]).astype(jnp.float32)

    def step(carry, item):
        window_in, window_cot, window_valid, window_wt = item

        def forward(param_set, values):
            return layer(param_set, values, window_valid)
        result, pull = jax.vjp(forward, params, window_in.astype(jnp.float32))
        grad_params, grad_in = pull(window_cot.astype(jnp.float32) * (window_valid * window_wt)[:, None])
        carry = tuple((total + part for total, part in zip(carry, grad_params)))
        return (carry, (result.astype(jnp.bfloat16), grad_in.astype(jnp.bfloat16)))
    init = tuple((jnp.zeros(item.shape, jnp.float32) for item in params))
    grads, (outputs, grad_inputs) = lax.scan(step, init, (tokens, grad_out, valid, window_weight))
    return (outputs, grad_inputs, grads[0], grads[1], grads[2], grads[3], grads[4], grads[5], grads[6], grads[7], grads[8], grads[9], grads[10], grads[11], grads[12], grads[13], grads[14])
```

```python
import math

import jax
import jax.numpy as jnp
from jax import lax
from jax.experimental import pallas as pl
from jax.experimental.pallas import tpu as pltpu
from jax.sharding import PartitionSpec as P

HEADS = 16
HEAD = 128
REPOS = 4
BF = jnp.bfloat16
F32 = jnp.float32

norm_epsilon = 1e-05


def normalize(values, gain, offset):
    centre = jnp.mean(values, axis=-1, keepdims=True)
    shifted = values - centre
    inverse = lax.rsqrt(jnp.mean(shifted * shifted, axis=-1, keepdims=True) + norm_epsilon)
    normed = shifted * inverse
    return (normed * gain + offset, normed, inverse)


def normalize_back(grad_in, normed, inverse, gain):
    scaled = grad_in * gain
    first_mean = jnp.mean(scaled, axis=-1, keepdims=True)
    second_mean = jnp.mean(scaled * normed, axis=-1, keepdims=True)
    grad_values = inverse * (scaled - first_mean - normed * second_mean)
    return (grad_values, jnp.sum(grad_in * normed, axis=0), jnp.sum(grad_in, axis=0))


def gelu_tanh(values):
    return jax.nn.gelu(values, approximate=True)


def after(value, other):
    return lax.optimization_barrier((value, other))[0]


def dot32(left, right):
    return jnp.dot(left, right, preferred_element_type=F32)


def dot_t(left, right):
    return lax.dot_general(left, right, (((1,), (1,)), ((), ())), preferred_element_type=F32)


def t_dot(left, right):
    return lax.dot_general(left, right, (((0,), (0,)), ((), ())), preferred_element_type=F32)


class Ring:
    def __init__(self, dp, seq):
        self.nd, self.ns = dp, seq
        self.me = lax.axis_index("dp")
        self.z = lax.axis_index("seq")
        self.order = list(range(0, dp, 2)) + list(range(1, dp, 2))
        self.owners = [self.me ^ k for k in self.order]

    def swap(self, value, mask):
        return lax.ppermute(value, "dp", [(i, i ^ mask) for i in range(self.nd)])

    def up(self, value, by=1):
        return lax.ppermute(value, "seq", [(i, (i + by) % self.ns) for i in range(self.ns)])

    def back(self, step):
        return lax.rem(self.z - step + self.ns, self.ns)

    def seq_gather(self, block):
        pieces = [block]
        for _ in range(self.ns - 1):
            pieces.append(self.up(pieces[-1]))
        return pieces

    def seq_gather_near(self, block):
        return [block] + [self.up(block, step) for step in range(1, self.ns)]

    def seq_place(self, pieces, axis=0):
        shape = pieces[0].shape
        full = jnp.zeros(shape[:axis] + (self.ns,) + shape[axis:], pieces[0].dtype)
        for step, piece in enumerate(pieces):
            full = lax.dynamic_update_slice_in_dim(
                full, jnp.expand_dims(piece, axis), self.back(step), axis
            )
        return full

    def seq_scatter(self, part):
        total = part(self.back(1))
        for step in range(2, self.ns + 1):
            total = self.up(total.astype(BF)).astype(F32) + part(self.back(step))
        return total

    def seq_scatter_near(self, part):
        total = part(self.z)
        for step in range(1, self.ns):
            owner = lax.rem(self.z + step, self.ns)
            total = total + self.up(part(owner).astype(BF), step).astype(F32)
        return total

    def dp_gather(self, block):
        if self.nd == 8:
            half = block.shape[0] // 2
            over_x = self.swap(block, 2)
            over_y = self.swap(block, 4)
            first = self.swap(over_x[:half], 4)
            second = self.swap(over_y[half:], 2)
            even = [block, over_x, over_y, first, second]
        else:
            pieces = {0: block}
            bit = 2
            while bit < self.nd:
                for k in list(pieces):
                    pieces[k | bit] = self.swap(pieces[k], bit)
                bit *= 2
            even = [pieces[k] for k in range(0, self.nd, 2)]
        even = jnp.concatenate(even, axis=0)
        return even, self.swap(even, 1)

    def dp_scatter(self, even, odd):
        held = even.astype(F32) + self.swap(odd.astype(BF), 1).astype(F32)
        rows = held.shape[0] * 2 // self.nd
        if self.nd == 8:
            half = rows // 2
            low = self.swap(held[3 * rows : 3 * rows + half].astype(BF), 4).astype(F32)
            high = self.swap(held[3 * rows + half :].astype(BF), 2).astype(F32)
            to_x = jnp.concatenate(
                [held[rows : rows + half] + low, held[rows + half : 2 * rows]], axis=0
            )
            to_y = jnp.concatenate(
                [held[2 * rows : 2 * rows + half], held[2 * rows + half : 3 * rows] + high], axis=0
            )
            return (
                held[:rows]
                + self.swap(to_x.astype(BF), 2).astype(F32)
                + self.swap(to_y.astype(BF), 4).astype(F32)
            )
        bit = self.nd // 2
        while bit > 1:
            cut = held.shape[0] // 2
            held = held[:cut] + self.swap(held[cut:].astype(BF), bit).astype(F32)
            bit //= 2
        return held

    def relative(self, value):
        size = value.shape[-1] // self.nd
        return jnp.concatenate(
            [
                lax.dynamic_slice_in_dim(value, owner * size, size, value.ndim - 1)
                for owner in self.owners
            ],
            axis=-1,
        )

    def natural(self, value):
        size = value.shape[-1] // self.nd
        at = []
        for place in range(self.nd):
            mask = self.me ^ place
            at.append(lax.shift_right_logical(mask, 1) + (mask & 1) * (self.nd // 2))
        return jnp.concatenate(
            [lax.dynamic_slice_in_dim(value, a * size, size, value.ndim - 1) for a in at], axis=-1
        )


LOG2E = 1.4426950408889634


def attend_kernel(info, query, key, value_t, valid, out, log_total, *, heads, scale):
    keys = key.shape[0]
    rows = query.shape[0]
    place = lax.broadcasted_iota(jnp.int32, (keys, rows), 1) + info[0]
    allowed = lax.broadcasted_iota(jnp.int32, (keys, rows), 0) <= place
    for h in range(heads):
        cols = slice(h * HEAD, (h + 1) * HEAD)
        scores = dot_t(key[...], query[:, cols]) * (scale * LOG2E)
        scores = jnp.where(allowed, scores, -1e30)
        top = jnp.max(scores, axis=0, keepdims=True)
        expo = jnp.exp2(scores - top)
        total = jnp.sum(expo, axis=0, keepdims=True)
        mixed = dot32(value_t[...], expo.astype(BF)) * (1.0 / total)
        out[:, cols] = (jnp.transpose(mixed) * valid[...]).astype(BF)
        log_total[h] = top + jnp.log2(total)


def attend(info, query, key, value_t, valid, pairs, scale):
    rows, width = query.shape
    keys = key.shape[0]
    heads = HEADS // pairs
    step = heads * HEAD
    whole = lambda k, info: (0, 0)
    return pl.pallas_call(
        lambda *refs: attend_kernel(*refs, heads=heads, scale=scale),
        grid_spec=pltpu.PrefetchScalarGridSpec(
            num_scalar_prefetch=1,
            grid=(pairs,),
            in_specs=[
                pl.BlockSpec((rows, step), lambda k, info: (0, info[1 + k])),
                pl.BlockSpec((keys, HEAD), whole),
                pl.BlockSpec((HEAD, keys), whole),
                pl.BlockSpec((rows, 1), whole),
            ],
            out_specs=[
                pl.BlockSpec((rows, step), lambda k, info: (0, k)),
                pl.BlockSpec((heads, 1, rows), lambda k, info: (k, 0, 0)),
            ],
        ),
        out_shape=[
            jax.ShapeDtypeStruct((rows, width), BF),
            jax.ShapeDtypeStruct((HEADS, 1, rows), F32),
        ],
        compiler_params=pltpu.CompilerParams(vmem_limit_bytes=48 * 1024 * 1024),
        cost_estimate=pl.CostEstimate(
            flops=4 * rows * width * keys,
            bytes_accessed=4 * rows * width,
            transcendentals=rows * HEADS * keys,
        ),
    )(info, query, key, value_t, valid)


def attend_back_kernel(
    info, query, grad, log_total, key, key_t, value, out, key_grad, value_grad, *, heads, scale
):
    keys = key.shape[0]
    rows = query.shape[0]
    place = lax.broadcasted_iota(jnp.int32, (keys, rows), 1) + info[0]
    allowed = lax.broadcasted_iota(jnp.int32, (keys, rows), 0) <= place

    @pl.when(pl.program_id(0) == 0)
    def _():
        key_grad[...] = jnp.zeros_like(key_grad)
        value_grad[...] = jnp.zeros_like(value_grad)

    for h in range(heads):
        cols = slice(h * HEAD, (h + 1) * HEAD)
        scores = dot_t(key[...], query[:, cols]) * (scale * LOG2E)
        scores = jnp.where(allowed, scores, -1e30)
        probs = jnp.exp2(scores - log_total[h])
        dprobs = dot_t(value[...], grad[:, cols])
        delta = jnp.sum(probs * dprobs, axis=0, keepdims=True)
        dscores = (probs * (dprobs - delta)).astype(BF)
        value_grad[...] += dot32(probs.astype(BF), grad[:, cols])
        key_grad[...] += dot32(dscores, query[:, cols]) * scale
        back = dot32(key_t[...], dscores) * scale
        out[:, cols] = jnp.transpose(back).astype(BF)


def attend_back(info, query, grad, log_total, key, key_t, value, pairs, scale):
    rows, width = query.shape
    keys = key.shape[0]
    heads = HEADS // pairs
    step = heads * HEAD
    whole = lambda k, info: (0, 0)
    natural = lambda k, info: (0, info[1 + k])
    return pl.pallas_call(
        lambda *refs: attend_back_kernel(*refs, heads=heads, scale=scale),
        grid_spec=pltpu.PrefetchScalarGridSpec(
            num_scalar_prefetch=1,
            grid=(pairs,),
            in_specs=[
                pl.BlockSpec((rows, step), natural),
                pl.BlockSpec((rows, step), lambda k, info: (0, k)),
                pl.BlockSpec((heads, 1, rows), lambda k, info: (k, 0, 0)),
                pl.BlockSpec((keys, HEAD), whole),
                pl.BlockSpec((HEAD, keys), whole),
                pl.BlockSpec((keys, HEAD), whole),
            ],
            out_specs=[
                pl.BlockSpec((rows, step), natural),
                pl.BlockSpec((keys, HEAD), whole),
                pl.BlockSpec((keys, HEAD), whole),
            ],
        ),
        out_shape=[
            jax.ShapeDtypeStruct((rows, width), BF),
            jax.ShapeDtypeStruct((keys, HEAD), F32),
            jax.ShapeDtypeStruct((keys, HEAD), F32),
        ],
        compiler_params=pltpu.CompilerParams(vmem_limit_bytes=48 * 1024 * 1024),
        cost_estimate=pl.CostEstimate(
            flops=10 * rows * width * keys,
            bytes_accessed=6 * rows * width,
            transcendentals=rows * HEADS * keys,
        ),
    )(info, query, grad, log_total, key, key_t, value)


def local(
    dp,
    seq,
    tokens,
    lengths,
    repos,
    ln1_gain,
    ln1_bias,
    w_query,
    b_query,
    w_key,
    w_value,
    b_value,
    w_out,
    b_out,
    ln2_gain,
    ln2_bias,
    w_fc,
    b_fc,
    w_proj,
    b_proj,
    grad_out,
):
    ring = Ring(dp, seq)
    me, z = ring.me, ring.z
    windows, span, width = tokens.shape
    rows = windows * span
    own = w_query.shape[0]
    block = own * seq
    hidden = w_fc.shape[1]
    part = hidden // dp
    piece = part // seq
    scale = 1.0 / math.sqrt(HEAD)
    kv_end = width + 2 * HEAD
    pairs = dp
    all_rows = dp * rows
    half_rows = all_rows // 2

    size_hi = lax.div(lengths, jnp.int32(64))
    columns = [
        ln1_gain[:, None],
        ln1_bias[:, None],
        b_query[:, None],
        b_out[:, None],
        ln2_gain[:, None],
        ln2_bias[:, None],
        b_proj[:, None],
        jnp.pad(b_value, (0, own - b_value.shape[0]))[:, None],
        jnp.broadcast_to(size_hi.astype(BF), (own,))[:, None],
        jnp.broadcast_to((lengths - 64 * size_hi).astype(BF), (own,))[:, None],
        jnp.broadcast_to(repos.astype(BF), (own,))[:, None],
        jnp.transpose(b_fc.reshape(-1, own)),
    ]
    n_plain = 11
    n_fc = b_fc.shape[0] // own
    vector_block = jnp.concatenate(columns, axis=1)
    vector_block = jnp.pad(vector_block, ((0, 0), (0, HEAD - vector_block.shape[1])))
    w_qkv = jnp.concatenate([w_query, w_key, w_value, vector_block], axis=1)

    qkv_z = ring.seq_gather(w_qkv)
    raw_even, raw_odd = ring.dp_gather(grad_out.reshape(rows, width))
    fc_turned = lax.all_to_all(
        w_fc.reshape(own, dp, part), "dp", split_axis=1, concat_axis=0, tiled=False
    ).reshape(dp * own, part)
    qkv_block = after(ring.seq_place(qkv_z).reshape(block, -1), raw_even)
    qkv_even, qkv_odd = ring.dp_gather(qkv_block)
    out_z = ring.seq_gather(after(w_out, qkv_z[-1]))
    out_block = after(ring.seq_place(out_z).reshape(block, -1), qkv_even)
    out_even, out_odd = ring.dp_gather(out_block)
    fc_z = ring.seq_gather(after(fc_turned, out_z[-1]))
    fc_all = ring.seq_place([p.reshape(dp, own, part) for p in fc_z], axis=1).reshape(width, part)
    proj_z = ring.seq_gather(after(w_proj, fc_z[-1]))
    proj_all = ring.seq_place(proj_z).reshape(part, width)

    vectors = jnp.transpose(
        jnp.concatenate([qkv_even[:, kv_end:], qkv_odd[:, kv_end:]], axis=0)
    ).astype(F32)
    g1, o1 = vectors[0], vectors[1]
    straight = ring.natural(vectors[:n_plain])
    bq, bo, g2, o2, bp = (straight[n] for n in range(2, 7))
    bv = straight[7].reshape(dp * seq, own)[:, : b_value.shape[0]].reshape(-1)
    heads_of = lambda n: straight[n].reshape(dp, block)[:, 0]
    all_lengths = heads_of(8) * 64.0 + heads_of(9)
    all_repos = heads_of(10)
    bf_own = jnp.transpose(
        vectors[n_plain : n_plain + n_fc, :block].reshape(n_fc, seq, own), (1, 0, 2)
    ).reshape(part)

    first_place = z * span
    places = first_place + jnp.arange(span, dtype=jnp.int32)
    same = (all_repos[None, :] == all_repos[:, None]).astype(F32)
    weights = jnp.sum(all_lengths) / (REPOS * jnp.sum(same * all_lengths[None, :], axis=1))
    rel_lengths = jnp.stack([all_lengths[o] for o in ring.owners])
    rel_weights = jnp.stack([weights[o] for o in ring.owners])
    all_valid = (places[None, :].astype(F32) < rel_lengths[:, None]).astype(F32)
    row_scale = (all_valid * rel_weights[:, None]).reshape(all_rows, 1)
    valid_rows = all_valid[0].reshape(rows, 1)

    two_even = (raw_even.astype(F32) * row_scale[:half_rows]).astype(BF)
    two_odd = (raw_odd.astype(F32) * row_scale[half_rows:]).astype(BF)
    two_all = jnp.concatenate([two_even, two_odd], axis=0)
    grad_top = grad_out.reshape(rows, width).astype(F32) * row_scale[:rows]
    d_b_proj = jnp.sum(grad_top.astype(BF).astype(F32), axis=0)

    token_rows = tokens.reshape(rows, width)
    normed1_out, normed1, inverse1 = normalize(ring.relative(token_rows).astype(F32), g1, o1)
    attn_in = normed1_out.astype(BF)
    cut = width // 2
    qkv = dot32(attn_in[:, :cut], qkv_even) + dot32(attn_in[:, cut:], qkv_odd)
    query_low = (qkv[:, :width] + bq).astype(BF)
    kv_low = jnp.concatenate(
        [qkv[:, width : width + HEAD], qkv[:, width + HEAD : kv_end] + bv], axis=1
    ).astype(BF)
    kv_all = ring.seq_place(ring.seq_gather_near(kv_low)).reshape(seq * span, 2 * HEAD)
    key_all, value_all = kv_all[:, :HEAD], kv_all[:, HEAD:]
    info = jnp.stack([first_place] + ring.owners)
    attn_low, log_total = attend(
        info, query_low, key_all, jnp.transpose(value_all), valid_rows, pairs, scale
    )
    hidden_one = (
        token_rows.astype(F32)
        + dot32(attn_low[:, :cut], out_even)
        + dot32(attn_low[:, cut:], out_odd)
        + bo
    )

    normed2_out, normed2, inverse2 = normalize(hidden_one, g2, o2)
    mlp_even, mlp_odd = ring.dp_gather(normed2_out.astype(BF))
    mlp_all = jnp.concatenate([mlp_even, mlp_odd], axis=0)
    pre_act = dot32(mlp_all, fc_all) + bf_own
    act_low = gelu_tanh(pre_act).astype(BF)
    d_w_proj = ring.seq_scatter(
        lambda owner: t_dot(
            lax.dynamic_slice(act_low, (0, owner * piece), (all_rows, piece)), two_all
        )
    )
    grad_act = dot_t(two_all, proj_all)
    gelu_pull = jax.vjp(gelu_tanh, pre_act)[1]
    grad_pre = gelu_pull(grad_act)[0].astype(BF)
    d_b_fc = jnp.sum(grad_pre.astype(F32), axis=0)
    grad_mlp_odd = dot_t(grad_pre[half_rows:], fc_all).astype(BF)
    grad_mlp_even = dot_t(grad_pre[:half_rows], fc_all)
    grad_mlp_in = ring.dp_scatter(grad_mlp_even, grad_mlp_odd)
    branch_odd = dot32(act_low[half_rows:], after(proj_all, grad_mlp_in)).astype(BF)
    branch_even = dot32(act_low[:half_rows], proj_all)
    branch_two = ring.dp_scatter(branch_even, branch_odd)
    output = (hidden_one + branch_two + bp).astype(BF).reshape(windows, span, width)
    d_fc = t_dot(mlp_all, after(grad_pre, d_w_proj)).reshape(dp, seq, own, part)
    fc_share = ring.seq_scatter(
        lambda owner: lax.dynamic_slice_in_dim(d_fc, owner, 1, 1).reshape(dp, own, part)
    )
    d_w_fc = (
        lax.all_to_all(fc_share.astype(BF), "dp", split_axis=0, concat_axis=1, tiled=False)
        .reshape(own, hidden)
        .astype(F32)
    )

    grad_norm2, d_g2, d_o2 = normalize_back(grad_mlp_in, normed2, inverse2, g2)
    grad_mid = grad_top + grad_norm2
    grad_one = grad_mid.astype(BF)
    d_b_out = jnp.sum(grad_one.astype(F32), axis=0)

    def scatter_rows(even, odd):
        share = ring.dp_scatter(even, odd)
        return ring.seq_scatter(lambda owner: lax.dynamic_slice_in_dim(share, owner * own, own, 0))

    d_w_out = scatter_rows(
        t_dot(attn_low[:, :cut], grad_one), t_dot(attn_low[:, cut:], grad_one).astype(BF)
    )
    grad_att = jnp.concatenate([dot_t(grad_one, out_even), dot_t(grad_one, out_odd)], axis=1)
    grad_att = (grad_att * valid_rows).astype(BF)
    query_grad, key_grad, value_grad = attend_back(
        info, query_low, grad_att, log_total, key_all, jnp.transpose(key_all), value_all, pairs, scale
    )
    kv_grads = jnp.concatenate([key_grad, value_grad], axis=1).reshape(seq, rows, 2 * HEAD)
    kv_grad = ring.seq_scatter_near(
        lambda owner: lax.dynamic_slice_in_dim(kv_grads, owner, 1, 0)[0]
    ).astype(BF)
    qkv_grad = jnp.concatenate([query_grad, kv_grad], axis=1)
    grad_attn_in = jnp.concatenate(
        [dot_t(qkv_grad, qkv_even[:, :kv_end]), dot_t(qkv_grad, qkv_odd[:, :kv_end])], axis=1
    )
    grad_norm1, d_g1, d_o1 = normalize_back(grad_attn_in, normed1, inverse1, g1)
    grad_tokens = (grad_mid + ring.natural(grad_norm1)).astype(BF).reshape(windows, span, width)
    d_b_query = jnp.sum(query_grad.astype(F32), axis=0)
    d_b_value = jnp.sum(kv_grad[:, HEAD:].astype(F32), axis=0)

    d_bv = jnp.pad(
        d_b_value.reshape(dp * seq, -1), ((0, 0), (0, own - b_value.shape[0]))
    ).reshape(-1)
    straight = jnp.stack([d_b_query, d_b_out, d_g2, d_o2, d_b_proj, d_bv])
    d_bf = jnp.pad(
        jnp.transpose(d_b_fc.reshape(seq, n_fc, own), (1, 0, 2)).reshape(n_fc, block),
        ((0, 0), (0, width - block)),
    )
    vector_grads = jnp.concatenate([d_g1[None], d_o1[None], ring.relative(straight), d_bf], axis=0)
    vector_grads = jnp.transpose(jnp.pad(vector_grads, ((0, HEAD - 8 - n_fc), (0, 0))))
    d_qkv = scatter_rows(
        jnp.concatenate([t_dot(attn_in[:, :cut], qkv_grad), vector_grads[:cut]], axis=1),
        jnp.concatenate(
            [t_dot(attn_in[:, cut:], qkv_grad).astype(BF), vector_grads[cut:].astype(BF)], axis=1
        ),
    )
    small = jnp.transpose(d_qkv[:, kv_end : kv_end + 8 + n_fc])
    return (
        output,
        grad_tokens,
        small[0],
        small[1],
        d_qkv[:, :width],
        small[2],
        d_qkv[:, width : width + HEAD],
        d_qkv[:, width + HEAD : kv_end],
        small[7, : b_value.shape[0]],
        d_w_out,
        small[3],
        small[4],
        small[5],
        d_w_fc,
        small[8:].reshape(-1),
        d_w_proj,
        small[6],
    )


def solution(mesh):
    dp, seq = mesh.shape["dp"], mesh.shape["seq"]
    both = P(("dp", "seq"))
    rows = P(("dp", "seq"), None)
    token = P("dp", "seq", None)

    def run(*args):
        return local(dp, seq, *args)

    return jax.shard_map(
        run,
        mesh=mesh,
        in_specs=(
            token,
            P("dp"),
            P("dp"),
            both,
            both,
            rows,
            both,
            rows,
            rows,
            both,
            rows,
            both,
            both,
            both,
            rows,
            both,
            rows,
            both,
            token,
        ),
        out_specs=(
            token,
            token,
            both,
            both,
            rows,
            both,
            rows,
            rows,
            both,
            rows,
            both,
            both,
            both,
            rows,
            both,
            rows,
            both,
        ),
        check_vma=False,
    )
```

```python
import math

import jax
import jax.numpy as jnp
from jax import lax
from jax.experimental import pallas as pl
from jax.experimental.pallas import tpu as pltpu
from jax.sharding import PartitionSpec as P

HEADS = 16
HEAD = 128
REPOS = 4
BF = jnp.bfloat16
F32 = jnp.float32

norm_epsilon = 1e-05


def normed(values):
    centre = jnp.mean(values, axis=-1, keepdims=True)
    shifted = values - centre
    inverse = lax.rsqrt(jnp.mean(shifted * shifted, axis=-1, keepdims=True) + norm_epsilon)
    return shifted * inverse, inverse


def dot32(left, right):
    return jnp.dot(left, right, preferred_element_type=F32)


def dot_t(left, right):
    return lax.dot_general(left, right, (((1,), (1,)), ((), ())), preferred_element_type=F32)


def t_dot(left, right):
    return lax.dot_general(left, right, (((0,), (0,)), ((), ())), preferred_element_type=F32)


class Ring:
    def __init__(self, dp, seq):
        self.nd, self.ns = dp, seq
        self.me = lax.axis_index("dp")
        self.z = lax.axis_index("seq")
        self.order = list(range(0, dp, 2)) + list(range(1, dp, 2))
        self.owners = [self.me ^ k for k in self.order]

    def swap(self, value, mask):
        return lax.ppermute(value, "dp", [(i, i ^ mask) for i in range(self.nd)])

    def up(self, value, by=1):
        return lax.ppermute(value, "seq", [(i, (i + by) % self.ns) for i in range(self.ns)])

    def back(self, step):
        return lax.rem(self.z - step + self.ns, self.ns)

    def seq_gather_near(self, block):
        return [block] + [self.up(block, step) for step in range(1, self.ns)]

    def seq_place(self, pieces, axis=0):
        shape = pieces[0].shape
        full = jnp.zeros(shape[:axis] + (self.ns,) + shape[axis:], pieces[0].dtype)
        for step, piece in enumerate(pieces):
            full = lax.dynamic_update_slice_in_dim(
                full, jnp.expand_dims(piece, axis), self.back(step), axis
            )
        return full

    def seq_scatter_near(self, part):
        total = part(self.z)
        for step in range(1, self.ns):
            owner = lax.rem(self.z + step, self.ns)
            total = total + self.up(part(owner).astype(BF), step).astype(F32)
        return total

    def cross(self, block):
        if self.nd == 8:
            return self.swap(block, 2), self.swap(block, 4)
        return ()

    def first(self, block, near):
        if self.nd == 8:
            three = (block,) + tuple(near)
            return three + tuple(self.swap(piece, 1) for piece in three)
        return ()

    def corner(self, block, near):
        if self.nd == 8:
            half = block.shape[0] // 2
            return self.swap(near[0][:half], 4), self.swap(near[1][half:], 2)
        pieces = {0: block}
        bit = 2
        while bit < self.nd:
            for k in list(pieces):
                pieces[k | bit] = self.swap(pieces[k], bit)
            bit *= 2
        return tuple(pieces[k] for k in range(0, self.nd, 2))

    def second(self, far):
        far = jnp.concatenate(far, axis=0)
        return far, self.swap(far, 1)

    def pieces(self, first, second):
        if self.nd == 8:
            return first[:3] + second[:1] + first[3:] + second[1:]
        return second

    def other(self, value):
        return self.swap(value, 1)

    def corner_sums(self, even, other):
        if self.nd != 8:
            return ()
        rows = even.shape[0] // 4
        at = 3 * rows
        half = rows // 2
        held = even[at:].astype(F32) + other[at:].astype(F32)
        return held[:half].astype(BF), held[half:].astype(BF)

    def send_corner(self, sums):
        if self.nd != 8:
            return ()
        return self.swap(sums[0], 4), self.swap(sums[1], 2)

    def cross_sums(self, even, other, far):
        if self.nd == 8:
            rows = even.shape[0] // 4
            half = rows // 2

            def held(start, size):
                return even[start : start + size].astype(F32) + other[start : start + size].astype(
                    F32
                )

            low, high = far
            to_x = jnp.concatenate(
                [
                    (held(rows, half) + low.astype(F32)).astype(BF),
                    held(rows + half, half).astype(BF),
                ],
                axis=0,
            )
            to_y = jnp.concatenate(
                [
                    held(2 * rows, half).astype(BF),
                    (held(2 * rows + half, half) + high.astype(F32)).astype(BF),
                ],
                axis=0,
            )
            return to_x, to_y
        held = even.astype(F32) + other.astype(F32)
        bit = self.nd // 2
        while bit > 2:
            cut = held.shape[0] // 2
            held = held[:cut] + self.swap(held[cut:].astype(BF), bit).astype(F32)
            bit //= 2
        return held.astype(BF), jnp.zeros_like(even[: even.shape[0] // (self.nd // 2)])

    def send_cross(self, sums):
        if self.nd == 8:
            return self.swap(sums[0], 2), self.swap(sums[1], 4)
        cut = sums[0].shape[0] // 2
        return self.swap(sums[0][cut:], 2), sums[0][:cut]

    def ends(self, even, other, near):
        if self.nd == 8:
            return even, other, near[0], near[1]
        nothing = jnp.zeros_like(near[0])
        return near[0], near[1], nothing, nothing

    def scatter_end(self, even, other, near):
        rows = even.shape[0] * 2 // self.nd
        return sum(part[:rows].astype(F32) for part in self.ends(even, other, near))


LOG2E = 1.4426950408889634


def attend_kernel(info, query, key, value_t, valid, out, log_total, *, heads, scale):
    keys = key.shape[0]
    rows = query.shape[0]
    place = lax.broadcasted_iota(jnp.int32, (keys, rows), 1) + info[0]
    allowed = lax.broadcasted_iota(jnp.int32, (keys, rows), 0) <= place
    for h in range(heads):
        cols = slice(h * HEAD, (h + 1) * HEAD)
        scores = dot_t(key[...], query[:, cols]) * (scale * LOG2E)
        scores = jnp.where(allowed, scores, -1e30)
        top = jnp.max(scores, axis=0, keepdims=True)
        expo = jnp.exp2(scores - top)
        total = jnp.sum(expo, axis=0, keepdims=True)
        mixed = dot32(value_t[...], expo.astype(BF)) * (1.0 / total)
        out[:, cols] = (jnp.transpose(mixed) * valid[...]).astype(BF)
        log_total[h] = top + jnp.log2(total)


def attend(info, query, key, value_t, valid, pairs, scale):
    rows, width = query.shape
    keys = key.shape[0]
    heads = HEADS // pairs
    step = heads * HEAD
    whole = lambda k, info: (0, 0)
    return pl.pallas_call(
        lambda *refs: attend_kernel(*refs, heads=heads, scale=scale),
        grid_spec=pltpu.PrefetchScalarGridSpec(
            num_scalar_prefetch=1,
            grid=(pairs,),
            in_specs=[
                pl.BlockSpec((rows, step), lambda k, info: (0, info[1 + k])),
                pl.BlockSpec((keys, HEAD), whole),
                pl.BlockSpec((HEAD, keys), whole),
                pl.BlockSpec((rows, 1), whole),
            ],
            out_specs=[
                pl.BlockSpec((rows, step), lambda k, info: (0, k)),
                pl.BlockSpec((heads, 1, rows), lambda k, info: (k, 0, 0)),
            ],
        ),
        out_shape=[
            jax.ShapeDtypeStruct((rows, width), BF),
            jax.ShapeDtypeStruct((HEADS, 1, rows), F32),
        ],
        compiler_params=pltpu.CompilerParams(vmem_limit_bytes=48 * 1024 * 1024),
        cost_estimate=cost(),
    )(info, query, key, value_t, valid)


def attend_back_kernel(
    info, query, grad, log_total, key, key_t, value, out, key_grad, value_grad, *, heads, scale
):
    keys = key.shape[0]
    rows = query.shape[0]
    place = lax.broadcasted_iota(jnp.int32, (keys, rows), 1) + info[0]
    allowed = lax.broadcasted_iota(jnp.int32, (keys, rows), 0) <= place

    @pl.when(pl.program_id(0) == 0)
    def _():
        key_grad[...] = jnp.zeros_like(key_grad)
        value_grad[...] = jnp.zeros_like(value_grad)

    for h in range(heads):
        cols = slice(h * HEAD, (h + 1) * HEAD)
        scores = dot_t(key[...], query[:, cols]) * (scale * LOG2E)
        scores = jnp.where(allowed, scores, -1e30)
        probs = jnp.exp2(scores - log_total[h])
        dprobs = dot_t(value[...], grad[:, cols])
        delta = jnp.sum(probs * dprobs, axis=0, keepdims=True)
        dscores = (probs * (dprobs - delta)).astype(BF)
        value_grad[...] += dot32(probs.astype(BF), grad[:, cols])
        key_grad[...] += dot32(dscores, query[:, cols]) * scale
        back = dot32(key_t[...], dscores) * scale
        out[:, cols] = jnp.transpose(back).astype(BF)


def attend_back(info, query, grad, log_total, key, key_t, value, pairs, scale):
    rows, width = query.shape
    keys = key.shape[0]
    heads = HEADS // pairs
    step = heads * HEAD
    whole = lambda k, info: (0, 0)
    natural = lambda k, info: (0, info[1 + k])
    return pl.pallas_call(
        lambda *refs: attend_back_kernel(*refs, heads=heads, scale=scale),
        grid_spec=pltpu.PrefetchScalarGridSpec(
            num_scalar_prefetch=1,
            grid=(pairs,),
            in_specs=[
                pl.BlockSpec((rows, step), natural),
                pl.BlockSpec((rows, step), lambda k, info: (0, k)),
                pl.BlockSpec((heads, 1, rows), lambda k, info: (k, 0, 0)),
                pl.BlockSpec((keys, HEAD), whole),
                pl.BlockSpec((HEAD, keys), whole),
                pl.BlockSpec((keys, HEAD), whole),
            ],
            out_specs=[
                pl.BlockSpec((rows, step), natural),
                pl.BlockSpec((keys, HEAD), whole),
                pl.BlockSpec((keys, HEAD), whole),
            ],
        ),
        out_shape=[
            jax.ShapeDtypeStruct((rows, width), BF),
            jax.ShapeDtypeStruct((keys, HEAD), F32),
            jax.ShapeDtypeStruct((keys, HEAD), F32),
        ],
        compiler_params=pltpu.CompilerParams(vmem_limit_bytes=48 * 1024 * 1024),
        cost_estimate=cost(),
    )(info, query, grad, log_total, key, key_t, value)


def fetches(gathered, weight, sems):
    return [
        pltpu.make_async_copy(gathered.at[n], weight.at[:, n], sems.at[n])
        for n in range(gathered.shape[0])
    ]


def row_copies(pieces, full, sems):
    copies = []
    at = 0
    for n, piece in enumerate(pieces):
        size = piece.shape[0]
        copies.append((at, pltpu.make_async_copy(piece, full.at[pl.ds(at, size)], sems.at[n])))
        at += size
    return copies


ROOT = math.sqrt(2.0 / math.pi)
CUBIC = 0.044715


def row_tile(rows):
    return math.gcd(rows, 512)


def by_row(i, *_):
    return (i, 0)


def by_column(i, *_):
    return (0, i)


def fixed(i, *_):
    return (0, 0)


IN_VMEM = pl.BlockSpec(memory_space=pltpu.VMEM)
IN_SMEM = pl.BlockSpec(memory_space=pltpu.SMEM)
ANYWHERE = pl.BlockSpec(memory_space=pl.ANY)


PARAMS = pltpu.CompilerParams(vmem_limit_bytes=54 * 1024 * 1024)


def cost(*_):
    return pl.CostEstimate(flops=1024, bytes_accessed=1024, transcendentals=0)


def columns_of(info, n, size):
    return pl.ds(pl.multiple_of(info[1 + n] * size, HEAD), size)


N_VECTORS = 16


def stack_rows(*lines):
    width = lines[0].shape[1]
    at = lax.broadcasted_iota(jnp.int32, (8, width), 0)
    rows = jnp.zeros((8, width), F32)
    for n, line in enumerate(lines):
        rows = jnp.where(at == n, line, rows)
    return rows


def vmem(shape, dtype):
    return pltpu.VMEM(shape, dtype)


def enter_call(info, tokens, pieces, dp, own, n_value):
    rows, width = tokens.shape
    block = width // dp
    wide = pieces[0].shape[1]
    kv_end = wide - HEAD
    count = len(pieces)

    def kernel(info, tokens, *refs):
        attn, query, kv, rel, nat, weight, sems = refs[count:]
        copies = row_copies(refs[:count], weight, sems)
        for _, copy in copies:
            copy.start()
        x = tokens[...].astype(F32)
        centre = jnp.mean(x, axis=-1, keepdims=True)
        x = x - centre
        inverse = lax.rsqrt(jnp.mean(x * x, axis=-1, keepdims=True) + norm_epsilon)
        for _, copy in copies:
            copy.wait()
        for n in range(dp):
            mine = slice(n * block, (n + 1) * block)
            place = columns_of(info, n, block)
            vectors = jnp.transpose(weight[mine, kv_end:].astype(F32))[:N_VECTORS]
            rel[:, mine] = vectors
            nat[:, place] = vectors
            x = tokens[:, place].astype(F32)
            attn[:, mine] = ((x - centre) * inverse * vectors[0:1] + vectors[1:2]).astype(BF)
        at = lax.broadcasted_iota(jnp.int32, (width, HEAD), 0)
        d = lax.broadcasted_iota(jnp.int32, (width, HEAD), 1)
        chosen = (at == lax.div(d, n_value) * own + lax.rem(d, n_value)).astype(BF)
        offset = dot32(nat[...].astype(BF), chosen)[7:8]
        both = dot32(attn[...], weight[:, width:kv_end])
        kv[:, :HEAD] = both[:, :HEAD].astype(BF)
        kv[:, HEAD:] = (both[:, HEAD:] + offset).astype(BF)
        for at in range(0, width, 512):
            mine = slice(at, at + 512)
            query[:, mine] = (dot32(attn[...], weight[:, mine]) + nat[2:3, mine]).astype(BF)

    return pl.pallas_call(
        kernel,
        name="enter",
        in_specs=[IN_SMEM, IN_VMEM] + [ANYWHERE] * count,
        out_specs=[IN_VMEM] * 5,
        scratch_shapes=[vmem((width, wide), BF), pltpu.SemaphoreType.DMA((count,))],
        out_shape=[
            jax.ShapeDtypeStruct((rows, width), BF),
            jax.ShapeDtypeStruct((rows, width), BF),
            jax.ShapeDtypeStruct((rows, 2 * HEAD), BF),
            jax.ShapeDtypeStruct((N_VECTORS, width), F32),
            jax.ShapeDtypeStruct((N_VECTORS, width), F32),
        ],
        compiler_params=PARAMS,
        cost_estimate=cost(2 * rows * width * kv_end, tokens, *pieces),
    )(info, tokens, *pieces)


def leave_call(attn, pieces, tokens, nat):
    rows, width = tokens.shape
    count = len(pieces)

    def kernel(attn, tokens, nat, *refs):
        hidden, mlp, weight, sems = refs[count:]
        copies = row_copies(refs[:count], weight, sems)
        for _, copy in copies:
            copy.start()
        for _, copy in copies:
            copy.wait()
        for at in range(0, width, 512):
            mine = slice(at, at + 512)
            hidden[:, mine] = (
                dot32(attn[...], weight[:, mine]) + tokens[:, mine].astype(F32) + nat[3:4, mine]
            )
        mlp[...] = (normed(hidden[...])[0] * nat[4:5] + nat[5:6]).astype(BF)

    return pl.pallas_call(
        kernel,
        name="leave",
        in_specs=[IN_VMEM] * 3 + [ANYWHERE] * count,
        out_specs=[IN_VMEM] * 2,
        scratch_shapes=[vmem((width, width), BF), pltpu.SemaphoreType.DMA((count,))],
        out_shape=[
            jax.ShapeDtypeStruct((rows, width), F32),
            jax.ShapeDtypeStruct((rows, width), BF),
        ],
        compiler_params=PARAMS,
        cost_estimate=cost(2 * rows * width * width, tokens, *pieces),
    )(attn, tokens, nat, *pieces)


def middle_call(grads, hidden, top, row_scale, valid, nat, pieces):
    rows, width = hidden.shape
    count = len(pieces)

    def kernel(g0, g1, g2, g3, hidden, top, scale, valid, nat, *refs):
        mid, one, sums, att, weight, sems = refs[count:]
        copies = row_copies(refs[:count], weight, sems)
        for _, copy in copies:
            copy.start()
        grad = (
            g0[...].astype(F32) + g1[...].astype(F32) + g2[...].astype(F32) + g3[...].astype(F32)
        )
        norm, inverse = normed(hidden[...])
        scaled = grad * nat[4:5]
        first = jnp.mean(scaled, axis=-1, keepdims=True)
        second = jnp.mean(scaled * norm, axis=-1, keepdims=True)
        grad_top = top[...].astype(F32) * scale[...]
        total = grad_top + inverse * (scaled - first - norm * second)
        mid[...] = total
        low = total.astype(BF)
        one[...] = low
        sums[...] = stack_rows(
            jnp.sum(low.astype(F32), axis=0, keepdims=True),
            jnp.sum(grad * norm, axis=0, keepdims=True),
            jnp.sum(grad, axis=0, keepdims=True),
            jnp.sum(grad_top.astype(BF).astype(F32), axis=0, keepdims=True),
        )
        for _, copy in copies:
            copy.wait()
        for at in range(0, width, 512):
            mine = slice(at, at + 512)
            att[:, mine] = (dot_t(one[...], weight[mine, :]) * valid[...]).astype(BF)

    return pl.pallas_call(
        kernel,
        name="middle",
        grid=(1,),
        in_specs=[pl.BlockSpec((rows, width), fixed)] * 4
        + [IN_VMEM] * 5
        + [ANYWHERE] * count,
        out_specs=[IN_VMEM] * 4,
        scratch_shapes=[vmem((width, width), BF), pltpu.SemaphoreType.DMA((count,))],
        out_shape=[
            jax.ShapeDtypeStruct((rows, width), F32),
            jax.ShapeDtypeStruct((rows, width), BF),
            jax.ShapeDtypeStruct((8, width), F32),
            jax.ShapeDtypeStruct((rows, width), BF),
        ],
        compiler_params=PARAMS,
        cost_estimate=cost(2 * rows * width * width, hidden, hidden, *pieces),
    )(*grads, hidden, top, row_scale, valid, nat, *pieces)


def last_call(
    info, query_grad, kv_grad, pieces, tokens, attn, rel, mid, sums, d_bf, dp, own, n_value
):
    rows, width = tokens.shape
    block = width // dp
    wide = pieces[0].shape[1]
    count = len(pieces)

    def kernel(info, query, kv, tokens, attn, rel, mid, sums, d_bf, *refs):
        out, small, weight, back, norm, line, sems = refs[count:]
        copies = row_copies(refs[:count], weight, sems)
        for _, copy in copies:
            copy.start()
        value, inverse = normed(tokens[...].astype(F32))
        norm[...] = value
        d_query = jnp.sum(query[...].astype(F32), axis=0, keepdims=True)
        d_value = jnp.sum(kv[:, HEAD:].astype(F32), axis=0, keepdims=True)
        d = lax.broadcasted_iota(jnp.int32, (HEAD, width), 0)
        at = lax.broadcasted_iota(jnp.int32, (HEAD, width), 1)
        chosen = (at == lax.div(d, n_value) * own + lax.rem(d, n_value)).astype(F32)
        spread = jnp.dot(
            jnp.broadcast_to(d_value, (8, HEAD)),
            chosen,
            preferred_element_type=F32,
            precision=lax.Precision.HIGHEST,
        )[:1]
        line[...] = stack_rows(d_query, spread)
        for _, copy in copies:
            copy.wait()
        first = jnp.zeros((rows, 1), F32)
        second = jnp.zeros((rows, 1), F32)
        for n in range(dp):
            mine = slice(n * block, (n + 1) * block)
            grad = dot_t(query[...], weight[mine, :width]) + dot_t(
                kv[...], weight[mine, width : width + 2 * HEAD]
            )
            back[:, mine] = grad
            scaled = grad * rel[0:1, mine]
            first += jnp.sum(scaled, axis=-1, keepdims=True)
            second += jnp.sum(scaled * norm[:, columns_of(info, n, block)], axis=-1, keepdims=True)
        first = first / width
        second = second / width
        for n in range(dp):
            place = columns_of(info, n, block)
            mine = slice(n * block, (n + 1) * block)
            value = norm[:, place]
            grad = back[:, mine]
            scaled = grad * rel[0:1, mine]
            out[:, place] = (mid[:, place] + inverse * (scaled - first - value * second)).astype(BF)
            top = stack_rows(
                jnp.sum(grad * value, axis=0, keepdims=True),
                jnp.sum(grad, axis=0, keepdims=True),
            )
            small[mine, : 2 * HEAD] = t_dot(attn[:, mine], kv[...]).astype(BF)
            low = d_bf[...] if n == 0 else jnp.zeros_like(d_bf[...])
            rows_out = jnp.concatenate(
                [top, sums[:, place], line[:, place], low, jnp.zeros((HEAD - 32, block), F32)]
            )
            small[mine, 2 * HEAD :] = jnp.transpose(rows_out).astype(BF)

    return pl.pallas_call(
        kernel,
        name="last",
        in_specs=[IN_SMEM] + [IN_VMEM] * 8 + [ANYWHERE] * count,
        out_specs=[IN_VMEM] * 2,
        scratch_shapes=[
            vmem((width, wide), BF),
            vmem((rows, width), F32),
            vmem((rows, width), F32),
            vmem((8, width), F32),
            pltpu.SemaphoreType.DMA((count,)),
        ],
        out_shape=[
            jax.ShapeDtypeStruct((rows, width), BF),
            jax.ShapeDtypeStruct((width, 3 * HEAD), BF),
        ],
        compiler_params=PARAMS,
        cost_estimate=cost(2 * rows * width * wide, tokens, mid, *pieces),
    )(info, query_grad, kv_grad, tokens, attn, rel, mid, sums, d_bf, *pieces)


def start_at_first(step, tile, copies):
    @pl.when(step == 0)
    def _():
        for _, copy in copies:
            copy.start()

    for at, copy in copies:
        pl.when(step == at // tile)(copy.wait)


def grad_act_call(pieces, row_scale, weight):
    rows, width = row_scale.shape[0], weight.shape[1]
    part = weight.shape[0]
    tile = row_tile(rows)
    count = len(pieces)

    def kernel(scale, weight, *refs):
        two, out, full, sems = refs[count:]
        step = pl.program_id(0)
        start_at_first(step, tile, row_copies(refs[:count], full, sems))
        raw = full[pl.ds(pl.multiple_of(step * tile, tile), tile), :]
        low = (raw.astype(F32) * scale[...]).astype(BF)
        two[...] = low
        out[...] = dot_t(low, weight[...]).astype(BF)

    return pl.pallas_call(
        kernel,
        name="grad_act",
        grid=(rows // tile,),
        in_specs=[pl.BlockSpec((tile, 1), by_row), pl.BlockSpec((part, width), fixed)]
        + [ANYWHERE] * count,
        out_specs=[pl.BlockSpec((tile, width), by_row), pl.BlockSpec((tile, part), by_row)],
        out_shape=[
            jax.ShapeDtypeStruct((rows, width), BF),
            jax.ShapeDtypeStruct((rows, part), BF),
        ],
        scratch_shapes=[vmem((rows, width), BF), pltpu.SemaphoreType.DMA((count,))],
        compiler_params=PARAMS,
        cost_estimate=cost(2 * rows * width * part, weight, *pieces, *pieces),
    )(row_scale, weight, *pieces)


def feed_call(pieces, offset, grad_act, gathered):
    rows = grad_act.shape[0]
    tile = row_tile(rows)
    count = len(pieces)
    seq, groups, own, part = gathered.shape
    width = seq * groups * own

    def kernel(offset, back, gathered, *refs):
        whole, act, pre, total, weight, full, sems, more = refs[count:]
        step = pl.program_id(0)

        @pl.when(step == 0)
        def _():
            for copy in fetches(gathered, weight, sems):
                copy.start()
            total[...] = jnp.zeros_like(total)

        start_at_first(step, tile, row_copies(refs[:count], full, more))

        @pl.when(step == 0)
        def _():
            for copy in fetches(gathered, weight, sems):
                copy.wait()

        rows_in = full[pl.ds(pl.multiple_of(step * tile, tile), tile), :]
        whole[...] = rows_in
        for at in range(0, part, 256):
            mine = slice(at, at + 256)
            v = dot32(rows_in, weight[:, :, :, mine].reshape(width, 256)) + offset[:, mine]
            square = v * v
            t = jnp.tanh(ROOT * v * (1.0 + CUBIC * square))
            up = 0.5 + 0.5 * t
            act[:, mine] = (v * up).astype(BF)
            slope = up + (0.5 * ROOT) * v * (1.0 - t * t) * (1.0 + (3.0 * CUBIC) * square)
            grad = (back[:, mine].astype(F32) * slope).astype(BF)
            pre[:, mine] = grad
            total[:, mine] += jnp.sum(grad.astype(F32), axis=0, keepdims=True)

    return pl.pallas_call(
        kernel,
        name="feed",
        grid=(rows // tile,),
        in_specs=[pl.BlockSpec((1, part), fixed), pl.BlockSpec((tile, part), by_row), ANYWHERE]
        + [ANYWHERE] * count,
        out_specs=[
            pl.BlockSpec((tile, width), by_row),
            pl.BlockSpec((tile, part), by_row),
            pl.BlockSpec((tile, part), by_row),
            pl.BlockSpec((1, part), fixed),
        ],
        out_shape=[
            jax.ShapeDtypeStruct((rows, width), BF),
            jax.ShapeDtypeStruct((rows, part), BF),
            jax.ShapeDtypeStruct((rows, part), BF),
            jax.ShapeDtypeStruct((1, part), F32),
        ],
        scratch_shapes=[
            vmem((groups, seq, own, part), BF),
            vmem((rows, width), BF),
            pltpu.SemaphoreType.DMA((seq,)),
            pltpu.SemaphoreType.DMA((count,)),
        ],
        compiler_params=PARAMS,
        cost_estimate=cost(2 * rows * width * part, gathered, grad_act, *pieces, *pieces),
    )(offset, grad_act, gathered, *pieces)


def grad_mlp_call(value, second_half, gathered):
    rows, part = value.shape[0] // 2, value.shape[1]
    tile = row_tile(rows)
    seq, groups, own, _ = gathered.shape
    width = seq * groups * own
    skip = rows // tile if second_half else 0

    def kernel(value, gathered, out, weight, sems):
        @pl.when(pl.program_id(0) == 0)
        def _():
            copies = fetches(gathered, weight, sems)
            for copy in copies:
                copy.start()
            for copy in copies:
                copy.wait()

        out[...] = dot_t(value[...], weight[...].reshape(width, part)).astype(BF)

    return pl.pallas_call(
        kernel,
        name="grad_mlp",
        grid=(rows // tile,),
        in_specs=[pl.BlockSpec((tile, part), lambda i: (i + skip, 0)), ANYWHERE],
        out_specs=pl.BlockSpec((tile, width), by_row),
        out_shape=jax.ShapeDtypeStruct((rows, width), BF),
        scratch_shapes=[vmem((groups, seq, own, part), BF), pltpu.SemaphoreType.DMA((seq,))],
        compiler_params=PARAMS,
        cost_estimate=cost(2 * rows * width * part, value, gathered),
    )(value, gathered)


def branch_call(value, second_half, weight):
    rows, part = value.shape[0] // 2, value.shape[1]
    width = weight.shape[1]
    tile = row_tile(rows)
    skip = rows // tile if second_half else 0

    def kernel(value, weight, out):
        out[...] = dot32(value[...], weight[...]).astype(BF)

    return pl.pallas_call(
        kernel,
        name="branch",
        grid=(rows // tile,),
        in_specs=[
            pl.BlockSpec((tile, part), lambda i: (i + skip, 0)),
            pl.BlockSpec((part, width), fixed),
        ],
        out_specs=pl.BlockSpec((tile, width), by_row),
        out_shape=jax.ShapeDtypeStruct((rows, width), BF),
        compiler_params=PARAMS,
        cost_estimate=cost(2 * rows * width * part, value, weight),
    )(value, weight)


def d_rows_call(left, second_half, right, dp):
    rows, width = right.shape
    blocks = dp // 2
    size = left.shape[1] // dp
    skip = blocks if second_half else 0

    def kernel(left, right, out):
        out[...] = t_dot(left[...], right[...]).astype(BF)

    return pl.pallas_call(
        kernel,
        name="d_rows",
        grid=(blocks,),
        in_specs=[
            pl.BlockSpec((rows, size), lambda i: (0, i + skip)),
            pl.BlockSpec((rows, width), fixed),
        ],
        out_specs=pl.BlockSpec((size, width), by_row),
        out_shape=jax.ShapeDtypeStruct((size * blocks, width), BF),
        compiler_params=PARAMS,
        cost_estimate=cost(),
    )(left, right)


def d_proj_call(act, two, seq):
    rows, part = act.shape
    width = two.shape[1]
    tile = max(part // seq, HEAD)

    def kernel(act, two, out):
        out[...] = t_dot(act[...], two[...]).astype(BF)

    return pl.pallas_call(
        kernel,
        name="d_proj",
        grid=(part // tile,),
        in_specs=[pl.BlockSpec((rows, tile), by_column), pl.BlockSpec((rows, width), fixed)],
        out_specs=pl.BlockSpec((tile, width), by_row),
        out_shape=jax.ShapeDtypeStruct((part, width), BF),
        compiler_params=PARAMS,
        cost_estimate=cost(2 * rows * width * part, act, two),
    )(act, two)


def d_fc_call(mlp, grad_pre, dp, seq):
    rows, width = mlp.shape
    part = grad_pre.shape[1]
    own = width // (dp * seq)
    tile = width // dp

    def kernel(mlp, grad, out):
        out[...] = t_dot(mlp[...], grad[...]).astype(BF).reshape(seq, 1, own, part)

    return pl.pallas_call(
        kernel,
        name="d_fc",
        grid=(dp,),
        in_specs=[pl.BlockSpec((rows, tile), by_column), pl.BlockSpec((rows, part), fixed)],
        out_specs=pl.BlockSpec((seq, 1, own, part), lambda i: (0, i, 0, 0)),
        out_shape=jax.ShapeDtypeStruct((seq, dp, own, part), BF),
        compiler_params=PARAMS,
        cost_estimate=cost(2 * rows * width * part, mlp, grad_pre),
    )(mlp, grad_pre)


def local(
    dp,
    seq,
    tokens,
    lengths,
    repos,
    ln1_gain,
    ln1_bias,
    w_query,
    b_query,
    w_key,
    w_value,
    b_value,
    w_out,
    b_out,
    ln2_gain,
    ln2_bias,
    w_fc,
    b_fc,
    w_proj,
    b_proj,
    grad_out,
):
    ring = Ring(dp, seq)
    me, z = ring.me, ring.z
    windows, span, width = tokens.shape
    rows = windows * span
    own = w_query.shape[0]
    block = own * seq
    hidden = w_fc.shape[1]
    part = hidden // dp
    piece = part // seq
    scale = 1.0 / math.sqrt(HEAD)
    kv_end = width + 2 * HEAD
    pairs = dp
    all_rows = dp * rows

    size_hi = lax.div(lengths, jnp.int32(64))
    columns = [
        ln1_gain[:, None],
        ln1_bias[:, None],
        b_query[:, None],
        b_out[:, None],
        ln2_gain[:, None],
        ln2_bias[:, None],
        b_proj[:, None],
        jnp.pad(b_value, (0, own - b_value.shape[0]))[:, None],
        jnp.broadcast_to(size_hi.astype(BF), (own,))[:, None],
        jnp.broadcast_to((lengths - 64 * size_hi).astype(BF), (own,))[:, None],
        jnp.broadcast_to(repos.astype(BF), (own,))[:, None],
        jnp.transpose(b_fc.reshape(-1, own)),
    ]
    n_plain = 11
    n_fc = b_fc.shape[0] // own
    vector_block = jnp.concatenate(columns, axis=1)
    vector_block = jnp.pad(vector_block, ((0, 0), (0, HEAD - vector_block.shape[1])))
    w_qkv = jnp.concatenate([w_query, w_key, w_value, vector_block], axis=1)

    token = jnp.zeros((), F32)

    def tick(*values):
        nonlocal token
        values, token = lax.optimization_barrier((values, token))
        return values

    first_place = z * span
    info = jnp.stack([first_place] + ring.owners)
    token_rows = tokens.reshape(rows, width)
    raw = grad_out.reshape(rows, width)
    n_value = b_value.shape[0]
    raw_near = ring.cross(raw)
    qkv_z = ring.seq_gather_near(w_qkv)
    qkv_z, w_out, raw, raw_near = tick(qkv_z, w_out, raw, raw_near)

    qkv_block = ring.seq_place(qkv_z).reshape(block, -1)
    qkv_near = ring.cross(qkv_block)
    out_z = ring.seq_gather_near(w_out)
    qkv_block, qkv_near, out_z, w_proj = tick(qkv_block, qkv_near, out_z, w_proj)
    proj_all = lax.all_gather(w_proj, "seq", axis=0, tiled=True)

    qkv_far = ring.corner(qkv_block, qkv_near)
    qkv_first = ring.first(qkv_block, qkv_near)
    out_block = ring.seq_place(out_z).reshape(block, -1)
    qkv_far, out_block, qkv_first = tick(qkv_far, out_block, qkv_first)

    qkv_second = ring.second(qkv_far)
    out_near = ring.cross(out_block)
    qkv_second, qkv_first = tick(qkv_second, qkv_first)
    qkv_all = ring.pieces(qkv_first, qkv_second)
    attn_in, query_low, kv_low, rel, nat = enter_call(info, token_rows, qkv_all, dp, own, n_value)
    kv_low, attn_in, query_low, rel, w_fc = tick(kv_low, attn_in, query_low, rel, w_fc)
    kv_z = ring.seq_gather_near(kv_low)
    fc_turned = lax.all_to_all(
        w_fc.reshape(own, dp, part), "dp", split_axis=1, concat_axis=0, tiled=False
    )

    all_lengths = (rel[8] * 64.0 + rel[9]).reshape(dp, block)[:, :1]
    all_repos = rel[10].reshape(dp, block)[:, :1]
    same = (all_repos == all_repos.reshape(1, dp)).astype(F32)
    weights = jnp.sum(all_lengths) / (
        REPOS * jnp.sum(same * all_lengths.reshape(1, dp), axis=1, keepdims=True)
    )
    places = (first_place + jnp.arange(span, dtype=jnp.int32)).astype(F32)
    all_valid = (places[None, :] < all_lengths).astype(F32)
    row_scale = (all_valid * weights).reshape(all_rows, 1)
    valid_rows = all_valid[0].reshape(rows, 1)
    bf_own = jnp.transpose(
        rel[n_plain : n_plain + n_fc, :block].reshape(n_fc, seq, own), (1, 0, 2)
    ).reshape(1, part)
    own_scale = row_scale[:rows]
    kv_z, raw, out_block, out_near, row_scale, own_scale, bf_own, fc_turned = tick(
        kv_z, raw, out_block, out_near, row_scale, own_scale, bf_own, fc_turned
    )
    fc_all = lax.all_gather(fc_turned.reshape(dp, own, part), "seq", axis=0, tiled=False)

    out_far = ring.corner(out_block, out_near)
    out_first = ring.first(out_block, out_near)
    kv_all = ring.seq_place(kv_z).reshape(seq * span, 2 * HEAD)
    key_all, value_all = kv_all[:, :HEAD], kv_all[:, HEAD:]
    attn_low, log_total = attend(
        info, query_low, key_all, jnp.transpose(value_all), valid_rows, pairs, scale
    )
    attn_low, raw, out_far, out_first = tick(attn_low, raw, out_far, out_first)
    out_second = ring.second(out_far)
    out_second, attn_low = tick(out_second, attn_low)
    raw_far = ring.corner(raw, raw_near)
    raw_first = ring.first(raw, raw_near)
    out_all = ring.pieces(out_first, out_second)
    hidden_one, mlp_own = leave_call(attn_low, out_all, token_rows, nat)
    mlp_own, raw_far, raw_first = tick(mlp_own, raw_far, raw_first)

    mlp_near = ring.cross(mlp_own)
    raw_second = ring.second(raw_far)
    raw_second, proj_all = tick(raw_second, proj_all)
    two_all, grad_act = grad_act_call(ring.pieces(raw_first, raw_second), row_scale, proj_all)
    mlp_own, two_all, grad_act, mlp_near = tick(mlp_own, two_all, grad_act, mlp_near)
    mlp_far = ring.corner(mlp_own, mlp_near)
    mlp_first = ring.first(mlp_own, mlp_near)
    mlp_far, mlp_first, fc_all = tick(mlp_far, mlp_first, fc_all)
    mlp_second = ring.second(mlp_far)
    mlp_second, fc_all = tick(mlp_second, fc_all)
    mlp_all, act_low, grad_pre, d_b_fc = feed_call(
        ring.pieces(mlp_first, mlp_second), bf_own, grad_act, fc_all
    )
    odd = grad_mlp_call(grad_pre, True, fc_all)
    odd, grad_pre = tick(odd, grad_pre)
    other = ring.other(odd)
    even = grad_mlp_call(grad_pre, False, fc_all)
    even, other = tick(even, other)
    corner = ring.corner_sums(even, other)
    corner, act_low = tick(corner, act_low)
    far = ring.send_corner(corner)
    branch_odd = branch_call(act_low, True, proj_all)
    far, branch_odd, act_low, grad_pre = tick(far, branch_odd, act_low, grad_pre)
    cross = ring.cross_sums(even, other, far)
    cross, act_low, grad_pre, branch_odd = tick(cross, act_low, grad_pre, branch_odd)
    near = ring.send_cross(cross)
    branch_other = ring.other(branch_odd)
    branch_even = branch_call(act_low, False, proj_all)
    d_fc = d_fc_call(mlp_all, grad_pre, dp, seq)
    near, branch_even, branch_other, d_fc = tick(near, branch_even, branch_other, d_fc)
    fc_share = lax.psum_scatter(d_fc, "seq", scatter_dimension=0, tiled=False)
    corner = ring.corner_sums(branch_even, branch_other)
    corner, near = tick(corner, near)

    branch_far = ring.send_corner(corner)
    d_bf = jnp.transpose(d_b_fc.reshape(seq, n_fc, own), (1, 0, 2)).reshape(n_fc, block)
    d_bf = jnp.pad(d_bf, ((0, 8 - n_fc), (0, 0)))
    grad_mid, grad_one, sums, grad_att = middle_call(
        ring.ends(even, other, near), hidden_one, raw, own_scale, valid_rows, nat, out_all
    )
    grad_att, grad_one, branch_far = tick(grad_att, grad_one, branch_far)
    cross = ring.cross_sums(branch_even, branch_other, branch_far)
    cross, grad_att = tick(cross, grad_att)
    branch_near = ring.send_cross(cross)
    query_grad, key_grad, value_grad = attend_back(
        info, query_low, grad_att, log_total, key_all, jnp.transpose(key_all), value_all, pairs, scale
    )
    d_q_odd = d_rows_call(attn_in, True, query_grad, dp)
    kv_grads = jnp.concatenate([key_grad, value_grad], axis=1).reshape(seq, rows, 2 * HEAD)
    kv_mine = lax.dynamic_slice_in_dim(kv_grads, z, 1, 0)[0]
    kv_sends = [
        lax.dynamic_slice_in_dim(kv_grads, lax.rem(z + step, seq), 1, 0)[0].astype(BF)
        for step in range(1, seq)
    ]
    query_grad, kv_mine, kv_sends, grad_one, d_q_odd, branch_near = tick(
        query_grad, kv_mine, kv_sends, grad_one, d_q_odd, branch_near
    )
    d_q_other = ring.other(d_q_odd)
    kv_parts = [ring.up(part, step + 1) for step, part in enumerate(kv_sends)]
    d_q_even = d_rows_call(attn_in, False, query_grad, dp)
    d_out_odd = d_rows_call(attn_low, True, grad_one, dp)
    d_q_other, d_q_even, d_out_odd, grad_one = tick(d_q_other, d_q_even, d_out_odd, grad_one)
    corner = ring.corner_sums(d_q_even, d_q_other)
    corner, act_low = tick(corner, act_low)
    q_far = ring.send_corner(corner)
    d_proj = d_proj_call(act_low, two_all, seq)
    q_far, d_proj, kv_parts, d_out_odd, grad_one, fc_share = tick(
        q_far, d_proj, kv_parts, d_out_odd, grad_one, fc_share
    )
    proj_share = lax.psum_scatter(d_proj, "seq", scatter_dimension=0, tiled=True)
    cross = ring.cross_sums(d_q_even, d_q_other, q_far)
    kv_grad = (kv_mine + sum(part.astype(F32) for part in kv_parts)).astype(BF)
    cross, kv_grad, d_out_odd, grad_one = tick(cross, kv_grad, d_out_odd, grad_one)
    q_near = ring.send_cross(cross)
    d_out_other = ring.other(d_out_odd)
    d_out_even = d_rows_call(attn_low, False, grad_one, dp)
    grad_rows, small = last_call(
        info,
        query_grad,
        kv_grad,
        qkv_all,
        token_rows,
        attn_in,
        rel,
        grad_mid,
        sums,
        d_bf,
        dp,
        own,
        n_value,
    )
    grad_tokens = grad_rows.reshape(windows, span, width)
    cut = width // 2
    out_corner = ring.corner_sums(d_out_even, d_out_other)
    small_odd = small[cut:]
    q_near, small, small_odd, out_corner = tick(q_near, small, small_odd, out_corner)
    out_far_back = ring.send_corner(out_corner)
    small_other = ring.other(small_odd)
    q_share = ring.scatter_end(d_q_even, d_q_other, q_near)
    branch_two = ring.scatter_end(branch_even, branch_other, branch_near)
    output = (hidden_one + branch_two + nat[6:7]).astype(BF).reshape(windows, span, width)
    out_far_back, q_share, small_other, output = tick(out_far_back, q_share, small_other, output)
    small_corner = ring.corner_sums(small[:cut], small_other)
    cross = ring.cross_sums(d_out_even, d_out_other, out_far_back)
    cross, small_corner, q_share = tick(cross, small_corner, q_share)
    small_far = ring.send_corner(small_corner)
    small_far, proj_share = tick(small_far, proj_share)
    out_near_back = ring.send_cross(cross)
    small_cross = ring.cross_sums(small[:cut], small_other, small_far)
    small_near = ring.send_cross(small_cross)
    d_w_query = ring.seq_scatter_near(
        lambda owner: lax.dynamic_slice_in_dim(q_share, owner * own, own, 0)
    )
    out_near_back, small_near, d_w_query, fc_share = tick(
        out_near_back, small_near, d_w_query, fc_share
    )
    out_share = ring.scatter_end(d_out_even, d_out_other, out_near_back)
    d_w_out = ring.seq_scatter_near(
        lambda owner: lax.dynamic_slice_in_dim(out_share, owner * own, own, 0)
    )
    small_share = ring.scatter_end(small[:cut], small_other, small_near)
    d_small = ring.seq_scatter_near(
        lambda owner: lax.dynamic_slice_in_dim(small_share, owner * own, own, 0)
    )
    d_w_proj = proj_share.astype(F32)
    d_w_fc = (
        lax.all_to_all(fc_share, "dp", split_axis=0, concat_axis=1, tiled=False)
        .reshape(own, hidden)
        .astype(F32)
    )
    vectors = jnp.transpose(d_small[:, 2 * HEAD :])
    return (
        output,
        grad_tokens,
        vectors[0],
        vectors[1],
        d_w_query,
        vectors[16],
        d_small[:, :HEAD],
        d_small[:, HEAD : 2 * HEAD],
        vectors[17, : b_value.shape[0]],
        d_w_out,
        vectors[8],
        vectors[9],
        vectors[10],
        d_w_fc,
        vectors[24 : 24 + n_fc].reshape(-1),
        d_w_proj,
        vectors[11],
    )


def solution(mesh):
    dp, seq = mesh.shape["dp"], mesh.shape["seq"]
    both = P(("dp", "seq"))
    rows = P(("dp", "seq"), None)
    token = P("dp", "seq", None)

    def run(*args):
        return local(dp, seq, *args)

    return jax.shard_map(
        run,
        mesh=mesh,
        in_specs=(
            token,
            P("dp"),
            P("dp"),
            both,
            both,
            rows,
            both,
            rows,
            rows,
            both,
            rows,
            both,
            both,
            both,
            rows,
            both,
            rows,
            both,
            token,
        ),
        out_specs=(
            token,
            token,
            both,
            both,
            rows,
            both,
            rows,
            rows,
            both,
            rows,
            both,
            both,
            both,
            rows,
            both,
            rows,
            both,
        ),
        check_vma=False,
    )
```

```python
import math

import jax
import jax.numpy as jnp
from jax import lax
from jax.experimental import pallas as pl
from jax.experimental.pallas import tpu as pltpu
from jax.sharding import PartitionSpec as P

HEADS = 16
HEAD = 128
REPOS = 4
BF = jnp.bfloat16
F32 = jnp.float32

norm_epsilon = 1e-05


def normed(values):
    centre = jnp.mean(values, axis=-1, keepdims=True)
    shifted = values - centre
    inverse = lax.rsqrt(jnp.mean(shifted * shifted, axis=-1, keepdims=True) + norm_epsilon)
    return shifted * inverse, inverse


def dot32(left, right):
    return jnp.dot(left, right, preferred_element_type=F32)


def dot_t(left, right):
    return lax.dot_general(left, right, (((1,), (1,)), ((), ())), preferred_element_type=F32)


def t_dot(left, right):
    return lax.dot_general(left, right, (((0,), (0,)), ((), ())), preferred_element_type=F32)


class Ring:
    def __init__(self, dp, seq):
        self.nd, self.ns = dp, seq
        self.me = lax.axis_index("dp")
        self.z = lax.axis_index("seq")
        self.order = list(range(0, dp, 2)) + list(range(1, dp, 2))
        self.owners = [self.me ^ k for k in self.order]

    def swap(self, value, mask):
        return lax.ppermute(value, "dp", [(i, i ^ mask) for i in range(self.nd)])

    def up(self, value, by=1):
        return lax.ppermute(value, "seq", [(i, (i + by) % self.ns) for i in range(self.ns)])

    def back(self, step):
        return lax.rem(self.z - step + self.ns, self.ns)

    def seq_gather_near(self, block):
        return [block] + [self.up(block, step) for step in range(1, self.ns)]

    def seq_place(self, pieces, axis=0):
        shape = pieces[0].shape
        full = jnp.zeros(shape[:axis] + (self.ns,) + shape[axis:], pieces[0].dtype)
        for step, piece in enumerate(pieces):
            full = lax.dynamic_update_slice_in_dim(
                full, jnp.expand_dims(piece, axis), self.back(step), axis
            )
        return full

    def seq_cut(self, share, rows):
        mine = lax.dynamic_slice_in_dim(share, self.z * rows, rows, 0)
        sends = [
            lax.dynamic_slice_in_dim(
                share, lax.rem(self.z + step, self.ns) * rows, rows, 0
            ).astype(BF)
            for step in range(1, self.ns)
        ]
        return mine, sends

    def seq_sum(self, mine, sends):
        for step, part in enumerate(sends):
            mine = mine + self.up(part, step + 1).astype(F32)
        return mine

    def cross(self, block):
        if self.nd == 8:
            return self.swap(block, 2), self.swap(block, 4)
        return ()

    def first(self, block, near):
        if self.nd == 8:
            three = (block,) + tuple(near)
            return three + tuple(self.swap(piece, 1) for piece in three)
        return ()

    def corner(self, block, near):
        if self.nd == 8:
            half = block.shape[0] // 2
            return self.swap(near[0][:half], 4), self.swap(near[1][half:], 2)
        pieces = {0: block}
        bit = 2
        while bit < self.nd:
            for k in list(pieces):
                pieces[k | bit] = self.swap(pieces[k], bit)
            bit *= 2
        return tuple(pieces[k] for k in range(0, self.nd, 2))

    def second(self, far):
        far = jnp.concatenate(far, axis=0)
        return far, self.swap(far, 1)

    def pieces(self, first, second):
        if self.nd == 8:
            return first[:3] + second[:1] + first[3:] + second[1:]
        return second

    def other(self, value):
        if isinstance(value, (list, tuple)):
            return [self.swap(part, 1) for part in value]
        return self.swap(value, 1)

    def part(self, value, at):
        arrays = value if isinstance(value, (list, tuple)) else [value]
        rows = sum(a.shape[0] for a in arrays) * 2 // self.nd
        start = at * rows
        for array in arrays:
            if start < array.shape[0]:
                return array[start : start + rows]
            start -= array.shape[0]

    def corner_sums(self, even, other):
        if self.nd != 8:
            return ()
        held = self.part(even, 3).astype(F32) + self.part(other, 3).astype(F32)
        half = held.shape[0] // 2
        return held[:half].astype(BF), held[half:].astype(BF)

    def send_corner(self, sums):
        if self.nd != 8:
            return ()
        return self.swap(sums[0], 4), self.swap(sums[1], 2)

    def cross_sums(self, even, other, far):
        if self.nd == 8:
            low, high = far
            half = low.shape[0]

            def held(at, first):
                rows = slice(first, first + half)
                return self.part(even, at)[rows].astype(F32) + self.part(other, at)[rows].astype(F32)

            to_x = jnp.concatenate(
                [(held(1, 0) + low.astype(F32)).astype(BF), held(1, half).astype(BF)], axis=0
            )
            to_y = jnp.concatenate(
                [held(2, 0).astype(BF), (held(2, half) + high.astype(F32)).astype(BF)], axis=0
            )
            return to_x, to_y
        held = [
            self.part(even, at).astype(F32) + self.part(other, at).astype(F32)
            for at in range(self.nd // 2)
        ]
        while len(held) > 2:
            cut = len(held) // 2
            held = [
                a + self.swap(b.astype(BF), len(held)).astype(F32)
                for a, b in zip(held[:cut], held[cut:])
            ]
        return held[0].astype(BF), held[1].astype(BF)

    def send_cross(self, sums):
        if self.nd == 8:
            return self.swap(sums[0], 2), self.swap(sums[1], 4)
        return sums[0], self.swap(sums[1], 2)

    def ends(self, even, other, near):
        if self.nd == 8:
            return even, other, near[0], near[1]
        nothing = jnp.zeros_like(near[0])
        return near[0], near[1], nothing, nothing

    def scatter_end(self, even, other, near):
        if self.nd == 8:
            parts = (self.part(even, 0), self.part(other, 0)) + tuple(near)
        else:
            parts = near
        return sum(part.astype(F32) for part in parts)


LOG2E = 1.4426950408889634


def attend_kernel(info, query, key, value_t, valid, out, log_total, *, heads, scale):
    keys = key.shape[0]
    rows = query.shape[0]
    place = lax.broadcasted_iota(jnp.int32, (keys, rows), 1) + info[0]
    allowed = lax.broadcasted_iota(jnp.int32, (keys, rows), 0) <= place
    for h in range(heads):
        cols = slice(h * HEAD, (h + 1) * HEAD)
        scores = dot_t(key[...], query[:, cols]) * (scale * LOG2E)
        scores = jnp.where(allowed, scores, -1e30)
        top = jnp.max(scores, axis=0, keepdims=True)
        expo = jnp.exp2(scores - top)
        total = jnp.sum(expo, axis=0, keepdims=True)
        mixed = dot32(value_t[...], expo.astype(BF)) * (1.0 / total)
        out[:, cols] = (jnp.transpose(mixed) * valid[...]).astype(BF)
        log_total[h] = top + jnp.log2(total)


def attend(info, query, key, value_t, valid, pairs, scale):
    rows, width = query.shape
    keys = key.shape[0]
    heads = HEADS // pairs
    step = heads * HEAD
    whole = lambda k, info: (0, 0)
    return pl.pallas_call(
        lambda *refs: attend_kernel(*refs, heads=heads, scale=scale),
        grid_spec=pltpu.PrefetchScalarGridSpec(
            num_scalar_prefetch=1,
            grid=(pairs,),
            in_specs=[
                pl.BlockSpec((rows, step), lambda k, info: (0, info[1 + k])),
                pl.BlockSpec((keys, HEAD), whole),
                pl.BlockSpec((HEAD, keys), whole),
                pl.BlockSpec((rows, 1), whole),
            ],
            out_specs=[
                pl.BlockSpec((rows, step), lambda k, info: (0, k)),
                pl.BlockSpec((heads, 1, rows), lambda k, info: (k, 0, 0)),
            ],
        ),
        out_shape=[
            jax.ShapeDtypeStruct((rows, width), BF),
            jax.ShapeDtypeStruct((HEADS, 1, rows), F32),
        ],
        compiler_params=pltpu.CompilerParams(vmem_limit_bytes=48 * 1024 * 1024),
        cost_estimate=cost(),
    )(info, query, key, value_t, valid)


def attend_back_kernel(
    info, query, grad, log_total, key, key_t, value, out, key_grad, value_grad, *, heads, scale
):
    keys = key.shape[0]
    rows = query.shape[0]
    place = lax.broadcasted_iota(jnp.int32, (keys, rows), 1) + info[0]
    allowed = lax.broadcasted_iota(jnp.int32, (keys, rows), 0) <= place

    @pl.when(pl.program_id(0) == 0)
    def _():
        key_grad[...] = jnp.zeros_like(key_grad)
        value_grad[...] = jnp.zeros_like(value_grad)

    for h in range(heads):
        cols = slice(h * HEAD, (h + 1) * HEAD)
        scores = dot_t(key[...], query[:, cols]) * (scale * LOG2E)
        scores = jnp.where(allowed, scores, -1e30)
        probs = jnp.exp2(scores - log_total[h])
        dprobs = dot_t(value[...], grad[:, cols])
        delta = jnp.sum(probs * dprobs, axis=0, keepdims=True)
        dscores = (probs * (dprobs - delta)).astype(BF)
        value_grad[...] += dot32(probs.astype(BF), grad[:, cols])
        key_grad[...] += dot32(dscores, query[:, cols]) * scale
        back = dot32(key_t[...], dscores) * scale
        out[:, cols] = jnp.transpose(back).astype(BF)


def attend_back(info, query, grad, log_total, key, key_t, value, pairs, scale):
    rows, width = query.shape
    keys = key.shape[0]
    heads = HEADS // pairs
    step = heads * HEAD
    whole = lambda k, info: (0, 0)
    natural = lambda k, info: (0, info[1 + k])
    return pl.pallas_call(
        lambda *refs: attend_back_kernel(*refs, heads=heads, scale=scale),
        grid_spec=pltpu.PrefetchScalarGridSpec(
            num_scalar_prefetch=1,
            grid=(pairs,),
            in_specs=[
                pl.BlockSpec((rows, step), natural),
                pl.BlockSpec((rows, step), lambda k, info: (0, k)),
                pl.BlockSpec((heads, 1, rows), lambda k, info: (k, 0, 0)),
                pl.BlockSpec((keys, HEAD), whole),
                pl.BlockSpec((HEAD, keys), whole),
                pl.BlockSpec((keys, HEAD), whole),
            ],
            out_specs=[
                pl.BlockSpec((rows, step), natural),
                pl.BlockSpec((keys, HEAD), whole),
                pl.BlockSpec((keys, HEAD), whole),
            ],
        ),
        out_shape=[
            jax.ShapeDtypeStruct((rows, width), BF),
            jax.ShapeDtypeStruct((keys, HEAD), F32),
            jax.ShapeDtypeStruct((keys, HEAD), F32),
        ],
        compiler_params=pltpu.CompilerParams(vmem_limit_bytes=48 * 1024 * 1024),
        cost_estimate=cost(),
    )(info, query, grad, log_total, key, key_t, value)


def fetches(gathered, weight, sems):
    return [
        pltpu.make_async_copy(gathered.at[n], weight.at[:, n], sems.at[n])
        for n in range(gathered.shape[0])
    ]


def row_copies(pieces, full, sems):
    copies = []
    at = 0
    for n, piece in enumerate(pieces):
        size = piece.shape[0]
        copies.append((at, pltpu.make_async_copy(piece, full.at[pl.ds(at, size)], sems.at[n])))
        at += size
    return copies


ROOT = math.sqrt(2.0 / math.pi)
CUBIC = 0.044715


def row_tile(rows):
    return math.gcd(rows, 512)


def by_row(i, *_):
    return (i, 0)


def by_column(i, *_):
    return (0, i)


def fixed(i, *_):
    return (0, 0)


IN_VMEM = pl.BlockSpec(memory_space=pltpu.VMEM)
IN_SMEM = pl.BlockSpec(memory_space=pltpu.SMEM)
ANYWHERE = pl.BlockSpec(memory_space=pl.ANY)


PARAMS = pltpu.CompilerParams(vmem_limit_bytes=54 * 1024 * 1024)


def cost(*_):
    return pl.CostEstimate(flops=1024, bytes_accessed=1024, transcendentals=0)


def columns_of(info, n, size):
    return pl.ds(pl.multiple_of(info[1 + n] * size, HEAD), size)


N_VECTORS = 16


def stack_rows(*lines):
    width = lines[0].shape[1]
    at = lax.broadcasted_iota(jnp.int32, (8, width), 0)
    rows = jnp.zeros((8, width), F32)
    for n, line in enumerate(lines):
        rows = jnp.where(at == n, line, rows)
    return rows


def vmem(shape, dtype):
    return pltpu.VMEM(shape, dtype)


def enter_call(info, tokens, pieces, dp, own, n_value):
    rows, width = tokens.shape
    block = width // dp
    wide = pieces[0].shape[1]
    kv_end = wide - HEAD
    count = len(pieces)

    def kernel(info, tokens, *refs):
        attn, query, kv, rel, nat, weight, sems = refs[count:]
        copies = row_copies(refs[:count], weight, sems)
        for _, copy in copies:
            copy.start()
        x = tokens[...].astype(F32)
        centre = jnp.mean(x, axis=-1, keepdims=True)
        x = x - centre
        inverse = lax.rsqrt(jnp.mean(x * x, axis=-1, keepdims=True) + norm_epsilon)
        for _, copy in copies:
            copy.wait()
        for n in range(dp):
            mine = slice(n * block, (n + 1) * block)
            place = columns_of(info, n, block)
            vectors = jnp.transpose(weight[mine, kv_end:].astype(F32))[:N_VECTORS]
            rel[:, mine] = vectors
            nat[:, place] = vectors
            x = tokens[:, place].astype(F32)
            attn[:, mine] = ((x - centre) * inverse * vectors[0:1] + vectors[1:2]).astype(BF)
        at = lax.broadcasted_iota(jnp.int32, (width, HEAD), 0)
        d = lax.broadcasted_iota(jnp.int32, (width, HEAD), 1)
        chosen = (at == lax.div(d, n_value) * own + lax.rem(d, n_value)).astype(BF)
        offset = dot32(nat[...].astype(BF), chosen)[7:8]
        both = dot32(attn[...], weight[:, width:kv_end])
        kv[:, :HEAD] = both[:, :HEAD].astype(BF)
        kv[:, HEAD:] = (both[:, HEAD:] + offset).astype(BF)
        for at in range(0, width, 512):
            mine = slice(at, at + 512)
            query[:, mine] = (dot32(attn[...], weight[:, mine]) + nat[2:3, mine]).astype(BF)

    return pl.pallas_call(
        kernel,
        name="enter",
        in_specs=[IN_SMEM, IN_VMEM] + [ANYWHERE] * count,
        out_specs=[IN_VMEM] * 5,
        scratch_shapes=[vmem((width, wide), BF), pltpu.SemaphoreType.DMA((count,))],
        out_shape=[
            jax.ShapeDtypeStruct((rows, width), BF),
            jax.ShapeDtypeStruct((rows, width), BF),
            jax.ShapeDtypeStruct((rows, 2 * HEAD), BF),
            jax.ShapeDtypeStruct((N_VECTORS, width), F32),
            jax.ShapeDtypeStruct((N_VECTORS, width), F32),
        ],
        compiler_params=PARAMS,
        cost_estimate=cost(2 * rows * width * kv_end, tokens, *pieces),
    )(info, tokens, *pieces)


def leave_call(attn, pieces, tokens, nat):
    rows, width = tokens.shape
    count = len(pieces)

    def kernel(attn, tokens, nat, *refs):
        hidden, mlp, weight, sems = refs[count:]
        copies = row_copies(refs[:count], weight, sems)
        for _, copy in copies:
            copy.start()
        for _, copy in copies:
            copy.wait()
        for at in range(0, width, 512):
            mine = slice(at, at + 512)
            hidden[:, mine] = (
                dot32(attn[...], weight[:, mine]) + tokens[:, mine].astype(F32) + nat[3:4, mine]
            )
        mlp[...] = (normed(hidden[...])[0] * nat[4:5] + nat[5:6]).astype(BF)

    return pl.pallas_call(
        kernel,
        name="leave",
        in_specs=[IN_VMEM] * 3 + [ANYWHERE] * count,
        out_specs=[IN_VMEM] * 2,
        scratch_shapes=[vmem((width, width), BF), pltpu.SemaphoreType.DMA((count,))],
        out_shape=[
            jax.ShapeDtypeStruct((rows, width), F32),
            jax.ShapeDtypeStruct((rows, width), BF),
        ],
        compiler_params=PARAMS,
        cost_estimate=cost(2 * rows * width * width, tokens, *pieces),
    )(attn, tokens, nat, *pieces)


def middle_call(grads, hidden, top, row_scale, valid, nat, pieces):
    rows, width = hidden.shape
    count = len(pieces)

    def kernel(g0, g1, g2, g3, hidden, top, scale, valid, nat, *refs):
        mid, one, sums, att, weight, sems = refs[count:]
        copies = row_copies(refs[:count], weight, sems)
        for _, copy in copies:
            copy.start()
        grad = (
            g0[...].astype(F32) + g1[...].astype(F32) + g2[...].astype(F32) + g3[...].astype(F32)
        )
        norm, inverse = normed(hidden[...])
        scaled = grad * nat[4:5]
        first = jnp.mean(scaled, axis=-1, keepdims=True)
        second = jnp.mean(scaled * norm, axis=-1, keepdims=True)
        grad_top = top[...].astype(F32) * scale[...]
        total = grad_top + inverse * (scaled - first - norm * second)
        mid[...] = total
        low = total.astype(BF)
        one[...] = low
        sums[...] = stack_rows(
            jnp.sum(low.astype(F32), axis=0, keepdims=True),
            jnp.sum(grad * norm, axis=0, keepdims=True),
            jnp.sum(grad, axis=0, keepdims=True),
            jnp.sum(grad_top.astype(BF).astype(F32), axis=0, keepdims=True),
        )
        for _, copy in copies:
            copy.wait()
        for at in range(0, width, 512):
            mine = slice(at, at + 512)
            att[:, mine] = (dot_t(one[...], weight[mine, :]) * valid[...]).astype(BF)

    return pl.pallas_call(
        kernel,
        name="middle",
        grid=(1,),
        in_specs=[pl.BlockSpec((rows, width), fixed)] * 4
        + [IN_VMEM] * 5
        + [ANYWHERE] * count,
        out_specs=[IN_VMEM] * 4,
        scratch_shapes=[vmem((width, width), BF), pltpu.SemaphoreType.DMA((count,))],
        out_shape=[
            jax.ShapeDtypeStruct((rows, width), F32),
            jax.ShapeDtypeStruct((rows, width), BF),
            jax.ShapeDtypeStruct((8, width), F32),
            jax.ShapeDtypeStruct((rows, width), BF),
        ],
        compiler_params=PARAMS,
        cost_estimate=cost(2 * rows * width * width, hidden, hidden, *pieces),
    )(*grads, hidden, top, row_scale, valid, nat, *pieces)


def last_call(
    info, query_grad, kv_grad, pieces, tokens, attn, rel, mid, sums, d_bf, dp, own, n_value
):
    rows, width = tokens.shape
    block = width // dp
    wide = pieces[0].shape[1]
    count = len(pieces)

    def kernel(info, query, kv, tokens, attn, rel, mid, sums, d_bf, *refs):
        out, small, weight, back, norm, line, sems = refs[count:]
        copies = row_copies(refs[:count], weight, sems)
        for _, copy in copies:
            copy.start()
        value, inverse = normed(tokens[...].astype(F32))
        norm[...] = value
        d_query = jnp.sum(query[...].astype(F32), axis=0, keepdims=True)
        d_value = jnp.sum(kv[:, HEAD:].astype(F32), axis=0, keepdims=True)
        d = lax.broadcasted_iota(jnp.int32, (HEAD, width), 0)
        at = lax.broadcasted_iota(jnp.int32, (HEAD, width), 1)
        chosen = (at == lax.div(d, n_value) * own + lax.rem(d, n_value)).astype(F32)
        spread = jnp.dot(
            jnp.broadcast_to(d_value, (8, HEAD)),
            chosen,
            preferred_element_type=F32,
            precision=lax.Precision.HIGHEST,
        )[:1]
        line[...] = stack_rows(d_query, spread)
        for _, copy in copies:
            copy.wait()
        first = jnp.zeros((rows, 1), F32)
        second = jnp.zeros((rows, 1), F32)
        for n in range(dp):
            mine = slice(n * block, (n + 1) * block)
            grad = dot_t(query[...], weight[mine, :width]) + dot_t(
                kv[...], weight[mine, width : width + 2 * HEAD]
            )
            back[:, mine] = grad
            scaled = grad * rel[0:1, mine]
            first += jnp.sum(scaled, axis=-1, keepdims=True)
            second += jnp.sum(scaled * norm[:, columns_of(info, n, block)], axis=-1, keepdims=True)
        first = first / width
        second = second / width
        for n in range(dp):
            place = columns_of(info, n, block)
            mine = slice(n * block, (n + 1) * block)
            value = norm[:, place]
            grad = back[:, mine]
            scaled = grad * rel[0:1, mine]
            out[:, place] = (mid[:, place] + inverse * (scaled - first - value * second)).astype(BF)
            top = stack_rows(
                jnp.sum(grad * value, axis=0, keepdims=True),
                jnp.sum(grad, axis=0, keepdims=True),
            )
            small[mine, : 2 * HEAD] = t_dot(attn[:, mine], kv[...]).astype(BF)
            low = d_bf[...] if n == 0 else jnp.zeros_like(d_bf[...])
            rows_out = jnp.concatenate(
                [top, sums[:, place], line[:, place], low, jnp.zeros((HEAD - 32, block), F32)]
            )
            small[mine, 2 * HEAD :] = jnp.transpose(rows_out).astype(BF)

    return pl.pallas_call(
        kernel,
        name="last",
        in_specs=[IN_SMEM] + [IN_VMEM] * 8 + [ANYWHERE] * count,
        out_specs=[IN_VMEM] * 2,
        scratch_shapes=[
            vmem((width, wide), BF),
            vmem((rows, width), F32),
            vmem((rows, width), F32),
            vmem((8, width), F32),
            pltpu.SemaphoreType.DMA((count,)),
        ],
        out_shape=[
            jax.ShapeDtypeStruct((rows, width), BF),
            jax.ShapeDtypeStruct((width, 3 * HEAD), BF),
        ],
        compiler_params=PARAMS,
        cost_estimate=cost(2 * rows * width * wide, tokens, mid, *pieces),
    )(info, query_grad, kv_grad, tokens, attn, rel, mid, sums, d_bf, *pieces)


def start_at_first(step, tile, copies):
    @pl.when(step == 0)
    def _():
        for _, copy in copies:
            copy.start()

    for at, copy in copies:
        pl.when(step == at // tile)(copy.wait)


def grad_act_call(pieces, row_scale, weight):
    rows, width = row_scale.shape[0], weight.shape[1]
    part = weight.shape[0]
    tile = row_tile(rows)
    count = len(pieces)

    def kernel(scale, weight, *refs):
        two, out, full, sems = refs[count:]
        step = pl.program_id(0)
        start_at_first(step, tile, row_copies(refs[:count], full, sems))
        raw = full[pl.ds(pl.multiple_of(step * tile, tile), tile), :]
        low = (raw.astype(F32) * scale[...]).astype(BF)
        two[...] = low
        out[...] = dot_t(low, weight[...]).astype(BF)

    return pl.pallas_call(
        kernel,
        name="grad_act",
        grid=(rows // tile,),
        in_specs=[pl.BlockSpec((tile, 1), by_row), pl.BlockSpec((part, width), fixed)]
        + [ANYWHERE] * count,
        out_specs=[pl.BlockSpec((tile, width), by_row), pl.BlockSpec((tile, part), by_row)],
        out_shape=[
            jax.ShapeDtypeStruct((rows, width), BF),
            jax.ShapeDtypeStruct((rows, part), BF),
        ],
        scratch_shapes=[vmem((rows, width), BF), pltpu.SemaphoreType.DMA((count,))],
        compiler_params=PARAMS,
        cost_estimate=cost(2 * rows * width * part, weight, *pieces, *pieces),
    )(row_scale, weight, *pieces)


def feed_call(pieces, offset, grad_act, gathered):
    rows = grad_act.shape[0]
    tile = row_tile(rows)
    count = len(pieces)
    seq, groups, own, part = gathered.shape
    width = seq * groups * own

    def kernel(offset, back, gathered, *refs):
        whole, act, pre, total, weight, full, sems, more = refs[count:]
        step = pl.program_id(0)

        @pl.when(step == 0)
        def _():
            for copy in fetches(gathered, weight, sems):
                copy.start()
            total[...] = jnp.zeros_like(total)

        start_at_first(step, tile, row_copies(refs[:count], full, more))

        @pl.when(step == 0)
        def _():
            for copy in fetches(gathered, weight, sems):
                copy.wait()

        rows_in = full[pl.ds(pl.multiple_of(step * tile, tile), tile), :]
        whole[...] = rows_in
        for at in range(0, part, 256):
            mine = slice(at, at + 256)
            v = dot32(rows_in, weight[:, :, :, mine].reshape(width, 256)) + offset[:, mine]
            square = v * v
            t = jnp.tanh(ROOT * v * (1.0 + CUBIC * square))
            up = 0.5 + 0.5 * t
            act[:, mine] = (v * up).astype(BF)
            slope = up + (0.5 * ROOT) * v * (1.0 - t * t) * (1.0 + (3.0 * CUBIC) * square)
            grad = (back[:, mine].astype(F32) * slope).astype(BF)
            pre[:, mine] = grad
            total[:, mine] += jnp.sum(grad.astype(F32), axis=0, keepdims=True)

    return pl.pallas_call(
        kernel,
        name="feed",
        grid=(rows // tile,),
        in_specs=[pl.BlockSpec((1, part), fixed), pl.BlockSpec((tile, part), by_row), ANYWHERE]
        + [ANYWHERE] * count,
        out_specs=[
            pl.BlockSpec((tile, width), by_row),
            pl.BlockSpec((tile, part), by_row),
            pl.BlockSpec((tile, part), by_row),
            pl.BlockSpec((1, part), fixed),
        ],
        out_shape=[
            jax.ShapeDtypeStruct((rows, width), BF),
            jax.ShapeDtypeStruct((rows, part), BF),
            jax.ShapeDtypeStruct((rows, part), BF),
            jax.ShapeDtypeStruct((1, part), F32),
        ],
        scratch_shapes=[
            vmem((groups, seq, own, part), BF),
            vmem((rows, width), BF),
            pltpu.SemaphoreType.DMA((seq,)),
            pltpu.SemaphoreType.DMA((count,)),
        ],
        compiler_params=PARAMS,
        cost_estimate=cost(2 * rows * width * part, gathered, grad_act, *pieces, *pieces),
    )(offset, grad_act, gathered, *pieces)


def grad_mlp_call(value, second_half, gathered):
    rows, part = value.shape[0] // 2, value.shape[1]
    tile = row_tile(rows)
    seq, groups, own, _ = gathered.shape
    width = seq * groups * own
    skip = rows // tile if second_half else 0

    def kernel(value, gathered, out, weight, sems):
        @pl.when(pl.program_id(0) == 0)
        def _():
            copies = fetches(gathered, weight, sems)
            for copy in copies:
                copy.start()
            for copy in copies:
                copy.wait()

        out[...] = dot_t(value[...], weight[...].reshape(width, part)).astype(BF)

    return pl.pallas_call(
        kernel,
        name="grad_mlp",
        grid=(rows // tile,),
        in_specs=[pl.BlockSpec((tile, part), lambda i: (i + skip, 0)), ANYWHERE],
        out_specs=pl.BlockSpec((tile, width), by_row),
        out_shape=jax.ShapeDtypeStruct((rows, width), BF),
        scratch_shapes=[vmem((groups, seq, own, part), BF), pltpu.SemaphoreType.DMA((seq,))],
        compiler_params=PARAMS,
        cost_estimate=cost(2 * rows * width * part, value, gathered),
    )(value, gathered)


def branch_call(value, second_half, weight):
    rows, part = value.shape[0] // 2, value.shape[1]
    width = weight.shape[1]
    tile = row_tile(rows)
    skip = rows // tile if second_half else 0

    def kernel(value, weight, out):
        out[...] = dot32(value[...], weight[...]).astype(BF)

    return pl.pallas_call(
        kernel,
        name="branch",
        grid=(rows // tile,),
        in_specs=[
            pl.BlockSpec((tile, part), lambda i: (i + skip, 0)),
            pl.BlockSpec((part, width), fixed),
        ],
        out_specs=pl.BlockSpec((tile, width), by_row),
        out_shape=jax.ShapeDtypeStruct((rows, width), BF),
        compiler_params=PARAMS,
        cost_estimate=cost(2 * rows * width * part, value, weight),
    )(value, weight)


def d_rows_call(left, second_half, right, dp):
    rows, width = right.shape
    blocks = dp // 2
    size = left.shape[1] // dp
    skip = blocks if second_half else 0
    count = 2 if second_half else 1
    each = blocks // count

    def kernel(left, right, *outs):
        value = t_dot(left[...], right[...]).astype(BF)
        for n, out in enumerate(outs):

            @pl.when(pl.program_id(0) // each == n)
            def _(out=out):
                out[...] = value

    def place(n):
        return lambda i: (jnp.clip(i - n * each, 0, each - 1), 0)

    outs = pl.pallas_call(
        kernel,
        name="d_rows",
        grid=(blocks,),
        in_specs=[
            pl.BlockSpec((rows, size), lambda i: (0, i + skip)),
            pl.BlockSpec((rows, width), fixed),
        ],
        out_specs=[pl.BlockSpec((size, width), place(n)) for n in range(count)],
        out_shape=[jax.ShapeDtypeStruct((size * each, width), BF)] * count,
        compiler_params=PARAMS,
        cost_estimate=cost(),
    )(left, right)
    return outs if second_half else outs[0]


def d_proj_call(act, two, seq):
    rows, part = act.shape
    width = two.shape[1]
    tile = max(part // seq, HEAD)

    def kernel(act, two, out):
        out[...] = t_dot(act[...], two[...]).astype(BF)

    return pl.pallas_call(
        kernel,
        name="d_proj",
        grid=(part // tile,),
        in_specs=[pl.BlockSpec((rows, tile), by_column), pl.BlockSpec((rows, width), fixed)],
        out_specs=pl.BlockSpec((tile, width), by_row),
        out_shape=jax.ShapeDtypeStruct((part, width), BF),
        compiler_params=PARAMS,
        cost_estimate=cost(2 * rows * width * part, act, two),
    )(act, two)


def d_fc_call(mlp, grad_pre, dp, seq):
    rows, width = mlp.shape
    part = grad_pre.shape[1]
    own = width // (dp * seq)
    tile = width // dp

    def kernel(mlp, grad, out):
        out[...] = t_dot(mlp[...], grad[...]).astype(BF).reshape(seq, 1, own, part)

    return pl.pallas_call(
        kernel,
        name="d_fc",
        grid=(dp,),
        in_specs=[pl.BlockSpec((rows, tile), by_column), pl.BlockSpec((rows, part), fixed)],
        out_specs=pl.BlockSpec((seq, 1, own, part), lambda i: (0, i, 0, 0)),
        out_shape=jax.ShapeDtypeStruct((seq, dp, own, part), BF),
        compiler_params=PARAMS,
        cost_estimate=cost(2 * rows * width * part, mlp, grad_pre),
    )(mlp, grad_pre)


def local(
    dp,
    seq,
    tokens,
    lengths,
    repos,
    ln1_gain,
    ln1_bias,
    w_query,
    b_query,
    w_key,
    w_value,
    b_value,
    w_out,
    b_out,
    ln2_gain,
    ln2_bias,
    w_fc,
    b_fc,
    w_proj,
    b_proj,
    grad_out,
):
    ring = Ring(dp, seq)
    me, z = ring.me, ring.z
    windows, span, width = tokens.shape
    rows = windows * span
    own = w_query.shape[0]
    block = own * seq
    hidden = w_fc.shape[1]
    part = hidden // dp
    piece = part // seq
    scale = 1.0 / math.sqrt(HEAD)
    kv_end = width + 2 * HEAD
    pairs = dp
    all_rows = dp * rows

    size_hi = lax.div(lengths, jnp.int32(64))
    columns = [
        ln1_gain[:, None],
        ln1_bias[:, None],
        b_query[:, None],
        b_out[:, None],
        ln2_gain[:, None],
        ln2_bias[:, None],
        b_proj[:, None],
        jnp.pad(b_value, (0, own - b_value.shape[0]))[:, None],
        jnp.broadcast_to(size_hi.astype(BF), (own,))[:, None],
        jnp.broadcast_to((lengths - 64 * size_hi).astype(BF), (own,))[:, None],
        jnp.broadcast_to(repos.astype(BF), (own,))[:, None],
        jnp.transpose(b_fc.reshape(-1, own)),
    ]
    n_plain = 11
    n_fc = b_fc.shape[0] // own
    vector_block = jnp.concatenate(columns, axis=1)
    vector_block = jnp.pad(vector_block, ((0, 0), (0, HEAD - vector_block.shape[1])))
    w_qkv = jnp.concatenate([w_query, w_key, w_value, vector_block], axis=1)

    token = jnp.zeros((), F32)

    def tick(*values):
        nonlocal token
        values, token = lax.optimization_barrier((values, token))
        return values

    first_place = z * span
    info = jnp.stack([first_place] + ring.owners)
    token_rows = tokens.reshape(rows, width)
    raw = grad_out.reshape(rows, width)
    n_value = b_value.shape[0]
    raw_near = ring.cross(raw)
    qkv_z = ring.seq_gather_near(w_qkv)
    qkv_z, w_out, raw, raw_near = tick(qkv_z, w_out, raw, raw_near)

    qkv_block = ring.seq_place(qkv_z).reshape(block, -1)
    qkv_near = ring.cross(qkv_block)
    out_z = ring.seq_gather_near(w_out)
    qkv_block, qkv_near, out_z, w_proj = tick(qkv_block, qkv_near, out_z, w_proj)
    proj_all = lax.all_gather(w_proj, "seq", axis=0, tiled=True)

    qkv_far = ring.corner(qkv_block, qkv_near)
    qkv_first = ring.first(qkv_block, qkv_near)
    out_block = ring.seq_place(out_z).reshape(block, -1)
    qkv_far, out_block, qkv_first = tick(qkv_far, out_block, qkv_first)

    qkv_second = ring.second(qkv_far)
    out_near = ring.cross(out_block)
    qkv_second, qkv_first = tick(qkv_second, qkv_first)
    qkv_all = ring.pieces(qkv_first, qkv_second)
    attn_in, query_low, kv_low, rel, nat = enter_call(info, token_rows, qkv_all, dp, own, n_value)
    kv_low, attn_in, query_low, rel, w_fc = tick(kv_low, attn_in, query_low, rel, w_fc)
    kv_z = ring.seq_gather_near(kv_low)
    fc_turned = lax.all_to_all(
        w_fc.reshape(own, dp, part), "dp", split_axis=1, concat_axis=0, tiled=False
    )

    all_lengths = (rel[8] * 64.0 + rel[9]).reshape(dp, block)[:, :1]
    all_repos = rel[10].reshape(dp, block)[:, :1]
    same = (all_repos == all_repos.reshape(1, dp)).astype(F32)
    weights = jnp.sum(all_lengths) / (
        REPOS * jnp.sum(same * all_lengths.reshape(1, dp), axis=1, keepdims=True)
    )
    places = (first_place + jnp.arange(span, dtype=jnp.int32)).astype(F32)
    all_valid = (places[None, :] < all_lengths).astype(F32)
    row_scale = (all_valid * weights).reshape(all_rows, 1)
    valid_rows = all_valid[0].reshape(rows, 1)
    bf_own = jnp.transpose(
        rel[n_plain : n_plain + n_fc, :block].reshape(n_fc, seq, own), (1, 0, 2)
    ).reshape(1, part)
    own_scale = row_scale[:rows]
    kv_z, raw, out_block, out_near, row_scale, own_scale, bf_own, fc_turned = tick(
        kv_z, raw, out_block, out_near, row_scale, own_scale, bf_own, fc_turned
    )
    fc_all = lax.all_gather(fc_turned.reshape(dp, own, part), "seq", axis=0, tiled=False)

    out_far = ring.corner(out_block, out_near)
    out_first = ring.first(out_block, out_near)
    kv_all = ring.seq_place(kv_z).reshape(seq * span, 2 * HEAD)
    key_all, value_all = kv_all[:, :HEAD], kv_all[:, HEAD:]
    attn_low, log_total = attend(
        info, query_low, key_all, jnp.transpose(value_all), valid_rows, pairs, scale
    )
    attn_low, raw, out_far, out_first = tick(attn_low, raw, out_far, out_first)
    out_second = ring.second(out_far)
    out_second, attn_low = tick(out_second, attn_low)
    raw_far = ring.corner(raw, raw_near)
    raw_first = ring.first(raw, raw_near)
    out_all = ring.pieces(out_first, out_second)
    hidden_one, mlp_own = leave_call(attn_low, out_all, token_rows, nat)
    mlp_own, raw_far, raw_first = tick(mlp_own, raw_far, raw_first)

    mlp_near = ring.cross(mlp_own)
    raw_second = ring.second(raw_far)
    raw_second, proj_all = tick(raw_second, proj_all)
    two_all, grad_act = grad_act_call(ring.pieces(raw_first, raw_second), row_scale, proj_all)
    mlp_own, two_all, grad_act, mlp_near = tick(mlp_own, two_all, grad_act, mlp_near)
    mlp_far = ring.corner(mlp_own, mlp_near)
    mlp_first = ring.first(mlp_own, mlp_near)
    mlp_far, mlp_first, fc_all = tick(mlp_far, mlp_first, fc_all)
    mlp_second = ring.second(mlp_far)
    mlp_second, fc_all = tick(mlp_second, fc_all)
    mlp_all, act_low, grad_pre, d_b_fc = feed_call(
        ring.pieces(mlp_first, mlp_second), bf_own, grad_act, fc_all
    )
    odd = grad_mlp_call(grad_pre, True, fc_all)
    odd, grad_pre = tick(odd, grad_pre)
    other = ring.other(odd)
    even = grad_mlp_call(grad_pre, False, fc_all)
    even, other = tick(even, other)
    corner = ring.corner_sums(even, other)
    corner, act_low = tick(corner, act_low)
    far = ring.send_corner(corner)
    branch_odd = branch_call(act_low, True, proj_all)
    d_fc = d_fc_call(mlp_all, grad_pre, dp, seq)
    far, branch_odd, act_low, d_fc = tick(far, branch_odd, act_low, d_fc)
    fc_share = lax.psum_scatter(d_fc, "seq", scatter_dimension=0, tiled=False)
    cross = ring.cross_sums(even, other, far)
    cross, act_low, branch_odd = tick(cross, act_low, branch_odd)
    near = ring.send_cross(cross)
    branch_other = ring.other(branch_odd)
    branch_even = branch_call(act_low, False, proj_all)
    d_proj = d_proj_call(act_low, two_all, seq)
    near, branch_even, branch_other, d_proj = tick(near, branch_even, branch_other, d_proj)
    proj_share = lax.psum_scatter(d_proj, "seq", scatter_dimension=0, tiled=True)
    corner = ring.corner_sums(branch_even, branch_other)
    corner, near = tick(corner, near)

    branch_far = ring.send_corner(corner)
    d_bf = jnp.transpose(d_b_fc.reshape(seq, n_fc, own), (1, 0, 2)).reshape(n_fc, block)
    d_bf = jnp.pad(d_bf, ((0, 8 - n_fc), (0, 0)))
    grad_mid, grad_one, sums, grad_att = middle_call(
        ring.ends(even, other, near), hidden_one, raw, own_scale, valid_rows, nat, out_all
    )
    d_out_odd = d_rows_call(attn_low, True, grad_one, dp)
    grad_att, grad_one, d_out_odd, branch_far = tick(grad_att, grad_one, d_out_odd, branch_far)
    cross = ring.cross_sums(branch_even, branch_other, branch_far)
    cross, grad_att, grad_one, d_out_odd = tick(cross, grad_att, grad_one, d_out_odd)
    branch_near = ring.send_cross(cross)
    d_out_other = ring.other(d_out_odd)
    query_grad, key_grad, value_grad = attend_back(
        info, query_low, grad_att, log_total, key_all, jnp.transpose(key_all), value_all, pairs, scale
    )
    d_out_even = d_rows_call(attn_low, False, grad_one, dp)
    kv_grads = jnp.concatenate([key_grad, value_grad], axis=1)
    kv_mine, kv_sends = ring.seq_cut(kv_grads, rows)
    query_grad, kv_mine, kv_sends, d_out_even, d_out_other, branch_near, fc_share = tick(
        query_grad, kv_mine, kv_sends, d_out_even, d_out_other, branch_near, fc_share
    )
    corner = ring.corner_sums(d_out_even, d_out_other)
    corner, query_grad = tick(corner, query_grad)
    out_far_back = ring.send_corner(corner)
    kv_grad = ring.seq_sum(kv_mine, kv_sends).astype(BF)
    d_q_odd = d_rows_call(attn_in, True, query_grad, dp)
    out_far_back, kv_grad, d_q_odd, query_grad = tick(out_far_back, kv_grad, d_q_odd, query_grad)
    cross = ring.cross_sums(d_out_even, d_out_other, out_far_back)
    cross, d_q_odd, query_grad, kv_grad = tick(cross, d_q_odd, query_grad, kv_grad)
    out_near_back = ring.send_cross(cross)
    d_q_other = ring.other(d_q_odd)
    d_q_even = d_rows_call(attn_in, False, query_grad, dp)
    grad_rows, small = last_call(
        info,
        query_grad,
        kv_grad,
        qkv_all,
        token_rows,
        attn_in,
        rel,
        grad_mid,
        sums,
        d_bf,
        dp,
        own,
        n_value,
    )
    grad_tokens = grad_rows.reshape(windows, span, width)
    cut = width // 2
    small_odd = small[cut:]
    out_near_back, d_q_other, d_q_even, small, small_odd, branch_near = tick(
        out_near_back, d_q_other, d_q_even, small, small_odd, branch_near
    )
    corner = ring.corner_sums(d_q_even, d_q_other)
    corner, small_odd, out_near_back, branch_near = tick(
        corner, small_odd, out_near_back, branch_near
    )
    q_far = ring.send_corner(corner)
    small_other = ring.other(small_odd)
    out_share = ring.scatter_end(d_out_even, d_out_other, out_near_back)
    out_mine, out_sends = ring.seq_cut(out_share, own)
    branch_two = ring.scatter_end(branch_even, branch_other, branch_near)
    output = (hidden_one + branch_two + nat[6:7]).astype(BF).reshape(windows, span, width)
    q_far, small_other, out_mine, out_sends, output = tick(
        q_far, small_other, out_mine, out_sends, output
    )
    cross = ring.cross_sums(d_q_even, d_q_other, q_far)
    cross, small_other, out_sends = tick(cross, small_other, out_sends)
    q_near = ring.send_cross(cross)
    d_w_out = ring.seq_sum(out_mine, out_sends)
    small_corner = ring.corner_sums(small[:cut], small_other)
    q_near, d_w_out, small_corner, proj_share = tick(q_near, d_w_out, small_corner, proj_share)
    q_share = ring.scatter_end(d_q_even, d_q_other, q_near)
    q_mine, q_sends = ring.seq_cut(q_share, own)
    q_mine, q_sends, small_corner = tick(q_mine, q_sends, small_corner)
    d_w_query = ring.seq_sum(q_mine, q_sends)
    small_far = ring.send_corner(small_corner)
    small_near = ring.send_cross(ring.cross_sums(small[:cut], small_other, small_far))
    small_near, fc_share = tick(small_near, fc_share)
    fc_turned_back = lax.all_to_all(fc_share, "dp", split_axis=0, concat_axis=1, tiled=False)
    small_share = ring.scatter_end(small[:cut], small_other, small_near)
    d_small = ring.seq_sum(*ring.seq_cut(small_share, own))
    d_w_proj = proj_share.astype(F32)
    d_w_fc = fc_turned_back.reshape(own, hidden).astype(F32)
    vectors = jnp.transpose(d_small[:, 2 * HEAD :])
    return (
        output,
        grad_tokens,
        vectors[0],
        vectors[1],
        d_w_query,
        vectors[16],
        d_small[:, :HEAD],
        d_small[:, HEAD : 2 * HEAD],
        vectors[17, : b_value.shape[0]],
        d_w_out,
        vectors[8],
        vectors[9],
        vectors[10],
        d_w_fc,
        vectors[24 : 24 + n_fc].reshape(-1),
        d_w_proj,
        vectors[11],
    )


def solution(mesh):
    dp, seq = mesh.shape["dp"], mesh.shape["seq"]
    both = P(("dp", "seq"))
    rows = P(("dp", "seq"), None)
    token = P("dp", "seq", None)

    def run(*args):
        return local(dp, seq, *args)

    return jax.shard_map(
        run,
        mesh=mesh,
        in_specs=(
            token,
            P("dp"),
            P("dp"),
            both,
            both,
            rows,
            both,
            rows,
            rows,
            both,
            rows,
            both,
            both,
            both,
            rows,
            both,
            rows,
            both,
            token,
        ),
        out_specs=(
            token,
            token,
            both,
            both,
            rows,
            both,
            rows,
            rows,
            both,
            rows,
            both,
            both,
            both,
            rows,
            both,
            rows,
            both,
        ),
        check_vma=False,
    )
```

```python
import math

import jax
import jax.numpy as jnp
from jax import lax
from jax.experimental import pallas as pl
from jax.experimental.pallas import tpu as pltpu
from jax.sharding import PartitionSpec as P

HEADS = 16
HEAD = 128
REPOS = 4
BF = jnp.bfloat16
F32 = jnp.float32

norm_epsilon = 1e-05


def normed(values):
    centre = jnp.mean(values, axis=-1, keepdims=True)
    shifted = values - centre
    inverse = lax.rsqrt(jnp.mean(shifted * shifted, axis=-1, keepdims=True) + norm_epsilon)
    return shifted * inverse, inverse


def dot32(left, right):
    return jnp.dot(left, right, preferred_element_type=F32)


def dot_t(left, right):
    return lax.dot_general(left, right, (((1,), (1,)), ((), ())), preferred_element_type=F32)


def t_dot(left, right):
    return lax.dot_general(left, right, (((0,), (0,)), ((), ())), preferred_element_type=F32)


class Ring:
    def __init__(self, dp, seq):
        self.nd, self.ns = dp, seq
        self.me = lax.axis_index("dp")
        self.z = lax.axis_index("seq")
        self.order = list(range(0, dp, 2)) + list(range(1, dp, 2))
        self.owners = [self.me ^ k for k in self.order]

    def swap(self, value, mask):
        return lax.ppermute(value, "dp", [(i, i ^ mask) for i in range(self.nd)])

    def up(self, value, by=1):
        return lax.ppermute(value, "seq", [(i, (i + by) % self.ns) for i in range(self.ns)])

    def back(self, step):
        return lax.rem(self.z - step + self.ns, self.ns)

    def seq_gather_near(self, block):
        return [block] + [self.up(block, step) for step in range(1, self.ns)]

    def seq_place(self, pieces, axis=0):
        shape = pieces[0].shape
        full = jnp.zeros(shape[:axis] + (self.ns,) + shape[axis:], pieces[0].dtype)
        for step, piece in enumerate(pieces):
            full = lax.dynamic_update_slice_in_dim(
                full, jnp.expand_dims(piece, axis), self.back(step), axis
            )
        return full

    def seq_cut(self, share, rows):
        mine = lax.dynamic_slice_in_dim(share, self.z * rows, rows, 0)
        sends = [
            lax.dynamic_slice_in_dim(
                share, lax.rem(self.z + step, self.ns) * rows, rows, 0
            ).astype(BF)
            for step in range(1, self.ns)
        ]
        return mine, sends

    def seq_sum(self, mine, sends):
        for step, part in enumerate(sends):
            mine = mine + self.up(part, step + 1).astype(F32)
        return mine

    def cross(self, block):
        if self.nd == 8:
            return self.swap(block, 2), self.swap(block, 4)
        return ()

    def first(self, block, near):
        if self.nd == 8:
            three = (block,) + tuple(near)
            return three + tuple(self.swap(piece, 1) for piece in three)
        return ()

    def corner(self, block, near):
        if self.nd == 8:
            half = block.shape[0] // 2
            return self.swap(near[0][:half], 4), self.swap(near[1][half:], 2)
        pieces = {0: block}
        bit = 2
        while bit < self.nd:
            for k in list(pieces):
                pieces[k | bit] = self.swap(pieces[k], bit)
            bit *= 2
        return tuple(pieces[k] for k in range(0, self.nd, 2))

    def second(self, far):
        far = jnp.concatenate(far, axis=0)
        return far, self.swap(far, 1)

    def pieces(self, first, second):
        if self.nd == 8:
            return first[:3] + second[:1] + first[3:] + second[1:]
        return second

    def other(self, value):
        if isinstance(value, (list, tuple)):
            return [self.swap(part, 1) for part in value]
        return self.swap(value, 1)

    def part(self, value, at):
        arrays = value if isinstance(value, (list, tuple)) else [value]
        rows = sum(a.shape[0] for a in arrays) * 2 // self.nd
        start = at * rows
        for array in arrays:
            if start < array.shape[0]:
                return array[start : start + rows]
            start -= array.shape[0]

    def corner_sums(self, even, other):
        if self.nd != 8:
            return ()
        held = self.part(even, 3).astype(F32) + self.part(other, 3).astype(F32)
        half = held.shape[0] // 2
        return held[:half].astype(BF), held[half:].astype(BF)

    def send_corner(self, sums):
        if self.nd != 8:
            return ()
        return self.swap(sums[0], 4), self.swap(sums[1], 2)

    def cross_sums(self, even, other, far):
        if self.nd == 8:
            low, high = far
            half = low.shape[0]

            def held(at, first):
                rows = slice(first, first + half)
                return self.part(even, at)[rows].astype(F32) + self.part(other, at)[rows].astype(F32)

            to_x = jnp.concatenate(
                [(held(1, 0) + low.astype(F32)).astype(BF), held(1, half).astype(BF)], axis=0
            )
            to_y = jnp.concatenate(
                [held(2, 0).astype(BF), (held(2, half) + high.astype(F32)).astype(BF)], axis=0
            )
            return to_x, to_y
        held = [
            self.part(even, at).astype(F32) + self.part(other, at).astype(F32)
            for at in range(self.nd // 2)
        ]
        while len(held) > 2:
            cut = len(held) // 2
            held = [
                a + self.swap(b.astype(BF), len(held)).astype(F32)
                for a, b in zip(held[:cut], held[cut:])
            ]
        return held[0].astype(BF), held[1].astype(BF)

    def send_cross(self, sums):
        if self.nd == 8:
            return self.swap(sums[0], 2), self.swap(sums[1], 4)
        return sums[0], self.swap(sums[1], 2)

    def ends(self, even, other, near):
        if self.nd == 8:
            return even, other, near[0], near[1]
        nothing = jnp.zeros_like(near[0])
        return near[0], near[1], nothing, nothing

    def scatter_end(self, even, other, near):
        if self.nd == 8:
            parts = (self.part(even, 0), self.part(other, 0)) + tuple(near)
        else:
            parts = near
        return sum(part.astype(F32) for part in parts)


LOG2E = 1.4426950408889634


def attend_kernel(info, query, key, value_t, valid, out, log_total, *, heads, scale):
    keys = key.shape[0]
    rows = query.shape[0]
    place = lax.broadcasted_iota(jnp.int32, (keys, rows), 1) + info[0]
    allowed = lax.broadcasted_iota(jnp.int32, (keys, rows), 0) <= place
    for h in range(heads):
        cols = slice(h * HEAD, (h + 1) * HEAD)
        scores = dot_t(key[...], query[:, cols]) * (scale * LOG2E)
        scores = jnp.where(allowed, scores, -1e30)
        top = jnp.max(scores, axis=0, keepdims=True)
        expo = jnp.exp2(scores - top)
        total = jnp.sum(expo, axis=0, keepdims=True)
        mixed = dot32(value_t[...], expo.astype(BF)) * (1.0 / total)
        out[:, cols] = (jnp.transpose(mixed) * valid[...]).astype(BF)
        log_total[h] = top + jnp.log2(total)


def attend(info, query, key, value_t, valid, pairs, scale):
    rows, width = query.shape
    keys = key.shape[0]
    heads = HEADS // pairs
    step = heads * HEAD
    whole = lambda k, info: (0, 0)
    return pl.pallas_call(
        lambda *refs: attend_kernel(*refs, heads=heads, scale=scale),
        grid_spec=pltpu.PrefetchScalarGridSpec(
            num_scalar_prefetch=1,
            grid=(pairs,),
            in_specs=[
                pl.BlockSpec((rows, step), lambda k, info: (0, info[1 + k])),
                pl.BlockSpec((keys, HEAD), whole),
                pl.BlockSpec((HEAD, keys), whole),
                pl.BlockSpec((rows, 1), whole),
            ],
            out_specs=[
                pl.BlockSpec((rows, step), lambda k, info: (0, k)),
                pl.BlockSpec((heads, 1, rows), lambda k, info: (k, 0, 0)),
            ],
        ),
        out_shape=[
            jax.ShapeDtypeStruct((rows, width), BF),
            jax.ShapeDtypeStruct((HEADS, 1, rows), F32),
        ],
        compiler_params=pltpu.CompilerParams(vmem_limit_bytes=48 * 1024 * 1024),
        cost_estimate=cost(),
    )(info, query, key, value_t, valid)


def attend_back_kernel(
    info, query, grad, log_total, key, key_t, value, out, key_grad, value_grad, *, heads, scale
):
    keys = key.shape[0]
    rows = query.shape[0]
    place = lax.broadcasted_iota(jnp.int32, (keys, rows), 1) + info[0]
    allowed = lax.broadcasted_iota(jnp.int32, (keys, rows), 0) <= place

    @pl.when(pl.program_id(0) == 0)
    def _():
        key_grad[...] = jnp.zeros_like(key_grad)
        value_grad[...] = jnp.zeros_like(value_grad)

    for h in range(heads):
        cols = slice(h * HEAD, (h + 1) * HEAD)
        scores = dot_t(key[...], query[:, cols]) * (scale * LOG2E)
        scores = jnp.where(allowed, scores, -1e30)
        probs = jnp.exp2(scores - log_total[h])
        dprobs = dot_t(value[...], grad[:, cols])
        delta = jnp.sum(probs * dprobs, axis=0, keepdims=True)
        dscores = (probs * (dprobs - delta)).astype(BF)
        value_grad[...] += dot32(probs.astype(BF), grad[:, cols])
        key_grad[...] += dot32(dscores, query[:, cols]) * scale
        back = dot32(key_t[...], dscores) * scale
        out[:, cols] = jnp.transpose(back).astype(BF)


def attend_back(info, query, grad, log_total, key, key_t, value, pairs, scale):
    rows, width = query.shape
    keys = key.shape[0]
    heads = HEADS // pairs
    step = heads * HEAD
    whole = lambda k, info: (0, 0)
    natural = lambda k, info: (0, info[1 + k])
    return pl.pallas_call(
        lambda *refs: attend_back_kernel(*refs, heads=heads, scale=scale),
        grid_spec=pltpu.PrefetchScalarGridSpec(
            num_scalar_prefetch=1,
            grid=(pairs,),
            in_specs=[
                pl.BlockSpec((rows, step), natural),
                pl.BlockSpec((rows, step), lambda k, info: (0, k)),
                pl.BlockSpec((heads, 1, rows), lambda k, info: (k, 0, 0)),
                pl.BlockSpec((keys, HEAD), whole),
                pl.BlockSpec((HEAD, keys), whole),
                pl.BlockSpec((keys, HEAD), whole),
            ],
            out_specs=[
                pl.BlockSpec((rows, step), natural),
                pl.BlockSpec((keys, HEAD), whole),
                pl.BlockSpec((keys, HEAD), whole),
            ],
        ),
        out_shape=[
            jax.ShapeDtypeStruct((rows, width), BF),
            jax.ShapeDtypeStruct((keys, HEAD), F32),
            jax.ShapeDtypeStruct((keys, HEAD), F32),
        ],
        compiler_params=pltpu.CompilerParams(vmem_limit_bytes=48 * 1024 * 1024),
        cost_estimate=cost(),
    )(info, query, grad, log_total, key, key_t, value)


def fetches(gathered, weight, sems):
    return [
        pltpu.make_async_copy(gathered.at[n], weight.at[:, n], sems.at[n])
        for n in range(gathered.shape[0])
    ]


def row_copies(pieces, full, sems):
    copies = []
    at = 0
    for n, piece in enumerate(pieces):
        size = piece.shape[0]
        copies.append((at, pltpu.make_async_copy(piece, full.at[pl.ds(at, size)], sems.at[n])))
        at += size
    return copies


ROOT = math.sqrt(2.0 / math.pi)
CUBIC = 0.044715


def row_tile(rows):
    return math.gcd(rows, 512)


def by_row(i, *_):
    return (i, 0)


def by_column(i, *_):
    return (0, i)


def fixed(i, *_):
    return (0, 0)


IN_VMEM = pl.BlockSpec(memory_space=pltpu.VMEM)
IN_SMEM = pl.BlockSpec(memory_space=pltpu.SMEM)
ANYWHERE = pl.BlockSpec(memory_space=pl.ANY)


PARAMS = pltpu.CompilerParams(vmem_limit_bytes=54 * 1024 * 1024)


def cost(*_):
    return pl.CostEstimate(flops=1024, bytes_accessed=1024, transcendentals=0)


def columns_of(info, n, size):
    return pl.ds(pl.multiple_of(info[1 + n] * size, HEAD), size)


N_VECTORS = 16


def stack_rows(*lines):
    width = lines[0].shape[1]
    at = lax.broadcasted_iota(jnp.int32, (8, width), 0)
    rows = jnp.zeros((8, width), F32)
    for n, line in enumerate(lines):
        rows = jnp.where(at == n, line, rows)
    return rows


def vmem(shape, dtype):
    return pltpu.VMEM(shape, dtype)


def enter_call(info, tokens, pieces, dp, own, n_value):
    rows, width = tokens.shape
    block = width // dp
    wide = pieces[0].shape[1]
    kv_end = wide - HEAD
    count = len(pieces)

    def kernel(info, tokens, *refs):
        attn, query, kv, rel, nat, weight, sems = refs[count:]
        copies = row_copies(refs[:count], weight, sems)
        for _, copy in copies:
            copy.start()
        x = tokens[...].astype(F32)
        centre = jnp.mean(x, axis=-1, keepdims=True)
        x = x - centre
        inverse = lax.rsqrt(jnp.mean(x * x, axis=-1, keepdims=True) + norm_epsilon)
        for _, copy in copies:
            copy.wait()
        for n in range(dp):
            mine = slice(n * block, (n + 1) * block)
            place = columns_of(info, n, block)
            vectors = jnp.transpose(weight[mine, kv_end:].astype(F32))[:N_VECTORS]
            rel[:, mine] = vectors
            nat[:, place] = vectors
            x = tokens[:, place].astype(F32)
            attn[:, mine] = ((x - centre) * inverse * vectors[0:1] + vectors[1:2]).astype(BF)
        at = lax.broadcasted_iota(jnp.int32, (width, HEAD), 0)
        d = lax.broadcasted_iota(jnp.int32, (width, HEAD), 1)
        chosen = (at == lax.div(d, n_value) * own + lax.rem(d, n_value)).astype(BF)
        offset = dot32(nat[...].astype(BF), chosen)[7:8]
        both = dot32(attn[...], weight[:, width:kv_end])
        kv[:, :HEAD] = both[:, :HEAD].astype(BF)
        kv[:, HEAD:] = (both[:, HEAD:] + offset).astype(BF)
        for at in range(0, width, 512):
            mine = slice(at, at + 512)
            query[:, mine] = (dot32(attn[...], weight[:, mine]) + nat[2:3, mine]).astype(BF)

    return pl.pallas_call(
        kernel,
        name="enter",
        in_specs=[IN_SMEM, IN_VMEM] + [ANYWHERE] * count,
        out_specs=[IN_VMEM] * 5,
        scratch_shapes=[vmem((width, wide), BF), pltpu.SemaphoreType.DMA((count,))],
        out_shape=[
            jax.ShapeDtypeStruct((rows, width), BF),
            jax.ShapeDtypeStruct((rows, width), BF),
            jax.ShapeDtypeStruct((rows, 2 * HEAD), BF),
            jax.ShapeDtypeStruct((N_VECTORS, width), F32),
            jax.ShapeDtypeStruct((N_VECTORS, width), F32),
        ],
        compiler_params=PARAMS,
        cost_estimate=cost(2 * rows * width * kv_end, tokens, *pieces),
    )(info, tokens, *pieces)


def leave_call(attn, pieces, tokens, nat):
    rows, width = tokens.shape
    count = len(pieces)

    def kernel(attn, tokens, nat, *refs):
        hidden, mlp, weight, sems = refs[count:]
        copies = row_copies(refs[:count], weight, sems)
        for _, copy in copies:
            copy.start()
        for _, copy in copies:
            copy.wait()
        for at in range(0, width, 512):
            mine = slice(at, at + 512)
            hidden[:, mine] = (
                dot32(attn[...], weight[:, mine]) + tokens[:, mine].astype(F32) + nat[3:4, mine]
            )
        mlp[...] = (normed(hidden[...])[0] * nat[4:5] + nat[5:6]).astype(BF)

    return pl.pallas_call(
        kernel,
        name="leave",
        in_specs=[IN_VMEM] * 3 + [ANYWHERE] * count,
        out_specs=[IN_VMEM] * 2,
        scratch_shapes=[vmem((width, width), BF), pltpu.SemaphoreType.DMA((count,))],
        out_shape=[
            jax.ShapeDtypeStruct((rows, width), F32),
            jax.ShapeDtypeStruct((rows, width), BF),
        ],
        compiler_params=PARAMS,
        cost_estimate=cost(2 * rows * width * width, tokens, *pieces),
    )(attn, tokens, nat, *pieces)


def middle_call(grads, hidden, top, row_scale, valid, nat, pieces):
    rows, width = hidden.shape
    count = len(pieces)

    def kernel(g0, g1, g2, g3, hidden, top, scale, valid, nat, *refs):
        mid, one, sums, att, weight, sems = refs[count:]
        copies = row_copies(refs[:count], weight, sems)
        for _, copy in copies:
            copy.start()
        grad = (
            g0[...].astype(F32) + g1[...].astype(F32) + g2[...].astype(F32) + g3[...].astype(F32)
        )
        norm, inverse = normed(hidden[...])
        scaled = grad * nat[4:5]
        first = jnp.mean(scaled, axis=-1, keepdims=True)
        second = jnp.mean(scaled * norm, axis=-1, keepdims=True)
        grad_top = top[...].astype(F32) * scale[...]
        total = grad_top + inverse * (scaled - first - norm * second)
        mid[...] = total
        low = total.astype(BF)
        one[...] = low
        sums[...] = stack_rows(
            jnp.sum(low.astype(F32), axis=0, keepdims=True),
            jnp.sum(grad * norm, axis=0, keepdims=True),
            jnp.sum(grad, axis=0, keepdims=True),
            jnp.sum(grad_top.astype(BF).astype(F32), axis=0, keepdims=True),
        )
        for _, copy in copies:
            copy.wait()
        for at in range(0, width, 512):
            mine = slice(at, at + 512)
            att[:, mine] = (dot_t(one[...], weight[mine, :]) * valid[...]).astype(BF)

    return pl.pallas_call(
        kernel,
        name="middle",
        grid=(1,),
        in_specs=[pl.BlockSpec((rows, width), fixed)] * 4
        + [IN_VMEM] * 5
        + [ANYWHERE] * count,
        out_specs=[IN_VMEM] * 4,
        scratch_shapes=[vmem((width, width), BF), pltpu.SemaphoreType.DMA((count,))],
        out_shape=[
            jax.ShapeDtypeStruct((rows, width), F32),
            jax.ShapeDtypeStruct((rows, width), BF),
            jax.ShapeDtypeStruct((8, width), F32),
            jax.ShapeDtypeStruct((rows, width), BF),
        ],
        compiler_params=PARAMS,
        cost_estimate=cost(2 * rows * width * width, hidden, hidden, *pieces),
    )(*grads, hidden, top, row_scale, valid, nat, *pieces)


def last_call(
    info, query_grad, kv_grad, pieces, tokens, attn, rel, mid, sums, d_bf, dp, own, n_value
):
    rows, width = tokens.shape
    block = width // dp
    wide = pieces[0].shape[1]
    count = len(pieces)

    def kernel(info, query, kv, tokens, attn, rel, mid, sums, d_bf, *refs):
        out, small, weight, back, norm, line, sems = refs[count:]
        copies = row_copies(refs[:count], weight, sems)
        for _, copy in copies:
            copy.start()
        value, inverse = normed(tokens[...].astype(F32))
        norm[...] = value
        d_query = jnp.sum(query[...].astype(F32), axis=0, keepdims=True)
        d_value = jnp.sum(kv[:, HEAD:].astype(F32), axis=0, keepdims=True)
        d = lax.broadcasted_iota(jnp.int32, (HEAD, width), 0)
        at = lax.broadcasted_iota(jnp.int32, (HEAD, width), 1)
        chosen = (at == lax.div(d, n_value) * own + lax.rem(d, n_value)).astype(F32)
        spread = jnp.dot(
            jnp.broadcast_to(d_value, (8, HEAD)),
            chosen,
            preferred_element_type=F32,
            precision=lax.Precision.HIGHEST,
        )[:1]
        line[...] = stack_rows(d_query, spread)
        for _, copy in copies:
            copy.wait()
        first = jnp.zeros((rows, 1), F32)
        second = jnp.zeros((rows, 1), F32)
        for n in range(dp):
            mine = slice(n * block, (n + 1) * block)
            grad = dot_t(query[...], weight[mine, :width]) + dot_t(
                kv[...], weight[mine, width : width + 2 * HEAD]
            )
            back[:, mine] = grad
            scaled = grad * rel[0:1, mine]
            first += jnp.sum(scaled, axis=-1, keepdims=True)
            second += jnp.sum(scaled * norm[:, columns_of(info, n, block)], axis=-1, keepdims=True)
        first = first / width
        second = second / width
        for n in range(dp):
            place = columns_of(info, n, block)
            mine = slice(n * block, (n + 1) * block)
            value = norm[:, place]
            grad = back[:, mine]
            scaled = grad * rel[0:1, mine]
            out[:, place] = (mid[:, place] + inverse * (scaled - first - value * second)).astype(BF)
            top = stack_rows(
                jnp.sum(grad * value, axis=0, keepdims=True),
                jnp.sum(grad, axis=0, keepdims=True),
            )
            small[mine, : 2 * HEAD] = t_dot(attn[:, mine], kv[...]).astype(BF)
            low = d_bf[...] if n == 0 else jnp.zeros_like(d_bf[...])
            rows_out = jnp.concatenate(
                [top, sums[:, place], line[:, place], low, jnp.zeros((HEAD - 32, block), F32)]
            )
            small[mine, 2 * HEAD :] = jnp.transpose(rows_out).astype(BF)

    return pl.pallas_call(
        kernel,
        name="last",
        in_specs=[IN_SMEM] + [IN_VMEM] * 8 + [ANYWHERE] * count,
        out_specs=[IN_VMEM] * 2,
        scratch_shapes=[
            vmem((width, wide), BF),
            vmem((rows, width), F32),
            vmem((rows, width), F32),
            vmem((8, width), F32),
            pltpu.SemaphoreType.DMA((count,)),
        ],
        out_shape=[
            jax.ShapeDtypeStruct((rows, width), BF),
            jax.ShapeDtypeStruct((width, 3 * HEAD), BF),
        ],
        compiler_params=PARAMS,
        cost_estimate=cost(2 * rows * width * wide, tokens, mid, *pieces),
    )(info, query_grad, kv_grad, tokens, attn, rel, mid, sums, d_bf, *pieces)


def start_at_first(step, tile, copies):
    @pl.when(step == 0)
    def _():
        for _, copy in copies:
            copy.start()

    for at, copy in copies:
        pl.when(step == at // tile)(copy.wait)


def grad_act_call(pieces, row_scale, weight):
    rows, width = row_scale.shape[0], weight.shape[1]
    part = weight.shape[0]
    tile = row_tile(rows)
    count = len(pieces)

    def kernel(scale, weight, *refs):
        two, out, full, sems = refs[count:]
        step = pl.program_id(0)
        start_at_first(step, tile, row_copies(refs[:count], full, sems))
        raw = full[pl.ds(pl.multiple_of(step * tile, tile), tile), :]
        low = (raw.astype(F32) * scale[...]).astype(BF)
        two[...] = low
        out[...] = dot_t(low, weight[...]).astype(BF)

    return pl.pallas_call(
        kernel,
        name="grad_act",
        grid=(rows // tile,),
        in_specs=[pl.BlockSpec((tile, 1), by_row), pl.BlockSpec((part, width), fixed)]
        + [ANYWHERE] * count,
        out_specs=[pl.BlockSpec((tile, width), by_row), pl.BlockSpec((tile, part), by_row)],
        out_shape=[
            jax.ShapeDtypeStruct((rows, width), BF),
            jax.ShapeDtypeStruct((rows, part), BF),
        ],
        scratch_shapes=[vmem((rows, width), BF), pltpu.SemaphoreType.DMA((count,))],
        compiler_params=PARAMS,
        cost_estimate=cost(2 * rows * width * part, weight, *pieces, *pieces),
    )(row_scale, weight, *pieces)


def feed_call(pieces, offset, grad_act, gathered):
    rows = grad_act.shape[0]
    tile = row_tile(rows)
    count = len(pieces)
    seq, groups, own, part = gathered.shape
    width = seq * groups * own

    def kernel(offset, back, gathered, *refs):
        whole, act, pre, total, weight, full, sems, more = refs[count:]
        step = pl.program_id(0)

        @pl.when(step == 0)
        def _():
            for copy in fetches(gathered, weight, sems):
                copy.start()
            total[...] = jnp.zeros_like(total)

        start_at_first(step, tile, row_copies(refs[:count], full, more))

        @pl.when(step == 0)
        def _():
            for copy in fetches(gathered, weight, sems):
                copy.wait()

        rows_in = full[pl.ds(pl.multiple_of(step * tile, tile), tile), :]
        whole[...] = rows_in
        for at in range(0, part, 256):
            mine = slice(at, at + 256)
            v = dot32(rows_in, weight[:, :, :, mine].reshape(width, 256)) + offset[:, mine]
            square = v * v
            t = jnp.tanh(v * (ROOT + (ROOT * CUBIC) * square))
            up = 0.5 + 0.5 * t
            act[:, mine] = (v * up).astype(BF)
            slope = up + (1.0 - t * t) * (v * (0.5 * ROOT + (1.5 * ROOT * CUBIC) * square))
            grad = (back[:, mine].astype(F32) * slope).astype(BF)
            pre[:, mine] = grad
            total[:, mine] += jnp.sum(grad.astype(F32), axis=0, keepdims=True)

    return pl.pallas_call(
        kernel,
        name="feed",
        grid=(rows // tile,),
        in_specs=[pl.BlockSpec((1, part), fixed), pl.BlockSpec((tile, part), by_row), ANYWHERE]
        + [ANYWHERE] * count,
        out_specs=[
            pl.BlockSpec((tile, width), by_row),
            pl.BlockSpec((tile, part), by_row),
            pl.BlockSpec((tile, part), by_row),
            pl.BlockSpec((1, part), fixed),
        ],
        out_shape=[
            jax.ShapeDtypeStruct((rows, width), BF),
            jax.ShapeDtypeStruct((rows, part), BF),
            jax.ShapeDtypeStruct((rows, part), BF),
            jax.ShapeDtypeStruct((1, part), F32),
        ],
        scratch_shapes=[
            vmem((groups, seq, own, part), BF),
            vmem((rows, width), BF),
            pltpu.SemaphoreType.DMA((seq,)),
            pltpu.SemaphoreType.DMA((count,)),
        ],
        compiler_params=PARAMS,
        cost_estimate=cost(2 * rows * width * part, gathered, grad_act, *pieces, *pieces),
    )(offset, grad_act, gathered, *pieces)


def grad_mlp_call(value, second_half, gathered):
    rows, part = value.shape[0] // 2, value.shape[1]
    tile = row_tile(rows)
    seq, groups, own, _ = gathered.shape
    width = seq * groups * own
    skip = rows // tile if second_half else 0

    def kernel(value, gathered, out, weight, sems):
        @pl.when(pl.program_id(0) == 0)
        def _():
            copies = fetches(gathered, weight, sems)
            for copy in copies:
                copy.start()
            for copy in copies:
                copy.wait()

        out[...] = dot_t(value[...], weight[...].reshape(width, part)).astype(BF)

    return pl.pallas_call(
        kernel,
        name="grad_mlp",
        grid=(rows // tile,),
        in_specs=[pl.BlockSpec((tile, part), lambda i: (i + skip, 0)), ANYWHERE],
        out_specs=pl.BlockSpec((tile, width), by_row),
        out_shape=jax.ShapeDtypeStruct((rows, width), BF),
        scratch_shapes=[vmem((groups, seq, own, part), BF), pltpu.SemaphoreType.DMA((seq,))],
        compiler_params=PARAMS,
        cost_estimate=cost(2 * rows * width * part, value, gathered),
    )(value, gathered)


def branch_call(value, second_half, weight):
    rows, part = value.shape[0] // 2, value.shape[1]
    width = weight.shape[1]
    tile = row_tile(rows)
    skip = rows // tile if second_half else 0

    def kernel(value, weight, out):
        out[...] = dot32(value[...], weight[...]).astype(BF)

    return pl.pallas_call(
        kernel,
        name="branch",
        grid=(rows // tile,),
        in_specs=[
            pl.BlockSpec((tile, part), lambda i: (i + skip, 0)),
            pl.BlockSpec((part, width), fixed),
        ],
        out_specs=pl.BlockSpec((tile, width), by_row),
        out_shape=jax.ShapeDtypeStruct((rows, width), BF),
        compiler_params=PARAMS,
        cost_estimate=cost(2 * rows * width * part, value, weight),
    )(value, weight)


def d_rows_call(left, second_half, right, dp):
    rows, width = right.shape
    blocks = dp // 2
    size = left.shape[1] // dp
    skip = blocks if second_half else 0
    count = 2 if second_half else 1
    each = blocks // count

    def kernel(left, right, *outs):
        value = t_dot(left[...], right[...]).astype(BF)
        for n, out in enumerate(outs):

            @pl.when(pl.program_id(0) // each == n)
            def _(out=out):
                out[...] = value

    def place(n):
        return lambda i: (jnp.clip(i - n * each, 0, each - 1), 0)

    outs = pl.pallas_call(
        kernel,
        name="d_rows",
        grid=(blocks,),
        in_specs=[
            pl.BlockSpec((rows, size), lambda i: (0, i + skip)),
            pl.BlockSpec((rows, width), fixed),
        ],
        out_specs=[pl.BlockSpec((size, width), place(n)) for n in range(count)],
        out_shape=[jax.ShapeDtypeStruct((size * each, width), BF)] * count,
        compiler_params=PARAMS,
        cost_estimate=cost(),
    )(left, right)
    return outs if second_half else outs[0]


def d_proj_call(act, two, seq):
    rows, part = act.shape
    width = two.shape[1]
    tile = max(part // seq, HEAD)

    def kernel(act, two, out):
        out[...] = t_dot(act[...], two[...]).astype(BF)

    return pl.pallas_call(
        kernel,
        name="d_proj",
        grid=(part // tile,),
        in_specs=[pl.BlockSpec((rows, tile), by_column), pl.BlockSpec((rows, width), fixed)],
        out_specs=pl.BlockSpec((tile, width), by_row),
        out_shape=jax.ShapeDtypeStruct((part, width), BF),
        compiler_params=PARAMS,
        cost_estimate=cost(2 * rows * width * part, act, two),
    )(act, two)


def d_fc_call(mlp, grad_pre, dp, seq):
    rows, width = mlp.shape
    part = grad_pre.shape[1]
    own = width // (dp * seq)
    tile = width // dp

    def kernel(mlp, grad, out):
        out[...] = t_dot(mlp[...], grad[...]).astype(BF).reshape(seq, 1, own, part)

    return pl.pallas_call(
        kernel,
        name="d_fc",
        grid=(dp,),
        in_specs=[pl.BlockSpec((rows, tile), by_column), pl.BlockSpec((rows, part), fixed)],
        out_specs=pl.BlockSpec((seq, 1, own, part), lambda i: (0, i, 0, 0)),
        out_shape=jax.ShapeDtypeStruct((seq, dp, own, part), BF),
        compiler_params=PARAMS,
        cost_estimate=cost(2 * rows * width * part, mlp, grad_pre),
    )(mlp, grad_pre)


def local(
    dp,
    seq,
    tokens,
    lengths,
    repos,
    ln1_gain,
    ln1_bias,
    w_query,
    b_query,
    w_key,
    w_value,
    b_value,
    w_out,
    b_out,
    ln2_gain,
    ln2_bias,
    w_fc,
    b_fc,
    w_proj,
    b_proj,
    grad_out,
):
    ring = Ring(dp, seq)
    me, z = ring.me, ring.z
    windows, span, width = tokens.shape
    rows = windows * span
    own = w_query.shape[0]
    block = own * seq
    hidden = w_fc.shape[1]
    part = hidden // dp
    piece = part // seq
    scale = 1.0 / math.sqrt(HEAD)
    kv_end = width + 2 * HEAD
    pairs = dp
    all_rows = dp * rows

    size_hi = lax.div(lengths, jnp.int32(64))
    columns = [
        ln1_gain[:, None],
        ln1_bias[:, None],
        b_query[:, None],
        b_out[:, None],
        ln2_gain[:, None],
        ln2_bias[:, None],
        b_proj[:, None],
        jnp.pad(b_value, (0, own - b_value.shape[0]))[:, None],
        jnp.broadcast_to(size_hi.astype(BF), (own,))[:, None],
        jnp.broadcast_to((lengths - 64 * size_hi).astype(BF), (own,))[:, None],
        jnp.broadcast_to(repos.astype(BF), (own,))[:, None],
        jnp.transpose(b_fc.reshape(-1, own)),
    ]
    n_plain = 11
    n_fc = b_fc.shape[0] // own
    vector_block = jnp.concatenate(columns, axis=1)
    vector_block = jnp.pad(vector_block, ((0, 0), (0, HEAD - vector_block.shape[1])))
    w_qkv = jnp.concatenate([w_query, w_key, w_value, vector_block], axis=1)

    token = jnp.zeros((), F32)

    def tick(*values):
        nonlocal token
        values, token = lax.optimization_barrier((values, token))
        return values

    first_place = z * span
    info = jnp.stack([first_place] + ring.owners)
    token_rows = tokens.reshape(rows, width)
    raw = grad_out.reshape(rows, width)
    n_value = b_value.shape[0]
    raw_near = ring.cross(raw)
    qkv_z = ring.seq_gather_near(w_qkv)
    qkv_z, w_out, raw, raw_near = tick(qkv_z, w_out, raw, raw_near)

    qkv_block = ring.seq_place(qkv_z).reshape(block, -1)
    qkv_near = ring.cross(qkv_block)
    out_z = ring.seq_gather_near(w_out)
    qkv_block, qkv_near, out_z, w_proj = tick(qkv_block, qkv_near, out_z, w_proj)
    proj_all = lax.all_gather(w_proj, "seq", axis=0, tiled=True)

    qkv_far = ring.corner(qkv_block, qkv_near)
    qkv_first = ring.first(qkv_block, qkv_near)
    out_block = ring.seq_place(out_z).reshape(block, -1)
    qkv_far, out_block, qkv_first = tick(qkv_far, out_block, qkv_first)

    qkv_second = ring.second(qkv_far)
    out_near = ring.cross(out_block)
    qkv_second, qkv_first = tick(qkv_second, qkv_first)
    qkv_all = ring.pieces(qkv_first, qkv_second)
    attn_in, query_low, kv_low, rel, nat = enter_call(info, token_rows, qkv_all, dp, own, n_value)
    kv_low, attn_in, query_low, rel, w_fc = tick(kv_low, attn_in, query_low, rel, w_fc)
    kv_z = ring.seq_gather_near(kv_low)
    fc_turned = lax.all_to_all(
        w_fc.reshape(own, dp, part), "dp", split_axis=1, concat_axis=0, tiled=False
    )

    all_lengths = (rel[8] * 64.0 + rel[9]).reshape(dp, block)[:, :1]
    all_repos = rel[10].reshape(dp, block)[:, :1]
    same = (all_repos == all_repos.reshape(1, dp)).astype(F32)
    weights = jnp.sum(all_lengths) / (
        REPOS * jnp.sum(same * all_lengths.reshape(1, dp), axis=1, keepdims=True)
    )
    places = (first_place + jnp.arange(span, dtype=jnp.int32)).astype(F32)
    all_valid = (places[None, :] < all_lengths).astype(F32)
    row_scale = (all_valid * weights).reshape(all_rows, 1)
    valid_rows = all_valid[0].reshape(rows, 1)
    bf_own = jnp.transpose(
        rel[n_plain : n_plain + n_fc, :block].reshape(n_fc, seq, own), (1, 0, 2)
    ).reshape(1, part)
    own_scale = row_scale[:rows]
    kv_z, raw, out_block, out_near, row_scale, own_scale, bf_own, fc_turned = tick(
        kv_z, raw, out_block, out_near, row_scale, own_scale, bf_own, fc_turned
    )
    fc_all = lax.all_gather(fc_turned.reshape(dp, own, part), "seq", axis=0, tiled=False)

    out_far = ring.corner(out_block, out_near)
    out_first = ring.first(out_block, out_near)
    kv_all = ring.seq_place(kv_z).reshape(seq * span, 2 * HEAD)
    key_all, value_all = kv_all[:, :HEAD], kv_all[:, HEAD:]
    attn_low, log_total = attend(
        info, query_low, key_all, jnp.transpose(value_all), valid_rows, pairs, scale
    )
    attn_low, raw, out_far, out_first = tick(attn_low, raw, out_far, out_first)
    out_second = ring.second(out_far)
    out_second, attn_low = tick(out_second, attn_low)
    raw_far = ring.corner(raw, raw_near)
    raw_first = ring.first(raw, raw_near)
    out_all = ring.pieces(out_first, out_second)
    hidden_one, mlp_own = leave_call(attn_low, out_all, token_rows, nat)
    mlp_own, raw_far, raw_first = tick(mlp_own, raw_far, raw_first)

    mlp_near = ring.cross(mlp_own)
    raw_second = ring.second(raw_far)
    raw_second, proj_all = tick(raw_second, proj_all)
    two_all, grad_act = grad_act_call(ring.pieces(raw_first, raw_second), row_scale, proj_all)
    mlp_own, two_all, grad_act, mlp_near = tick(mlp_own, two_all, grad_act, mlp_near)
    mlp_far = ring.corner(mlp_own, mlp_near)
    mlp_first = ring.first(mlp_own, mlp_near)
    mlp_far, mlp_first = tick(mlp_far, mlp_first)
    mlp_second = ring.second(mlp_far)
    (mlp_second,) = tick(mlp_second)
    (fc_all,) = tick(fc_all)
    mlp_all, act_low, grad_pre, d_b_fc = feed_call(
        ring.pieces(mlp_first, mlp_second), bf_own, grad_act, fc_all
    )
    odd = grad_mlp_call(grad_pre, True, fc_all)
    odd, grad_pre = tick(odd, grad_pre)
    other = ring.other(odd)
    even = grad_mlp_call(grad_pre, False, fc_all)
    even, other = tick(even, other)
    corner = ring.corner_sums(even, other)
    corner, act_low = tick(corner, act_low)
    far = ring.send_corner(corner)
    branch_odd = branch_call(act_low, True, proj_all)
    d_fc = d_fc_call(mlp_all, grad_pre, dp, seq)
    far, branch_odd, act_low, d_fc = tick(far, branch_odd, act_low, d_fc)
    fc_share = lax.psum_scatter(d_fc, "seq", scatter_dimension=0, tiled=False)
    cross = ring.cross_sums(even, other, far)
    cross, act_low, branch_odd = tick(cross, act_low, branch_odd)
    near = ring.send_cross(cross)
    branch_other = ring.other(branch_odd)
    branch_even = branch_call(act_low, False, proj_all)
    d_proj = d_proj_call(act_low, two_all, seq)
    near, branch_even, branch_other, d_proj = tick(near, branch_even, branch_other, d_proj)
    proj_share = lax.psum_scatter(d_proj, "seq", scatter_dimension=0, tiled=True)
    corner = ring.corner_sums(branch_even, branch_other)
    corner, near = tick(corner, near)

    branch_far = ring.send_corner(corner)
    d_bf = jnp.transpose(d_b_fc.reshape(seq, n_fc, own), (1, 0, 2)).reshape(n_fc, block)
    d_bf = jnp.pad(d_bf, ((0, 8 - n_fc), (0, 0)))
    grad_mid, grad_one, sums, grad_att = middle_call(
        ring.ends(even, other, near), hidden_one, raw, own_scale, valid_rows, nat, out_all
    )
    d_out_odd = d_rows_call(attn_low, True, grad_one, dp)
    grad_att, grad_one, d_out_odd, branch_far = tick(grad_att, grad_one, d_out_odd, branch_far)
    cross = ring.cross_sums(branch_even, branch_other, branch_far)
    cross, grad_att, grad_one, d_out_odd = tick(cross, grad_att, grad_one, d_out_odd)
    branch_near = ring.send_cross(cross)
    d_out_other = ring.other(d_out_odd)
    query_grad, key_grad, value_grad = attend_back(
        info, query_low, grad_att, log_total, key_all, jnp.transpose(key_all), value_all, pairs, scale
    )
    d_out_even = d_rows_call(attn_low, False, grad_one, dp)
    kv_grads = jnp.concatenate([key_grad, value_grad], axis=1)
    kv_mine, kv_sends = ring.seq_cut(kv_grads, rows)
    query_grad, kv_mine, kv_sends, d_out_even, d_out_other, branch_near, fc_share = tick(
        query_grad, kv_mine, kv_sends, d_out_even, d_out_other, branch_near, fc_share
    )
    corner = ring.corner_sums(d_out_even, d_out_other)
    corner, query_grad = tick(corner, query_grad)
    out_far_back = ring.send_corner(corner)
    kv_grad = ring.seq_sum(kv_mine, kv_sends).astype(BF)
    d_q_odd = d_rows_call(attn_in, True, query_grad, dp)
    out_far_back, kv_grad, d_q_odd, query_grad = tick(out_far_back, kv_grad, d_q_odd, query_grad)
    cross = ring.cross_sums(d_out_even, d_out_other, out_far_back)
    cross, d_q_odd, query_grad, kv_grad = tick(cross, d_q_odd, query_grad, kv_grad)
    out_near_back = ring.send_cross(cross)
    d_q_other = ring.other(d_q_odd)
    d_q_even = d_rows_call(attn_in, False, query_grad, dp)
    grad_rows, small = last_call(
        info,
        query_grad,
        kv_grad,
        qkv_all,
        token_rows,
        attn_in,
        rel,
        grad_mid,
        sums,
        d_bf,
        dp,
        own,
        n_value,
    )
    grad_tokens = grad_rows.reshape(windows, span, width)
    cut = width // 2
    small_odd = small[cut:]
    out_near_back, d_q_other, d_q_even, small, small_odd, branch_near = tick(
        out_near_back, d_q_other, d_q_even, small, small_odd, branch_near
    )
    corner = ring.corner_sums(d_q_even, d_q_other)
    corner, small_odd, out_near_back, branch_near = tick(
        corner, small_odd, out_near_back, branch_near
    )
    q_far = ring.send_corner(corner)
    small_other = ring.other(small_odd)
    out_share = ring.scatter_end(d_out_even, d_out_other, out_near_back)
    out_mine, out_sends = ring.seq_cut(out_share, own)
    branch_two = ring.scatter_end(branch_even, branch_other, branch_near)
    output = (hidden_one + branch_two + nat[6:7]).astype(BF).reshape(windows, span, width)
    small_other, out_mine, out_sends, output = tick(small_other, out_mine, out_sends, output)
    small_far = ring.send_corner(ring.corner_sums(small[:cut], small_other))
    q_far, small_far = tick(q_far, small_far)
    cross = ring.cross_sums(d_q_even, d_q_other, q_far)
    small_cross = ring.cross_sums(small[:cut], small_other, small_far)
    cross, out_sends, small_cross = tick(cross, out_sends, small_cross)
    q_near = ring.send_cross(cross)
    small_near = ring.send_cross(small_cross)
    d_w_out = ring.seq_sum(out_mine, out_sends)
    q_near, small_near, d_w_out, proj_share = tick(q_near, small_near, d_w_out, proj_share)
    q_share = ring.scatter_end(d_q_even, d_q_other, q_near)
    small_share = ring.scatter_end(small[:cut], small_other, small_near)
    q_mine, q_sends = ring.seq_cut(q_share, own)
    small_mine, small_sends = ring.seq_cut(small_share, own)
    sends = [jnp.concatenate(pair, axis=1) for pair in zip(q_sends, small_sends)]
    q_mine, small_mine, sends, fc_share = tick(q_mine, small_mine, sends, fc_share)
    fc_turned_back = lax.all_to_all(fc_share, "dp", split_axis=0, concat_axis=1, tiled=False)
    both = ring.seq_sum(jnp.concatenate([q_mine, small_mine], axis=1), sends)
    d_w_query, d_small = both[:, :width], both[:, width:]
    d_w_proj = proj_share.astype(F32)
    d_w_fc = fc_turned_back.reshape(own, hidden).astype(F32)
    vectors = jnp.transpose(d_small[:, 2 * HEAD :])
    return (
        output,
        grad_tokens,
        vectors[0],
        vectors[1],
        d_w_query,
        vectors[16],
        d_small[:, :HEAD],
        d_small[:, HEAD : 2 * HEAD],
        vectors[17, : b_value.shape[0]],
        d_w_out,
        vectors[8],
        vectors[9],
        vectors[10],
        d_w_fc,
        vectors[24 : 24 + n_fc].reshape(-1),
        d_w_proj,
        vectors[11],
    )


def solution(mesh):
    dp, seq = mesh.shape["dp"], mesh.shape["seq"]
    both = P(("dp", "seq"))
    rows = P(("dp", "seq"), None)
    token = P("dp", "seq", None)

    def run(*args):
        return local(dp, seq, *args)

    return jax.shard_map(
        run,
        mesh=mesh,
        in_specs=(
            token,
            P("dp"),
            P("dp"),
            both,
            both,
            rows,
            both,
            rows,
            rows,
            both,
            rows,
            both,
            both,
            both,
            rows,
            both,
            rows,
            both,
            token,
        ),
        out_specs=(
            token,
            token,
            both,
            both,
            rows,
            both,
            rows,
            rows,
            both,
            rows,
            both,
            both,
            both,
            rows,
            both,
            rows,
            both,
        ),
        check_vma=False,
    )
```

```python
import math

import jax
import jax.numpy as jnp
from jax import lax
from jax.experimental import pallas as pl
from jax.experimental.pallas import tpu as pltpu
from jax.sharding import PartitionSpec as P

HEADS = 16
HEAD = 128
REPOS = 4
BF = jnp.bfloat16
F32 = jnp.float32

norm_epsilon = 1e-05


def normed(values):
    centre = jnp.mean(values, axis=-1, keepdims=True)
    shifted = values - centre
    inverse = lax.rsqrt(jnp.mean(shifted * shifted, axis=-1, keepdims=True) + norm_epsilon)
    return shifted * inverse, inverse


def dot32(left, right):
    return jnp.dot(left, right, preferred_element_type=F32)


def dot_t(left, right):
    return lax.dot_general(left, right, (((1,), (1,)), ((), ())), preferred_element_type=F32)


def t_dot(left, right):
    return lax.dot_general(left, right, (((0,), (0,)), ((), ())), preferred_element_type=F32)


class Ring:
    def __init__(self, dp, seq):
        self.nd, self.ns = dp, seq
        self.me = lax.axis_index("dp")
        self.z = lax.axis_index("seq")
        self.order = list(range(0, dp, 2)) + list(range(1, dp, 2))
        self.owners = [self.me ^ k for k in self.order]

    def swap(self, value, mask):
        return lax.ppermute(value, "dp", [(i, i ^ mask) for i in range(self.nd)])

    def up(self, value, by=1):
        return lax.ppermute(value, "seq", [(i, (i + by) % self.ns) for i in range(self.ns)])

    def back(self, step):
        return lax.rem(self.z - step + self.ns, self.ns)

    def seq_gather_near(self, block):
        return [block] + [self.up(block, step) for step in range(1, self.ns)]

    def seq_place(self, pieces, axis=0):
        shape = pieces[0].shape
        full = jnp.zeros(shape[:axis] + (self.ns,) + shape[axis:], pieces[0].dtype)
        for step, piece in enumerate(pieces):
            full = lax.dynamic_update_slice_in_dim(
                full, jnp.expand_dims(piece, axis), self.back(step), axis
            )
        return full

    def seq_cut(self, share, rows):
        mine = lax.dynamic_slice_in_dim(share, self.z * rows, rows, 0)
        sends = [
            lax.dynamic_slice_in_dim(
                share, lax.rem(self.z + step, self.ns) * rows, rows, 0
            ).astype(BF)
            for step in range(1, self.ns)
        ]
        return mine, sends

    def seq_sum(self, mine, sends):
        for step, part in enumerate(sends):
            mine = mine + self.up(part, step + 1).astype(F32)
        return mine

    def cross(self, block):
        if self.nd == 8:
            return self.swap(block, 2), self.swap(block, 4)
        return ()

    def first(self, block, near):
        if self.nd == 8:
            three = (block,) + tuple(near)
            return three + tuple(self.swap(piece, 1) for piece in three)
        return ()

    def corner(self, block, near):
        if self.nd == 8:
            half = block.shape[0] // 2
            return self.swap(near[0][:half], 4), self.swap(near[1][half:], 2)
        pieces = {0: block}
        bit = 2
        while bit < self.nd:
            for k in list(pieces):
                pieces[k | bit] = self.swap(pieces[k], bit)
            bit *= 2
        return tuple(pieces[k] for k in range(0, self.nd, 2))

    def second(self, far):
        far = jnp.concatenate(far, axis=0)
        return far, self.swap(far, 1)

    def pieces(self, first, second):
        if self.nd == 8:
            return first[:3] + second[:1] + first[3:] + second[1:]
        return second

    def other(self, value):
        if isinstance(value, (list, tuple)):
            return [self.swap(part, 1) for part in value]
        return self.swap(value, 1)

    def part(self, value, at):
        arrays = value if isinstance(value, (list, tuple)) else [value]
        rows = sum(a.shape[0] for a in arrays) * 2 // self.nd
        start = at * rows
        for array in arrays:
            if start < array.shape[0]:
                return array[start : start + rows]
            start -= array.shape[0]

    def corner_sums(self, even, other):
        if self.nd != 8:
            return ()
        held = self.part(even, 3).astype(F32) + self.part(other, 3).astype(F32)
        half = held.shape[0] // 2
        return held[:half].astype(BF), held[half:].astype(BF)

    def send_corner(self, sums):
        if self.nd != 8:
            return ()
        return self.swap(sums[0], 4), self.swap(sums[1], 2)

    def cross_sums(self, even, other, far):
        if self.nd == 8:
            low, high = far
            half = low.shape[0]

            def held(at, first):
                rows = slice(first, first + half)
                return self.part(even, at)[rows].astype(F32) + self.part(other, at)[rows].astype(F32)

            to_x = jnp.concatenate(
                [(held(1, 0) + low.astype(F32)).astype(BF), held(1, half).astype(BF)], axis=0
            )
            to_y = jnp.concatenate(
                [held(2, 0).astype(BF), (held(2, half) + high.astype(F32)).astype(BF)], axis=0
            )
            return to_x, to_y
        held = [
            self.part(even, at).astype(F32) + self.part(other, at).astype(F32)
            for at in range(self.nd // 2)
        ]
        while len(held) > 2:
            cut = len(held) // 2
            held = [
                a + self.swap(b.astype(BF), len(held)).astype(F32)
                for a, b in zip(held[:cut], held[cut:])
            ]
        return held[0].astype(BF), held[1].astype(BF)

    def send_cross(self, sums):
        if self.nd == 8:
            return self.swap(sums[0], 2), self.swap(sums[1], 4)
        return sums[0], self.swap(sums[1], 2)

    def ends(self, even, other, near):
        if self.nd == 8:
            return even, other, near[0], near[1]
        nothing = jnp.zeros_like(near[0])
        return near[0], near[1], nothing, nothing

    def scatter_end(self, even, other, near):
        if self.nd == 8:
            parts = (self.part(even, 0), self.part(other, 0)) + tuple(near)
        else:
            parts = near
        return sum(part.astype(F32) for part in parts)


LOG2E = 1.4426950408889634


def attend_kernel(info, query, key, value_t, valid, out, log_total, *, heads, scale):
    keys = key.shape[0]
    rows = query.shape[0]
    place = lax.broadcasted_iota(jnp.int32, (keys, rows), 1) + info[0]
    allowed = lax.broadcasted_iota(jnp.int32, (keys, rows), 0) <= place
    for h in range(heads):
        cols = slice(h * HEAD, (h + 1) * HEAD)
        scores = dot_t(key[...], query[:, cols]) * (scale * LOG2E)
        scores = jnp.where(allowed, scores, -1e30)
        top = jnp.max(scores, axis=0, keepdims=True)
        expo = jnp.exp2(scores - top)
        total = jnp.sum(expo, axis=0, keepdims=True)
        mixed = dot32(value_t[...], expo.astype(BF)) * (1.0 / total)
        out[:, cols] = (jnp.transpose(mixed) * valid[...]).astype(BF)
        log_total[h] = top + jnp.log2(total)


def attend(info, query, key, value_t, valid, pairs, scale):
    rows, width = query.shape
    keys = key.shape[0]
    heads = HEADS // pairs
    step = heads * HEAD
    whole = lambda k, info: (0, 0)
    return pl.pallas_call(
        lambda *refs: attend_kernel(*refs, heads=heads, scale=scale),
        grid_spec=pltpu.PrefetchScalarGridSpec(
            num_scalar_prefetch=1,
            grid=(pairs,),
            in_specs=[
                pl.BlockSpec((rows, step), lambda k, info: (0, info[1 + k])),
                pl.BlockSpec((keys, HEAD), whole),
                pl.BlockSpec((HEAD, keys), whole),
                pl.BlockSpec((rows, 1), whole),
            ],
            out_specs=[
                pl.BlockSpec((rows, step), lambda k, info: (0, k)),
                pl.BlockSpec((heads, 1, rows), lambda k, info: (k, 0, 0)),
            ],
        ),
        out_shape=[
            jax.ShapeDtypeStruct((rows, width), BF),
            jax.ShapeDtypeStruct((HEADS, 1, rows), F32),
        ],
        compiler_params=pltpu.CompilerParams(vmem_limit_bytes=48 * 1024 * 1024),
        cost_estimate=cost(),
    )(info, query, key, value_t, valid)


def attend_back_kernel(
    info, query, grad, log_total, key, key_t, value, out, key_grad, value_grad, *, heads, scale
):
    keys = key.shape[0]
    rows = query.shape[0]
    place = lax.broadcasted_iota(jnp.int32, (keys, rows), 1) + info[0]
    allowed = lax.broadcasted_iota(jnp.int32, (keys, rows), 0) <= place

    @pl.when(pl.program_id(0) == 0)
    def _():
        key_grad[...] = jnp.zeros_like(key_grad)
        value_grad[...] = jnp.zeros_like(value_grad)

    for h in range(heads):
        cols = slice(h * HEAD, (h + 1) * HEAD)
        scores = dot_t(key[...], query[:, cols]) * (scale * LOG2E)
        scores = jnp.where(allowed, scores, -1e30)
        probs = jnp.exp2(scores - log_total[h])
        dprobs = dot_t(value[...], grad[:, cols])
        delta = jnp.sum(probs * dprobs, axis=0, keepdims=True)
        dscores = (probs * (dprobs - delta)).astype(BF)
        value_grad[...] += dot32(probs.astype(BF), grad[:, cols])
        key_grad[...] += dot32(dscores, query[:, cols]) * scale
        back = dot32(key_t[...], dscores) * scale
        out[:, cols] = jnp.transpose(back).astype(BF)


def attend_back(info, query, grad, log_total, key, key_t, value, pairs, scale):
    rows, width = query.shape
    keys = key.shape[0]
    heads = HEADS // pairs
    step = heads * HEAD
    whole = lambda k, info: (0, 0)
    natural = lambda k, info: (0, info[1 + k])
    return pl.pallas_call(
        lambda *refs: attend_back_kernel(*refs, heads=heads, scale=scale),
        grid_spec=pltpu.PrefetchScalarGridSpec(
            num_scalar_prefetch=1,
            grid=(pairs,),
            in_specs=[
                pl.BlockSpec((rows, step), natural),
                pl.BlockSpec((rows, step), lambda k, info: (0, k)),
                pl.BlockSpec((heads, 1, rows), lambda k, info: (k, 0, 0)),
                pl.BlockSpec((keys, HEAD), whole),
                pl.BlockSpec((HEAD, keys), whole),
                pl.BlockSpec((keys, HEAD), whole),
            ],
            out_specs=[
                pl.BlockSpec((rows, step), natural),
                pl.BlockSpec((keys, HEAD), whole),
                pl.BlockSpec((keys, HEAD), whole),
            ],
        ),
        out_shape=[
            jax.ShapeDtypeStruct((rows, width), BF),
            jax.ShapeDtypeStruct((keys, HEAD), F32),
            jax.ShapeDtypeStruct((keys, HEAD), F32),
        ],
        compiler_params=pltpu.CompilerParams(vmem_limit_bytes=48 * 1024 * 1024),
        cost_estimate=cost(),
    )(info, query, grad, log_total, key, key_t, value)


def fetches(gathered, weight, sems):
    return [
        pltpu.make_async_copy(gathered.at[n], weight.at[:, n], sems.at[n])
        for n in range(gathered.shape[0])
    ]


def row_copies(pieces, full, sems):
    copies = []
    at = 0
    for n, piece in enumerate(pieces):
        size = piece.shape[0]
        copies.append((at, pltpu.make_async_copy(piece, full.at[pl.ds(at, size)], sems.at[n])))
        at += size
    return copies


ROOT = math.sqrt(2.0 / math.pi)
CUBIC = 0.044715


def row_tile(rows):
    return math.gcd(rows, 512)


def by_row(i, *_):
    return (i, 0)


def by_column(i, *_):
    return (0, i)


def fixed(i, *_):
    return (0, 0)


IN_VMEM = pl.BlockSpec(memory_space=pltpu.VMEM)
IN_SMEM = pl.BlockSpec(memory_space=pltpu.SMEM)
ANYWHERE = pl.BlockSpec(memory_space=pl.ANY)


PARAMS = pltpu.CompilerParams(vmem_limit_bytes=54 * 1024 * 1024)


def cost(*_):
    return pl.CostEstimate(flops=1024, bytes_accessed=1024, transcendentals=0)


def columns_of(info, n, size):
    return pl.ds(pl.multiple_of(info[1 + n] * size, HEAD), size)


N_VECTORS = 16


def stack_rows(*lines):
    width = lines[0].shape[1]
    at = lax.broadcasted_iota(jnp.int32, (8, width), 0)
    rows = jnp.zeros((8, width), F32)
    for n, line in enumerate(lines):
        rows = jnp.where(at == n, line, rows)
    return rows


def vmem(shape, dtype):
    return pltpu.VMEM(shape, dtype)


def enter_call(info, tokens, pieces, dp, own, n_value):
    rows, width = tokens.shape
    block = width // dp
    wide = pieces[0].shape[1]
    kv_end = wide - HEAD
    count = len(pieces)

    def kernel(info, tokens, *refs):
        attn, query, kv, rel, nat, weight, sems = refs[count:]
        copies = row_copies(refs[:count], weight, sems)
        for _, copy in copies:
            copy.start()
        x = tokens[...].astype(F32)
        centre = jnp.mean(x, axis=-1, keepdims=True)
        x = x - centre
        inverse = lax.rsqrt(jnp.mean(x * x, axis=-1, keepdims=True) + norm_epsilon)
        for _, copy in copies:
            copy.wait()
        for n in range(dp):
            mine = slice(n * block, (n + 1) * block)
            place = columns_of(info, n, block)
            vectors = jnp.transpose(weight[mine, kv_end:].astype(F32))[:N_VECTORS]
            rel[:, mine] = vectors
            nat[:, place] = vectors
            x = tokens[:, place].astype(F32)
            attn[:, mine] = ((x - centre) * inverse * vectors[0:1] + vectors[1:2]).astype(BF)
        at = lax.broadcasted_iota(jnp.int32, (width, HEAD), 0)
        d = lax.broadcasted_iota(jnp.int32, (width, HEAD), 1)
        chosen = (at == lax.div(d, n_value) * own + lax.rem(d, n_value)).astype(BF)
        offset = dot32(nat[...].astype(BF), chosen)[7:8]
        both = dot32(attn[...], weight[:, width:kv_end])
        kv[:, :HEAD] = both[:, :HEAD].astype(BF)
        kv[:, HEAD:] = (both[:, HEAD:] + offset).astype(BF)
        for at in range(0, width, 512):
            mine = slice(at, at + 512)
            query[:, mine] = (dot32(attn[...], weight[:, mine]) + nat[2:3, mine]).astype(BF)

    return pl.pallas_call(
        kernel,
        name="enter",
        in_specs=[IN_SMEM, IN_VMEM] + [ANYWHERE] * count,
        out_specs=[IN_VMEM] * 5,
        scratch_shapes=[vmem((width, wide), BF), pltpu.SemaphoreType.DMA((count,))],
        out_shape=[
            jax.ShapeDtypeStruct((rows, width), BF),
            jax.ShapeDtypeStruct((rows, width), BF),
            jax.ShapeDtypeStruct((rows, 2 * HEAD), BF),
            jax.ShapeDtypeStruct((N_VECTORS, width), F32),
            jax.ShapeDtypeStruct((N_VECTORS, width), F32),
        ],
        compiler_params=PARAMS,
        cost_estimate=cost(2 * rows * width * kv_end, tokens, *pieces),
    )(info, tokens, *pieces)


def leave_call(attn, pieces, tokens, nat):
    rows, width = tokens.shape
    count = len(pieces)

    def kernel(attn, tokens, nat, *refs):
        hidden, mlp, weight, sems = refs[count:]
        copies = row_copies(refs[:count], weight, sems)
        for _, copy in copies:
            copy.start()
        for _, copy in copies:
            copy.wait()
        for at in range(0, width, 512):
            mine = slice(at, at + 512)
            hidden[:, mine] = (
                dot32(attn[...], weight[:, mine]) + tokens[:, mine].astype(F32) + nat[3:4, mine]
            )
        mlp[...] = (normed(hidden[...])[0] * nat[4:5] + nat[5:6]).astype(BF)

    return pl.pallas_call(
        kernel,
        name="leave",
        in_specs=[IN_VMEM] * 3 + [ANYWHERE] * count,
        out_specs=[IN_VMEM] * 2,
        scratch_shapes=[vmem((width, width), BF), pltpu.SemaphoreType.DMA((count,))],
        out_shape=[
            jax.ShapeDtypeStruct((rows, width), F32),
            jax.ShapeDtypeStruct((rows, width), BF),
        ],
        compiler_params=PARAMS,
        cost_estimate=cost(2 * rows * width * width, tokens, *pieces),
    )(attn, tokens, nat, *pieces)


def middle_call(grads, hidden, top, row_scale, valid, nat, pieces):
    rows, width = hidden.shape
    count = len(pieces)

    def kernel(g0, g1, g2, g3, hidden, top, scale, valid, nat, *refs):
        mid, one, sums, att, weight, sems = refs[count:]
        copies = row_copies(refs[:count], weight, sems)
        for _, copy in copies:
            copy.start()
        grad = (
            g0[...].astype(F32) + g1[...].astype(F32) + g2[...].astype(F32) + g3[...].astype(F32)
        )
        norm, inverse = normed(hidden[...])
        scaled = grad * nat[4:5]
        first = jnp.mean(scaled, axis=-1, keepdims=True)
        second = jnp.mean(scaled * norm, axis=-1, keepdims=True)
        grad_top = top[...].astype(F32) * scale[...]
        total = grad_top + inverse * (scaled - first - norm * second)
        mid[...] = total
        low = total.astype(BF)
        one[...] = low
        sums[...] = stack_rows(
            jnp.sum(low.astype(F32), axis=0, keepdims=True),
            jnp.sum(grad * norm, axis=0, keepdims=True),
            jnp.sum(grad, axis=0, keepdims=True),
            jnp.sum(grad_top.astype(BF).astype(F32), axis=0, keepdims=True),
        )
        for _, copy in copies:
            copy.wait()
        for at in range(0, width, 512):
            mine = slice(at, at + 512)
            att[:, mine] = (dot_t(one[...], weight[mine, :]) * valid[...]).astype(BF)

    return pl.pallas_call(
        kernel,
        name="middle",
        grid=(1,),
        in_specs=[pl.BlockSpec((rows, width), fixed)] * 4
        + [IN_VMEM] * 5
        + [ANYWHERE] * count,
        out_specs=[IN_VMEM] * 4,
        scratch_shapes=[vmem((width, width), BF), pltpu.SemaphoreType.DMA((count,))],
        out_shape=[
            jax.ShapeDtypeStruct((rows, width), F32),
            jax.ShapeDtypeStruct((rows, width), BF),
            jax.ShapeDtypeStruct((8, width), F32),
            jax.ShapeDtypeStruct((rows, width), BF),
        ],
        compiler_params=PARAMS,
        cost_estimate=cost(2 * rows * width * width, hidden, hidden, *pieces),
    )(*grads, hidden, top, row_scale, valid, nat, *pieces)


def last_call(
    info, query_grad, kv_grad, pieces, tokens, attn, rel, mid, sums, d_bf, dp, own, n_value
):
    rows, width = tokens.shape
    block = width // dp
    wide = pieces[0].shape[1]
    count = len(pieces)

    def kernel(info, query, kv, tokens, attn, rel, mid, sums, d_bf, *refs):
        out, small, weight, back, norm, line, sems = refs[count:]
        copies = row_copies(refs[:count], weight, sems)
        for _, copy in copies:
            copy.start()
        value, inverse = normed(tokens[...].astype(F32))
        norm[...] = value
        d_query = jnp.sum(query[...].astype(F32), axis=0, keepdims=True)
        d_value = jnp.sum(kv[:, HEAD:].astype(F32), axis=0, keepdims=True)
        d = lax.broadcasted_iota(jnp.int32, (HEAD, width), 0)
        at = lax.broadcasted_iota(jnp.int32, (HEAD, width), 1)
        chosen = (at == lax.div(d, n_value) * own + lax.rem(d, n_value)).astype(F32)
        spread = jnp.dot(
            jnp.broadcast_to(d_value, (8, HEAD)),
            chosen,
            preferred_element_type=F32,
            precision=lax.Precision.HIGHEST,
        )[:1]
        line[...] = stack_rows(d_query, spread)
        for _, copy in copies:
            copy.wait()
        first = jnp.zeros((rows, 1), F32)
        second = jnp.zeros((rows, 1), F32)
        for n in range(dp):
            mine = slice(n * block, (n + 1) * block)
            grad = dot_t(query[...], weight[mine, :width]) + dot_t(
                kv[...], weight[mine, width : width + 2 * HEAD]
            )
            back[:, mine] = grad
            scaled = grad * rel[0:1, mine]
            first += jnp.sum(scaled, axis=-1, keepdims=True)
            second += jnp.sum(scaled * norm[:, columns_of(info, n, block)], axis=-1, keepdims=True)
        first = first / width
        second = second / width
        for n in range(dp):
            place = columns_of(info, n, block)
            mine = slice(n * block, (n + 1) * block)
            value = norm[:, place]
            grad = back[:, mine]
            scaled = grad * rel[0:1, mine]
            out[:, place] = (mid[:, place] + inverse * (scaled - first - value * second)).astype(BF)
            top = stack_rows(
                jnp.sum(grad * value, axis=0, keepdims=True),
                jnp.sum(grad, axis=0, keepdims=True),
            )
            small[mine, : 2 * HEAD] = t_dot(attn[:, mine], kv[...]).astype(BF)
            low = d_bf[...] if n == 0 else jnp.zeros_like(d_bf[...])
            rows_out = jnp.concatenate(
                [top, sums[:, place], line[:, place], low, jnp.zeros((HEAD - 32, block), F32)]
            )
            small[mine, 2 * HEAD :] = jnp.transpose(rows_out).astype(BF)

    return pl.pallas_call(
        kernel,
        name="last",
        in_specs=[IN_SMEM] + [IN_VMEM] * 8 + [ANYWHERE] * count,
        out_specs=[IN_VMEM] * 2,
        scratch_shapes=[
            vmem((width, wide), BF),
            vmem((rows, width), F32),
            vmem((rows, width), F32),
            vmem((8, width), F32),
            pltpu.SemaphoreType.DMA((count,)),
        ],
        out_shape=[
            jax.ShapeDtypeStruct((rows, width), BF),
            jax.ShapeDtypeStruct((width, 3 * HEAD), BF),
        ],
        compiler_params=PARAMS,
        cost_estimate=cost(2 * rows * width * wide, tokens, mid, *pieces),
    )(info, query_grad, kv_grad, tokens, attn, rel, mid, sums, d_bf, *pieces)


def start_at_first(step, tile, copies):
    @pl.when(step == 0)
    def _():
        for _, copy in copies:
            copy.start()

    for at, copy in copies:
        pl.when(step == at // tile)(copy.wait)


def grad_act_call(pieces, row_scale, weight):
    rows, width = row_scale.shape[0], weight.shape[1]
    part = weight.shape[0]
    tile = row_tile(rows)
    count = len(pieces)

    def kernel(scale, weight, *refs):
        two, out, full, sems = refs[count:]
        step = pl.program_id(0)
        start_at_first(step, tile, row_copies(refs[:count], full, sems))
        raw = full[pl.ds(pl.multiple_of(step * tile, tile), tile), :]
        low = (raw.astype(F32) * scale[...]).astype(BF)
        two[...] = low
        out[...] = dot_t(low, weight[...]).astype(BF)

    return pl.pallas_call(
        kernel,
        name="grad_act",
        grid=(rows // tile,),
        in_specs=[pl.BlockSpec((tile, 1), by_row), pl.BlockSpec((part, width), fixed)]
        + [ANYWHERE] * count,
        out_specs=[pl.BlockSpec((tile, width), by_row), pl.BlockSpec((tile, part), by_row)],
        out_shape=[
            jax.ShapeDtypeStruct((rows, width), BF),
            jax.ShapeDtypeStruct((rows, part), BF),
        ],
        scratch_shapes=[vmem((rows, width), BF), pltpu.SemaphoreType.DMA((count,))],
        compiler_params=PARAMS,
        cost_estimate=cost(2 * rows * width * part, weight, *pieces, *pieces),
    )(row_scale, weight, *pieces)


def feed_call(pieces, offset, grad_act, gathered):
    rows = grad_act.shape[0]
    tile = row_tile(rows)
    count = len(pieces)
    seq, groups, own, part = gathered.shape
    width = seq * groups * own

    def kernel(offset, back, gathered, *refs):
        whole, act, pre, total, weight, full, sems, more = refs[count:]
        step = pl.program_id(0)

        @pl.when(step == 0)
        def _():
            for copy in fetches(gathered, weight, sems):
                copy.start()
            total[...] = jnp.zeros_like(total)

        start_at_first(step, tile, row_copies(refs[:count], full, more))

        @pl.when(step == 0)
        def _():
            for copy in fetches(gathered, weight, sems):
                copy.wait()

        rows_in = full[pl.ds(pl.multiple_of(step * tile, tile), tile), :]
        whole[...] = rows_in
        for at in range(0, part, 256):
            mine = slice(at, at + 256)
            v = dot32(rows_in, weight[:, :, :, mine].reshape(width, 256)) + offset[:, mine]
            square = v * v
            t = jnp.tanh(v * (ROOT + (ROOT * CUBIC) * square))
            up = 0.5 + 0.5 * t
            act[:, mine] = (v * up).astype(BF)
            slope = up + (1.0 - t * t) * (v * (0.5 * ROOT + (1.5 * ROOT * CUBIC) * square))
            grad = (back[:, mine].astype(F32) * slope).astype(BF)
            pre[:, mine] = grad
            total[:, mine] += jnp.sum(grad.astype(F32), axis=0, keepdims=True)

    return pl.pallas_call(
        kernel,
        name="feed",
        grid=(rows // tile,),
        in_specs=[pl.BlockSpec((1, part), fixed), pl.BlockSpec((tile, part), by_row), ANYWHERE]
        + [ANYWHERE] * count,
        out_specs=[
            pl.BlockSpec((tile, width), by_row),
            pl.BlockSpec((tile, part), by_row),
            pl.BlockSpec((tile, part), by_row),
            pl.BlockSpec((1, part), fixed),
        ],
        out_shape=[
            jax.ShapeDtypeStruct((rows, width), BF),
            jax.ShapeDtypeStruct((rows, part), BF),
            jax.ShapeDtypeStruct((rows, part), BF),
            jax.ShapeDtypeStruct((1, part), F32),
        ],
        scratch_shapes=[
            vmem((groups, seq, own, part), BF),
            vmem((rows, width), BF),
            pltpu.SemaphoreType.DMA((seq,)),
            pltpu.SemaphoreType.DMA((count,)),
        ],
        compiler_params=PARAMS,
        cost_estimate=cost(2 * rows * width * part, gathered, grad_act, *pieces, *pieces),
    )(offset, grad_act, gathered, *pieces)


def grad_mlp_call(value, second_half, gathered):
    rows, part = value.shape[0] // 2, value.shape[1]
    tile = row_tile(rows)
    seq, groups, own, _ = gathered.shape
    width = seq * groups * own
    skip = rows // tile if second_half else 0

    def kernel(value, gathered, out, weight, sems):
        @pl.when(pl.program_id(0) == 0)
        def _():
            copies = fetches(gathered, weight, sems)
            for copy in copies:
                copy.start()
            for copy in copies:
                copy.wait()

        out[...] = dot_t(value[...], weight[...].reshape(width, part)).astype(BF)

    return pl.pallas_call(
        kernel,
        name="grad_mlp",
        grid=(rows // tile,),
        in_specs=[pl.BlockSpec((tile, part), lambda i: (i + skip, 0)), ANYWHERE],
        out_specs=pl.BlockSpec((tile, width), by_row),
        out_shape=jax.ShapeDtypeStruct((rows, width), BF),
        scratch_shapes=[vmem((groups, seq, own, part), BF), pltpu.SemaphoreType.DMA((seq,))],
        compiler_params=PARAMS,
        cost_estimate=cost(2 * rows * width * part, value, gathered),
    )(value, gathered)


def branch_call(value, second_half, weight):
    rows, part = value.shape[0] // 2, value.shape[1]
    width = weight.shape[1]
    tile = row_tile(rows)
    skip = rows // tile if second_half else 0

    def kernel(value, weight, out):
        out[...] = dot32(value[...], weight[...]).astype(BF)

    return pl.pallas_call(
        kernel,
        name="branch",
        grid=(rows // tile,),
        in_specs=[
            pl.BlockSpec((tile, part), lambda i: (i + skip, 0)),
            pl.BlockSpec((part, width), fixed),
        ],
        out_specs=pl.BlockSpec((tile, width), by_row),
        out_shape=jax.ShapeDtypeStruct((rows, width), BF),
        compiler_params=PARAMS,
        cost_estimate=cost(2 * rows * width * part, value, weight),
    )(value, weight)


def d_rows_call(left, second_half, right, dp):
    rows, width = right.shape
    blocks = dp // 2
    size = left.shape[1] // dp
    skip = blocks if second_half else 0
    count = 2 if second_half else 1
    each = blocks // count

    def kernel(left, right, *outs):
        value = t_dot(left[...], right[...]).astype(BF)
        for n, out in enumerate(outs):

            @pl.when(pl.program_id(0) // each == n)
            def _(out=out):
                out[...] = value

    def place(n):
        return lambda i: (jnp.clip(i - n * each, 0, each - 1), 0)

    outs = pl.pallas_call(
        kernel,
        name="d_rows",
        grid=(blocks,),
        in_specs=[
            pl.BlockSpec((rows, size), lambda i: (0, i + skip)),
            pl.BlockSpec((rows, width), fixed),
        ],
        out_specs=[pl.BlockSpec((size, width), place(n)) for n in range(count)],
        out_shape=[jax.ShapeDtypeStruct((size * each, width), BF)] * count,
        compiler_params=PARAMS,
        cost_estimate=cost(),
    )(left, right)
    return outs if second_half else outs[0]


def d_proj_call(act, two, seq):
    rows, part = act.shape
    width = two.shape[1]
    tile = max(part // seq, HEAD)

    def kernel(act, two, out):
        out[...] = t_dot(act[...], two[...]).astype(BF)

    return pl.pallas_call(
        kernel,
        name="d_proj",
        grid=(part // tile,),
        in_specs=[pl.BlockSpec((rows, tile), by_column), pl.BlockSpec((rows, width), fixed)],
        out_specs=pl.BlockSpec((tile, width), by_row),
        out_shape=jax.ShapeDtypeStruct((part, width), BF),
        compiler_params=PARAMS,
        cost_estimate=cost(2 * rows * width * part, act, two),
    )(act, two)


def d_fc_call(mlp, grad_pre, dp, seq):
    rows, width = mlp.shape
    part = grad_pre.shape[1]
    own = width // (dp * seq)
    tile = width // dp

    def kernel(mlp, grad, out):
        out[...] = t_dot(mlp[...], grad[...]).astype(BF).reshape(seq, 1, own, part)

    return pl.pallas_call(
        kernel,
        name="d_fc",
        grid=(dp,),
        in_specs=[pl.BlockSpec((rows, tile), by_column), pl.BlockSpec((rows, part), fixed)],
        out_specs=pl.BlockSpec((seq, 1, own, part), lambda i: (0, i, 0, 0)),
        out_shape=jax.ShapeDtypeStruct((seq, dp, own, part), BF),
        compiler_params=PARAMS,
        cost_estimate=cost(2 * rows * width * part, mlp, grad_pre),
    )(mlp, grad_pre)


def local(
    dp,
    seq,
    tokens,
    lengths,
    repos,
    ln1_gain,
    ln1_bias,
    w_query,
    b_query,
    w_key,
    w_value,
    b_value,
    w_out,
    b_out,
    ln2_gain,
    ln2_bias,
    w_fc,
    b_fc,
    w_proj,
    b_proj,
    grad_out,
):
    ring = Ring(dp, seq)
    me, z = ring.me, ring.z
    windows, span, width = tokens.shape
    rows = windows * span
    own = w_query.shape[0]
    block = own * seq
    hidden = w_fc.shape[1]
    part = hidden // dp
    piece = part // seq
    scale = 1.0 / math.sqrt(HEAD)
    kv_end = width + 2 * HEAD
    pairs = dp
    all_rows = dp * rows

    size_hi = lax.div(lengths, jnp.int32(64))
    columns = [
        ln1_gain[:, None],
        ln1_bias[:, None],
        b_query[:, None],
        b_out[:, None],
        ln2_gain[:, None],
        ln2_bias[:, None],
        b_proj[:, None],
        jnp.pad(b_value, (0, own - b_value.shape[0]))[:, None],
        jnp.broadcast_to(size_hi.astype(BF), (own,))[:, None],
        jnp.broadcast_to((lengths - 64 * size_hi).astype(BF), (own,))[:, None],
        jnp.broadcast_to(repos.astype(BF), (own,))[:, None],
        jnp.transpose(b_fc.reshape(-1, own)),
    ]
    n_plain = 11
    n_fc = b_fc.shape[0] // own
    vector_block = jnp.concatenate(columns, axis=1)
    vector_block = jnp.pad(vector_block, ((0, 0), (0, HEAD - vector_block.shape[1])))
    w_qkv = jnp.concatenate([w_query, w_key, w_value, vector_block], axis=1)

    token = jnp.zeros((), F32)

    def tick(*values):
        nonlocal token
        values, token = lax.optimization_barrier((values, token))
        return values

    first_place = z * span
    info = jnp.stack([first_place] + ring.owners)
    token_rows = tokens.reshape(rows, width)
    raw = grad_out.reshape(rows, width)
    n_value = b_value.shape[0]
    raw_near = ring.cross(raw)
    qkv_z = ring.seq_gather_near(w_qkv)
    qkv_z, w_out, raw, raw_near = tick(qkv_z, w_out, raw, raw_near)

    qkv_block = ring.seq_place(qkv_z).reshape(block, -1)
    qkv_near = ring.cross(qkv_block)
    out_z = ring.seq_gather_near(w_out)
    qkv_block, qkv_near, out_z, w_proj = tick(qkv_block, qkv_near, out_z, w_proj)
    proj_all = lax.all_gather(w_proj, "seq", axis=0, tiled=True)

    qkv_far = ring.corner(qkv_block, qkv_near)
    qkv_first = ring.first(qkv_block, qkv_near)
    out_block = ring.seq_place(out_z).reshape(block, -1)
    qkv_far, out_block, qkv_first = tick(qkv_far, out_block, qkv_first)

    qkv_second = ring.second(qkv_far)
    out_near = ring.cross(out_block)
    qkv_second, qkv_first = tick(qkv_second, qkv_first)
    qkv_all = ring.pieces(qkv_first, qkv_second)
    attn_in, query_low, kv_low, rel, nat = enter_call(info, token_rows, qkv_all, dp, own, n_value)
    kv_low, attn_in, query_low, rel, w_fc = tick(kv_low, attn_in, query_low, rel, w_fc)
    kv_z = ring.seq_gather_near(kv_low)
    fc_turned = lax.all_to_all(
        w_fc.reshape(own, dp, part), "dp", split_axis=1, concat_axis=0, tiled=False
    )

    all_lengths = (rel[8] * 64.0 + rel[9]).reshape(dp, block)[:, :1]
    all_repos = rel[10].reshape(dp, block)[:, :1]
    same = (all_repos == all_repos.reshape(1, dp)).astype(F32)
    weights = jnp.sum(all_lengths) / (
        REPOS * jnp.sum(same * all_lengths.reshape(1, dp), axis=1, keepdims=True)
    )
    places = (first_place + jnp.arange(span, dtype=jnp.int32)).astype(F32)
    all_valid = (places[None, :] < all_lengths).astype(F32)
    row_scale = (all_valid * weights).reshape(all_rows, 1)
    valid_rows = all_valid[0].reshape(rows, 1)
    bf_own = jnp.transpose(
        rel[n_plain : n_plain + n_fc, :block].reshape(n_fc, seq, own), (1, 0, 2)
    ).reshape(1, part)
    own_scale = row_scale[:rows]
    kv_z, raw, out_block, out_near, row_scale, own_scale, bf_own, fc_turned = tick(
        kv_z, raw, out_block, out_near, row_scale, own_scale, bf_own, fc_turned
    )
    fc_all = lax.all_gather(fc_turned.reshape(dp, own, part), "seq", axis=0, tiled=False)

    out_far = ring.corner(out_block, out_near)
    out_first = ring.first(out_block, out_near)
    kv_all = ring.seq_place(kv_z).reshape(seq * span, 2 * HEAD)
    key_all, value_all = kv_all[:, :HEAD], kv_all[:, HEAD:]
    attn_low, log_total = attend(
        info, query_low, key_all, jnp.transpose(value_all), valid_rows, pairs, scale
    )
    attn_low, raw, out_far, out_first = tick(attn_low, raw, out_far, out_first)
    out_second = ring.second(out_far)
    out_second, attn_low = tick(out_second, attn_low)
    raw_far = ring.corner(raw, raw_near)
    raw_first = ring.first(raw, raw_near)
    out_all = ring.pieces(out_first, out_second)
    hidden_one, mlp_own = leave_call(attn_low, out_all, token_rows, nat)
    mlp_own, raw_far, raw_first = tick(mlp_own, raw_far, raw_first)

    mlp_near = ring.cross(mlp_own)
    raw_second = ring.second(raw_far)
    raw_second, proj_all = tick(raw_second, proj_all)
    two_all, grad_act = grad_act_call(ring.pieces(raw_first, raw_second), row_scale, proj_all)
    mlp_own, two_all, grad_act, mlp_near = tick(mlp_own, two_all, grad_act, mlp_near)
    mlp_far = ring.corner(mlp_own, mlp_near)
    mlp_first = ring.first(mlp_own, mlp_near)
    mlp_far, mlp_first = tick(mlp_far, mlp_first)
    mlp_second = ring.second(mlp_far)
    (mlp_second,) = tick(mlp_second)
    (fc_all,) = tick(fc_all)
    mlp_all, act_low, grad_pre, d_b_fc = feed_call(
        ring.pieces(mlp_first, mlp_second), bf_own, grad_act, fc_all
    )
    odd = grad_mlp_call(grad_pre, True, fc_all)
    odd, grad_pre = tick(odd, grad_pre)
    other = ring.other(odd)
    even = grad_mlp_call(grad_pre, False, fc_all)
    even, other = tick(even, other)
    corner = ring.corner_sums(even, other)
    corner, act_low = tick(corner, act_low)
    far = ring.send_corner(corner)
    d_fc = d_fc_call(mlp_all, grad_pre, dp, seq)
    d_fc, act_low = tick(d_fc, act_low)
    fc_share = lax.psum_scatter(d_fc, "seq", scatter_dimension=0, tiled=False)
    branch_odd = branch_call(act_low, True, proj_all)
    far, branch_odd, act_low = tick(far, branch_odd, act_low)
    cross = ring.cross_sums(even, other, far)
    cross, act_low, branch_odd = tick(cross, act_low, branch_odd)
    near = ring.send_cross(cross)
    branch_other = ring.other(branch_odd)
    branch_even = branch_call(act_low, False, proj_all)
    d_proj = d_proj_call(act_low, two_all, seq)
    near, branch_even, branch_other, d_proj = tick(near, branch_even, branch_other, d_proj)
    proj_share = lax.psum_scatter(d_proj, "seq", scatter_dimension=0, tiled=True)
    corner = ring.corner_sums(branch_even, branch_other)
    corner, near = tick(corner, near)

    branch_far = ring.send_corner(corner)
    d_bf = jnp.transpose(d_b_fc.reshape(seq, n_fc, own), (1, 0, 2)).reshape(n_fc, block)
    d_bf = jnp.pad(d_bf, ((0, 8 - n_fc), (0, 0)))
    grad_mid, grad_one, sums, grad_att = middle_call(
        ring.ends(even, other, near), hidden_one, raw, own_scale, valid_rows, nat, out_all
    )
    d_out_odd = d_rows_call(attn_low, True, grad_one, dp)
    grad_att, grad_one, d_out_odd, branch_far = tick(grad_att, grad_one, d_out_odd, branch_far)
    cross = ring.cross_sums(branch_even, branch_other, branch_far)
    cross, grad_att, grad_one, d_out_odd = tick(cross, grad_att, grad_one, d_out_odd)
    branch_near = ring.send_cross(cross)
    d_out_other = ring.other(d_out_odd)
    query_grad, key_grad, value_grad = attend_back(
        info, query_low, grad_att, log_total, key_all, jnp.transpose(key_all), value_all, pairs, scale
    )
    d_out_even = d_rows_call(attn_low, False, grad_one, dp)
    kv_grads = jnp.concatenate([key_grad, value_grad], axis=1)
    kv_mine, kv_sends = ring.seq_cut(kv_grads, rows)
    query_grad, kv_mine, kv_sends, d_out_even, d_out_other, branch_near, fc_share = tick(
        query_grad, kv_mine, kv_sends, d_out_even, d_out_other, branch_near, fc_share
    )
    corner = ring.corner_sums(d_out_even, d_out_other)
    corner, query_grad = tick(corner, query_grad)
    out_far_back = ring.send_corner(corner)
    kv_grad = ring.seq_sum(kv_mine, kv_sends).astype(BF)
    d_q_odd = d_rows_call(attn_in, True, query_grad, dp)
    out_far_back, kv_grad, d_q_odd, query_grad = tick(out_far_back, kv_grad, d_q_odd, query_grad)
    cross = ring.cross_sums(d_out_even, d_out_other, out_far_back)
    cross, d_q_odd, query_grad, kv_grad = tick(cross, d_q_odd, query_grad, kv_grad)
    out_near_back = ring.send_cross(cross)
    d_q_other = ring.other(d_q_odd)
    d_q_even = d_rows_call(attn_in, False, query_grad, dp)
    grad_rows, small = last_call(
        info,
        query_grad,
        kv_grad,
        qkv_all,
        token_rows,
        attn_in,
        rel,
        grad_mid,
        sums,
        d_bf,
        dp,
        own,
        n_value,
    )
    grad_tokens = grad_rows.reshape(windows, span, width)
    cut = width // 2
    small_odd = small[cut:]
    out_near_back, d_q_other, d_q_even, small, small_odd, branch_near = tick(
        out_near_back, d_q_other, d_q_even, small, small_odd, branch_near
    )
    corner = ring.corner_sums(d_q_even, d_q_other)
    corner, small_odd, out_near_back, branch_near = tick(
        corner, small_odd, out_near_back, branch_near
    )
    q_far = ring.send_corner(corner)
    small_other = ring.other(small_odd)
    out_share = ring.scatter_end(d_out_even, d_out_other, out_near_back)
    out_mine, out_sends = ring.seq_cut(out_share, own)
    branch_two = ring.scatter_end(branch_even, branch_other, branch_near)
    output = (hidden_one + branch_two + nat[6:7]).astype(BF).reshape(windows, span, width)
    small_other, out_mine, out_sends, output = tick(small_other, out_mine, out_sends, output)
    small_far = ring.send_corner(ring.corner_sums(small[:cut], small_other))
    q_far, small_far, proj_share = tick(q_far, small_far, proj_share)
    cross = ring.cross_sums(d_q_even, d_q_other, q_far)
    small_cross = ring.cross_sums(small[:cut], small_other, small_far)
    cross, out_sends, small_cross = tick(cross, out_sends, small_cross)
    q_near = ring.send_cross(cross)
    small_near = ring.send_cross(small_cross)
    d_w_out = ring.seq_sum(out_mine, out_sends)
    q_near, small_near, d_w_out = tick(q_near, small_near, d_w_out)
    q_share = ring.scatter_end(d_q_even, d_q_other, q_near)
    small_share = ring.scatter_end(small[:cut], small_other, small_near)
    q_mine, q_sends = ring.seq_cut(q_share, own)
    small_mine, small_sends = ring.seq_cut(small_share, own)
    sends = [jnp.concatenate(pair, axis=1) for pair in zip(q_sends, small_sends)]
    q_mine, small_mine, sends, fc_share = tick(q_mine, small_mine, sends, fc_share)
    fc_turned_back = lax.all_to_all(fc_share, "dp", split_axis=0, concat_axis=1, tiled=False)
    both = ring.seq_sum(jnp.concatenate([q_mine, small_mine], axis=1), sends)
    d_w_query, d_small = both[:, :width], both[:, width:]
    d_w_proj = proj_share.astype(F32)
    d_w_fc = fc_turned_back.reshape(own, hidden).astype(F32)
    vectors = jnp.transpose(d_small[:, 2 * HEAD :])
    return (
        output,
        grad_tokens,
        vectors[0],
        vectors[1],
        d_w_query,
        vectors[16],
        d_small[:, :HEAD],
        d_small[:, HEAD : 2 * HEAD],
        vectors[17, : b_value.shape[0]],
        d_w_out,
        vectors[8],
        vectors[9],
        vectors[10],
        d_w_fc,
        vectors[24 : 24 + n_fc].reshape(-1),
        d_w_proj,
        vectors[11],
    )


def solution(mesh):
    dp, seq = mesh.shape["dp"], mesh.shape["seq"]
    both = P(("dp", "seq"))
    rows = P(("dp", "seq"), None)
    token = P("dp", "seq", None)

    def run(*args):
        return local(dp, seq, *args)

    return jax.shard_map(
        run,
        mesh=mesh,
        in_specs=(
            token,
            P("dp"),
            P("dp"),
            both,
            both,
            rows,
            both,
            rows,
            rows,
            both,
            rows,
            both,
            both,
            both,
            rows,
            both,
            rows,
            both,
            token,
        ),
        out_specs=(
            token,
            token,
            both,
            both,
            rows,
            both,
            rows,
            rows,
            both,
            rows,
            both,
            both,
            both,
            rows,
            both,
            rows,
            both,
        ),
        check_vma=False,
    )
```
